128 devices in a mesh: expert: 4 (over x), dp: 32 (over y, z, core).
Axes of the slice: x: 4, y: 4, z: 4, core: 2. Of those that a mesh axis runs over, the one named last changes fastest.
Arguments:
- tokens: bfloat16 [32, 2048, 512], P('dp', 'expert'), may hold values from -6 to 6
- expert_ids: int32 [32, 2048, 8], P('dp', 'expert'), may hold values from 0 to 23, all different within a row; in each aligned block of 512 rows (0 to 511, 512 to 1023, ..., all dimensions but the last counted through in order) at most 320 rows name the same one
- cotangent: bfloat16 [32, 2048, 512], P('dp', 'expert'), may hold values from -6 to 6
- gain_heads: float32 [512], replicated, may hold values from 0.5 to 1.5
- key_value_weight: bfloat16 [512, 128], replicated, may hold values from -0.25 to 0.25
- router_weight: bfloat16 [512, 24], replicated, may hold values from -0.125 to 0.125
- query_weight: bfloat16 [24, 512, 64], P('expert'), may hold values from -0.25 to 0.25
- output_weight: bfloat16 [24, 64, 512], P('expert'), may hold values from -12 to 12
- gain_feed: float32 [512], replicated, may hold values from 0.5 to 1.5
- up_weight: bfloat16 [512, 2048], replicated, may hold values from -0.25 to 0.25
- down_weight: bfloat16 [2048, 512], replicated, may hold values from -0.25 to 0.25
Outputs:
- block_out: bfloat16 [32, 2048, 512], P('dp', 'expert')
- grad_tokens: bfloat16 [32, 2048, 512], P('dp', 'expert')
- grad_gain_heads: float32 [512], replicated
- grad_kv_weight: float32 [512, 128], replicated
- grad_router: float32 [512, 24], replicated
- grad_query_weight: float32 [24, 512, 64], P('expert')
- grad_output_weight: float32 [24, 64, 512], P('expert')
- grad_gain_feed: float32 [512], replicated
- grad_up_weight: float32 [512, 2048], replicated
- grad_down_weight: float32 [2048, 512], replicated
The draws below stay inside these ranges and needn't reach their ends.
Inputs may be any that keep to these rules, and one draw needn't show every extreme that they name: `expert_ids`: each row names 8 different experts; within the rows of one device no expert is named by more than 320 rows.
All inputs are finite; a program needn't handle non-finite values.
Results may differ from the reference program's by a relative error of at most 0.02.
Values may be sent and summed in bfloat16 or wider, within the bound.
No kernel may reach another device: no remote copies, remote signals or barrier semaphores. Data moves between devices by JAX's collectives and lax.ppermute only.
A program may use at most 192 MiB of HBM per device.

```python
import math
import jax
import jax.numpy as jnp
import numpy as np
from jax import lax

D = 512
HEAD = 64
EXPERTS = 24
TOPK = 8
FF = 2048
TOK_DEV = 512
CAP = 320
LENGTH = 2048
SEQS = 32


def shard_levels(rng, dims, pieces, smallest, top_value):
    level = 1.0
    for position, blocks in pieces:
        heights = jax.random.uniform(jax.random.fold_in(jax.random.fold_in(rng, 6), position), (blocks,), jnp.float32, smallest / len(pieces), top_value / len(pieces))
        level = level * jnp.repeat(jnp.exp(heights), dims[position] // blocks).reshape((-1,) + (1,) * (len(dims) - 1 - position))
    return level


def shared_out(stream_key, own, number, rows, number_of, top, bound, lean):
    sequence = jax.random.permutation(stream_key, number_of)
    packed, usual = portions_of(number_of, rows * top, bound, lean, True), portions_of(number_of, rows * top, bound, lean, False)
    places = jnp.arange(number_of)

    def named(sizes, rotation):
        used = int((sizes > 0).sum())
        fixed = max(1, used // 4)
        passed = fixed + (places - fixed + rotation * (used - fixed)) % max(1, number_of - fixed)
        return jnp.zeros((number_of,), jnp.int32).at[sequence[jnp.where(places < fixed, places, passed)]].set(jnp.asarray(sizes, jnp.int32))

    sizes = jnp.where(number % 4 == 0, named(packed, number // 4), named(usual, number - number // 4 - 1))
    mixed = jax.random.permutation(jax.random.fold_in(own, 3), number_of)
    giver, sink = mixed[0:number_of // 2 * 2:2], mixed[1:number_of // 2 * 2:2]
    room = jnp.minimum(sizes[giver] - 1, bound - sizes[sink]) // 2
    room = jnp.where((giver == sequence[0]) | (sink == sequence[0]) | (sizes[sink] == 0), 0, jnp.maximum(room, 0))
    passed = jax.random.randint(jax.random.fold_in(own, 4), (number_of // 2,), 0, 1 << 20) % (room + 1)
    sizes = sizes.at[giver].add(-passed).at[sink].add(passed)
    items = jnp.searchsorted(jnp.cumsum(sizes), jnp.arange(rows * top), side="right").astype(jnp.int32)
    listing = items.reshape(top, rows).T
    listing = listing[jax.random.permutation(jax.random.fold_in(own, 1), rows)]
    rotation = jax.random.randint(jax.random.fold_in(own, 2), (rows, 1), 0, top)
    return jnp.take_along_axis(listing, (jnp.arange(top)[None, :] + rotation) % top, axis=1)


def portions_of(amount, total, limit, slope, full):
    weights = [(1 << 20) // math.isqrt(rank ** slope) + 1 for rank in range(1, amount + 1)]
    largest = limit if full else min(limit, max(-(-total // amount), total * weights[0] // sum(weights)))
    least = 1 if total - largest >= amount - 1 else 0
    given, spare = [largest] + [least] * (amount - 1), total - largest - least * (amount - 1)
    while spare > 0:
        candidates = [i for i in range(1, amount) if given[i] < largest] or [i for i in range(1, amount) if given[i] < limit]
        mass, budget = sum([weights[i] for i in candidates]), spare
        for i in candidates:
            addition = min(limit - given[i], max(1, budget * weights[i] // mass), spare)
            given[i] = given[i] + addition
            spare = spare - addition
    return np.array(given)


def centred(rng, shape, spread, reach, split=(), held_as=jnp.bfloat16):
    values = spread * jax.random.normal(rng, shape, jnp.float32)
    if split:
        values = values * shard_levels(rng, shape, split, -0.22, 0.18)
    return jnp.clip(values, -reach, reach).astype(held_as)


def setup_inputs(seed: int = 0) -> dict:
    key_of = jax.random.split(jax.random.key(seed), 12)
    tokens = centred(key_of[0], (SEQS, LENGTH, D), 1.0, 6.0, ((0, 32), (1, 4)))
    expert_ids_keys = jax.random.split(jax.random.fold_in(key_of[1], 1), SEQS * LENGTH // TOK_DEV)
    expert_ids_turns = jax.random.permutation(jax.random.fold_in(key_of[1], 3), SEQS * LENGTH // TOK_DEV)
    expert_ids = jax.vmap(lambda own, number: shared_out(jax.random.fold_in(key_of[1], 2), own, number, TOK_DEV, EXPERTS, TOPK, CAP, 2))(expert_ids_keys, expert_ids_turns).reshape((SEQS, LENGTH, TOPK))
    cotangent = centred(key_of[2], (SEQS, LENGTH, D), 1.0, 6.0, ((0, 32), (1, 4)))
    gain_heads = jnp.clip(1.0 + 0.1 * jax.random.normal(key_of[3], (D,), jnp.float32), 0.5, 1.5)
    key_value_weight = centred(key_of[4], (D, 2 * HEAD), D ** -0.5, 0.25)
    router_weight = centred(key_of[5], (D, EXPERTS), (4 * D) ** -0.5, 0.125)
    query_weight = centred(key_of[6], (EXPERTS, D, HEAD), D ** -0.5, 0.25, ((0, 4),))
    output_weight = centred(key_of[7], (EXPERTS, HEAD, D), 3.0, 12.0, ((0, 4),))
    gain_feed = jnp.clip(1.0 + 0.1 * jax.random.normal(key_of[8], (D,), jnp.float32), 0.5, 1.5)
    up_weight = centred(key_of[9], (D, FF), D ** -0.5, 0.25)
    down_weight = centred(key_of[10], (FF, D), (FF // 4) ** -0.5, 0.25)
    return dict(tokens=tokens, expert_ids=expert_ids, cotangent=cotangent, gain_heads=gain_heads, key_value_weight=key_value_weight, router_weight=router_weight, query_weight=query_weight, output_weight=output_weight, gain_feed=gain_feed, up_weight=up_weight, down_weight=down_weight)


@jax.custom_vjp
def low(v):
    return lax.optimization_barrier(v.astype(jnp.bfloat16)).astype(jnp.float32)

@jax.custom_vjp
def low_back(v):
    return v

def low_keep(v):
    return (low(v), None)

def low_pass(kept, grad):
    return (grad,)

def back_keep(v):
    return (v, None)

def back_low(kept, grad):
    return (low(grad),)
low.defvjp(low_keep, low_pass)
low_back.defvjp(back_keep, back_low)
EPSILON = 1e-06
PRECISE = lax.Precision.HIGHEST
CURVE_SCALE = 0.7978845608028654
CURVE_CUBIC = 0.044715

def smooth_gate(value):
    return 0.5 * value * (1.0 + jnp.tanh(CURVE_SCALE * (value + CURVE_CUBIC * value * value * value)))

def normed(rows, gain):
    scale = lax.rsqrt(lax.optimization_barrier(jnp.mean(rows * rows, axis=-1, keepdims=True)) + EPSILON)
    return rows * scale * gain

def sequence_block(params, rows, routes):
    gain_heads, key_value_weight, router_weight, query_weight, output_weight, gain_feed, up_weight, down_weight = params
    hidden = low(normed(rows, gain_heads))
    key_value = low_back(low(jnp.dot(hidden, key_value_weight, precision=PRECISE)))
    keys = key_value[:, :HEAD]
    values = key_value[:, HEAD:]
    logits = jnp.dot(hidden, router_weight, precision=PRECISE)
    picked = jnp.take_along_axis(logits, routes, axis=1)
    peak = lax.optimization_barrier(jnp.max(picked, axis=1, keepdims=True))
    raised = jnp.exp(picked - peak)
    gates = raised / lax.optimization_barrier(jnp.sum(raised, axis=1, keepdims=True))
    table = (routes[:, :, None] == jnp.arange(EXPERTS, dtype=jnp.int32)[None, None, :]).astype(jnp.float32)
    dense_gates = jnp.einsum('tr,tre->et', gates, table, precision=PRECISE)
    places = jnp.arange(LENGTH, dtype=jnp.int32)
    allowed = places[None, :] <= places[:, None]

    def one_expert(total, items):
        w_query, w_out, expert_gates = items
        query = low_back(low(jnp.dot(low_back(hidden), w_query, precision=PRECISE)))
        scores = low_back(jnp.dot(query, keys.T, precision=PRECISE)) * HEAD ** (-0.5)
        scores = jnp.where(allowed, scores, -jnp.inf)
        top = lax.optimization_barrier(jnp.max(scores, axis=1, keepdims=True))
        lifted = jnp.exp(scores - top)
        shares = low(lifted / lax.optimization_barrier(jnp.sum(lifted, axis=1, keepdims=True)))
        mixed = low_back(low(jnp.dot(shares, values, precision=PRECISE)))
        routed = low_back(low(jnp.dot(mixed, w_out, precision=PRECISE)))
        return (total + expert_gates[:, None] * routed, None)
    attention, _ = lax.scan(jax.checkpoint(one_expert), jnp.zeros((LENGTH, D), jnp.float32), (query_weight, output_weight, dense_gates))
    middle = rows + attention
    hidden_feed = low(normed(middle, gain_feed))
    before_gate = low_back(jnp.dot(hidden_feed, up_weight, precision=PRECISE))
    active = low(smooth_gate(before_gate))
    return middle + jnp.dot(active, down_weight, precision=PRECISE)

def reference(tokens, expert_ids, cotangent, gain_heads, key_value_weight, router_weight, query_weight, output_weight, gain_feed, up_weight, down_weight):
    params = (gain_heads.astype(jnp.float32), key_value_weight.astype(jnp.float32), router_weight.astype(jnp.float32), query_weight.astype(jnp.float32), output_weight.astype(jnp.float32), gain_feed.astype(jnp.float32), up_weight.astype(jnp.float32), down_weight.astype(jnp.float32))
    rows_all = tokens.astype(jnp.float32)

    def forward(weights, inputs):

        def one_sequence(items):
            return sequence_block(weights, items[0], items[1])
        return lax.map(jax.checkpoint(one_sequence), (inputs, expert_ids))
    result, pull = jax.vjp(forward, params, rows_all)
    grads, grad_rows = pull(cotangent.astype(jnp.float32))
    return (result.astype(jnp.bfloat16), grad_rows.astype(jnp.bfloat16), grads[0], grads[1], grads[2], grads[3], grads[4], grads[5], grads[6], grads[7])
```

```python
from functools import partial

import jax
import jax.numpy as jnp
from jax import lax
from jax.experimental import pallas as pl
from jax.experimental.pallas import tpu as pltpu
from jax.sharding import Mesh, PartitionSpec as P

D = 512
HEAD = 64
EXPERTS = 24
TOPK = 8
FF = 2048
TOK = 512
GROUPS = 4
LENGTH = TOK * GROUPS
OWN = EXPERTS // GROUPS * HEAD
HALF = OWN // 2
TILE = 256
LANES = TOPK * TILE
TILES = LENGTH // TILE
ROUTES = TOK * TOPK
CHUNK = 256
SMALL = 160

EPSILON = 1e-06
CURVE_SCALE = 0.7978845608028654
CURVE_CUBIC = 0.044715
SCORE = HEAD**-0.5
SCORE2 = SCORE * 1.4426950408889634
LOW = -1e30

F32 = jnp.float32
BF16 = jnp.bfloat16
MIB = 1 << 20


def nn(a, b):
    return lax.dot_general(a, b, (((1,), (0,)), ((), ())), preferred_element_type=F32)


def nt(a, b):
    return lax.dot_general(a, b, (((1,), (1,)), ((), ())), preferred_element_type=F32)


def tn(a, b):
    return lax.dot_general(a, b, (((0,), (0,)), ((), ())), preferred_element_type=F32)


def split_two(value):
    high = value.astype(BF16)
    return high, (value - high.astype(F32)).astype(BF16)


def scale_of(rows):
    return lax.rsqrt(jnp.mean(rows * rows, axis=-1, keepdims=True) + EPSILON)


def lanes_of(tile, slot):
    return pl.ds(tile * LANES + slot * TILE, TILE)


def tokens_of(tile):
    return pl.ds(tile * TILE, TILE)


def block(index, size):
    return pl.ds(pl.multiple_of(index * size, size), size)


def slots_of(expert):
    return range(max(0, expert - (EXPERTS - TOPK)), min(TOPK - 1, expert) + 1)


def prepare(tok_ref, ids_ref, gain_ref, wkv_ref, wr_ref, hid_ref, kv_ref, gates_ref, slot_ref):
    rows = tok_ref[...].astype(F32)
    hidden = (rows * scale_of(rows) * gain_ref[...]).astype(BF16)
    hid_ref[...] = hidden
    kv_ref[...] = nn(hidden, wkv_ref[...]).astype(BF16)
    logits = nt(wr_ref[...], hidden)
    ids = ids_ref[...]
    names = lax.broadcasted_iota(jnp.int32, (EXPERTS, TOK), 0)
    chosen = names == ids[0:1]
    for route in range(1, TOPK):
        chosen = chosen | (names == ids[route : route + 1])
    count = jnp.where(chosen, 1.0, 0.0)
    below = lax.broadcasted_iota(jnp.int32, (EXPERTS, EXPERTS), 0) > lax.broadcasted_iota(
        jnp.int32, (EXPERTS, EXPERTS), 1
    )
    rank = nn(jnp.where(below, 1.0, 0.0).astype(BF16), count.astype(BF16))
    slot_ref[...] = jnp.where(chosen, rank, -1.0).astype(jnp.int32)
    peak = jnp.max(jnp.where(chosen, logits, -3e38), axis=0, keepdims=True)
    raised = jnp.where(chosen, jnp.exp(logits - peak), 0.0)
    gates_ref[...] = raised / jnp.sum(raised, axis=0, keepdims=True)


def compact(slot_ref, dense_ref, tile, slot):
    value = jnp.zeros((HEAD, TILE), F32)
    for expert in range(slot, slot + EXPERTS - TOPK + 1):
        here = slot_ref[pl.ds(expert, 1), tokens_of(tile)] == slot
        value = jnp.where(here, dense_ref[pl.ds(expert * HEAD, HEAD), tokens_of(tile)], value)
    return value


def expand(slot_ref, packed_ref, tile, expert):
    row = slot_ref[pl.ds(expert, 1), tokens_of(tile)]
    value = jnp.zeros((HEAD, TILE), F32)
    for slot in slots_of(expert):
        value = jnp.where(row == slot, packed_ref[:, lanes_of(tile, slot)].astype(F32), value)
    return value


def causal():
    return lax.broadcasted_iota(jnp.int32, (TILE, TILE), 0) <= lax.broadcasted_iota(
        jnp.int32, (TILE, TILE), 1
    )


def attend(
    place_ref,
    hid_ref,
    slot_ref,
    wq0,
    wq1,
    wq2,
    wq3,
    kv0,
    kv1,
    kv2,
    kv3,
    qc_ref,
    mixed_ref,
    lse_ref,
    kv_ref,
    qall,
    keys,
    vt,
    peak,
    total,
    acc,
):
    x = place_ref[0]
    for away, (wq, kv) in enumerate(((wq0, kv0), (wq1, kv1), (wq2, kv2), (wq3, kv3))):
        owner = lax.rem(x + GROUPS - away, GROUPS)
        kv_ref[block(owner, TOK), :] = kv[...]
        keys[block(owner, TOK), :] = kv[:, 0:HEAD]
        turned = kv[:, HEAD : 2 * HEAD].astype(F32).T.astype(BF16)
        vt[2 * owner] = turned[:, 0:TILE]
        vt[2 * owner + 1] = turned[:, TILE : 2 * TILE]
        qall[block(owner, OWN), :] = nt(wq[...], hid_ref[...])
    for tile in range(2):
        for slot in range(TOPK):
            qc_ref[:, lanes_of(tile, slot)] = compact(slot_ref, qall, tile, slot).astype(BF16)

    for tile in range(2):
        last = 2 * x + tile

        def step(index, first):
            for slot in range(TOPK):
                at = pl.ds(slot * TILE, TILE)
                scores = nn(keys[block(index, TILE), :], qc_ref[:, lanes_of(tile, slot)])
                if first:
                    scores = jnp.where(causal(), scores, LOW)
                    top = jnp.max(scores, axis=0, keepdims=True)
                else:
                    before = peak[:, at]
                    top = jnp.maximum(before, jnp.max(scores, axis=0, keepdims=True))
                lifted = jnp.exp2((scores - top) * SCORE2)
                share = jnp.sum(lifted, axis=0, keepdims=True)
                part = nn(vt[index], lifted.astype(BF16))
                if not first:
                    fade = jnp.exp2((before - top) * SCORE2)
                    share = total[:, at] * fade + share
                    part = acc[:, at] * fade + part
                peak[:, at] = top
                total[:, at] = share
                acc[:, at] = part

        step(last, True)

        @pl.loop(0, last)
        def _(index):
            step(index, False)

        here = pl.ds(tile * LANES, LANES)
        mixed_ref[:, here] = (acc[...] / total[...]).astype(BF16)
        lse_ref[:, here] = peak[...] * SCORE2 + jnp.log2(total[...])


def middle_part(
    place_ref,
    tok_ref,
    cot_ref,
    mixed_ref,
    slot_ref,
    gates_ref,
    hid_ref,
    wo0,
    wo1,
    wo2,
    wo3,
    gain_ref,
    up_ref,
    down_ref,
    out_ref,
    gm_ref,
    gt_ref,
    delta_ref,
    gl_ref,
    small_ref,
    keep_ref,
    send_ref,
    dense,
    feed,
    feed_t,
    middle,
    result,
    back,
    gm16,
    gdense,
    sums,
):
    x = place_ref[0]
    core = place_ref[1]
    for tile in range(2):
        for expert in range(EXPERTS):
            value = expand(slot_ref, mixed_ref, tile, expert)
            gate = gates_ref[pl.ds(expert, 1), tokens_of(tile)]
            dense[pl.ds(expert * HEAD, HEAD), tokens_of(tile)] = (value * gate).astype(BF16)
    total = tok_ref[...].astype(F32)
    outs = (wo0, wo1, wo2, wo3)
    owners = [lax.rem(x + GROUPS - away, GROUPS) for away in range(GROUPS)]
    for owner, wo in zip(owners, outs):
        total = total + tn(dense[block(owner, OWN), :], wo[...])
    middle[...] = total
    scale = scale_of(total)
    feed32 = total * scale * gain_ref[...]
    feed[...] = feed32.astype(BF16)
    feed_t[...] = feed32.T.astype(BF16)
    result[...] = total
    back[...] = jnp.zeros_like(back)

    @pl.loop(0, FF // CHUNK)
    def _(index):
        up = up_ref[:, block(index, CHUNK)]
        down = down_ref[block(index, CHUNK), :]
        before = nn(feed[...], up)
        square = before * before
        curve = jnp.tanh(CURVE_SCALE * before * (1.0 + CURVE_CUBIC * square))
        rise = 0.5 * (1.0 + curve)
        active = (before * rise).astype(BF16)
        slope = rise + 0.5 * before * (1.0 - curve * curve) * (
            CURVE_SCALE * (1.0 + 3.0 * CURVE_CUBIC * square)
        )
        result[...] += nn(active, down)
        grad_before = (nt(cot_ref[...], down) * slope).astype(BF16)
        back[...] += nt(grad_before, up)
        grad_up = nn(feed_t[...], grad_before).astype(BF16).reshape(16, 32, CHUNK)
        grad_down = tn(active, cot_ref[...]).astype(BF16).reshape(16, 16, D)
        inner = lax.rem(index, 4)

        def put(ref):
            to = block(inner, 16)
            for group in range(2):
                ref[to, pl.ds(32 * group, 32), :] = grad_up[:, :, 128 * group : 128 * group + 128]
            for group in range(4):
                ref[to, pl.ds(64 + 16 * group, 16), :] = grad_down[
                    :, :, 128 * group : 128 * group + 128
                ]

        mine = index // 4 == core

        @pl.when(mine)
        def _():
            put(keep_ref)

        @pl.when(jnp.logical_not(mine))
        def _():
            put(send_ref)

    out_ref[...] = result[...].astype(BF16)
    total = middle[...]
    scale = scale_of(total)
    unit = total * scale
    grad = back[...]
    inner = grad * gain_ref[...]
    gain_grad = jnp.sum(grad * unit, axis=0, keepdims=True)
    grad_middle = cot_ref[...].astype(F32) + scale * (
        inner - unit * jnp.mean(inner * unit, axis=-1, keepdims=True)
    )
    gm_ref[...] = grad_middle
    gm16[...] = grad_middle.astype(BF16)
    for owner, wo in zip(owners, outs):
        gdense[block(owner, OWN), :] = nt(wo[...], gm16[...])
        grad_out = nn(dense[block(owner, OWN), :], gm16[...]).astype(BF16)

        def put(ref, half):
            part = grad_out[half * HALF : (half + 1) * HALF].reshape(4, HALF // 4, D)
            for group in range(4):
                ref[pl.ds(owner * 16 + 4 * group, 4), pl.ds(128, 48), :] = part[
                    :, :, 128 * group : 128 * group + 128
                ]

        @pl.when(core == 0)
        def _():
            put(keep_ref, 0)
            put(send_ref, 1)

        @pl.when(core == 1)
        def _():
            put(keep_ref, 1)
            put(send_ref, 0)

    sums[...] = jnp.zeros_like(sums)
    for tile in range(2):
        for slot in range(TOPK):
            at = lanes_of(tile, slot)
            value = jnp.zeros((HEAD, TILE), F32)
            gate = jnp.zeros((1, TILE), F32)
            for expert in range(slot, slot + EXPERTS - TOPK + 1):
                here = slot_ref[pl.ds(expert, 1), tokens_of(tile)] == slot
                value = jnp.where(
                    here, gdense[pl.ds(expert * HEAD, HEAD), tokens_of(tile)], value
                )
                gate = jnp.where(here, gates_ref[pl.ds(expert, 1), tokens_of(tile)], gate)
            mixed = mixed_ref[:, at].astype(F32)
            dots = jnp.sum(mixed * value, axis=0, keepdims=True)
            rounded = (value * gate).astype(BF16)
            gt_ref[:, at] = rounded
            delta_ref[:, at] = jnp.sum(mixed * rounded.astype(F32), axis=0, keepdims=True)
            for expert in range(slot, slot + EXPERTS - TOPK + 1):
                here = slot_ref[pl.ds(expert, 1), tokens_of(tile)] == slot
                sums[pl.ds(expert, 1), tokens_of(tile)] += jnp.where(here, dots, 0.0)
    gates = gates_ref[...]
    dots = sums[...]
    grad_logits = gates * (dots - jnp.sum(gates * dots, axis=0, keepdims=True))
    gl_ref[...] = grad_logits
    high, low = split_two(grad_logits)
    small_ref[...] = jnp.concatenate(
        [
            nn(high, hid_ref[...]) + nn(low, hid_ref[...]),
            gain_grad,
            jnp.zeros((7, D), F32),
        ],
        axis=0,
    )


def attend_back(
    place_ref,
    qc_ref,
    gt_ref,
    lse_ref,
    delta_ref,
    kv_ref,
    slot_ref,
    hid_ref,
    wq0,
    wq1,
    wq2,
    wq3,
    own_ref,
    pair1_ref,
    pair2_ref,
    pair3_ref,
    rows_ref,
    keep_ref,
    send_ref,
    keys,
    values,
    kt,
    q_nat,
    g_nat,
    dkeys,
    dvalues,
    dq,
    dqc,
    dqall,
    ds_all,
    p_all,
):
    x = place_ref[0]
    core = place_ref[1]
    keys[...] = kv_ref[:, 0:HEAD]
    values[...] = kv_ref[:, HEAD : 2 * HEAD]
    for tile in range(TILES):
        kt[tile] = kv_ref[pl.ds(tile * TILE, TILE), 0:HEAD].astype(F32).T.astype(BF16)
    for piece in range(2 * TOPK):
        at = pl.ds(piece * TILE, TILE)
        q_nat[at, :] = qc_ref[:, at].astype(F32).T.astype(BF16)
        g_nat[at, :] = gt_ref[:, at].astype(F32).T.astype(BF16)
    dkeys[...] = jnp.zeros_like(dkeys)
    dvalues[...] = jnp.zeros_like(dvalues)
    for tile in range(2):
        last = 2 * x + tile
        dq[...] = jnp.zeros_like(dq)

        def step(index, masked):
            at = block(index, TILE)
            for slot in range(TOPK):
                route = lanes_of(tile, slot)
                scores = nn(keys[at, :], qc_ref[:, route])
                shares = jnp.exp2(scores * SCORE2 - lse_ref[:, route])
                if masked:
                    shares = jnp.where(causal(), shares, 0.0)
                grad_shares = nn(values[at, :], gt_ref[:, route])
                grad_scores = (shares * (grad_shares - delta_ref[:, route])).astype(BF16)
                here = pl.ds(slot * TILE, TILE)
                p_all[:, here] = shares.astype(BF16)
                ds_all[:, here] = grad_scores
                dq[:, here] += nn(kt[index], grad_scores)
            whole = pl.ds(tile * LANES, LANES)
            dkeys[at, :] += nn(ds_all[...], q_nat[whole, :])
            dvalues[at, :] += nn(p_all[...], g_nat[whole, :])

        step(last, True)

        @pl.loop(0, last)
        def _(index):
            step(index, False)

        dqc[:, pl.ds(tile * LANES, LANES)] = (dq[...] * SCORE).astype(BF16)

    for away, ref in enumerate((own_ref, pair1_ref, pair2_ref, pair3_ref)):
        at = block(lax.rem(x + away, GROUPS), TOK)
        ref[...] = jnp.concatenate([dkeys[at, :] * SCORE, dvalues[at, :]], axis=1).astype(
            ref.dtype
        )
    for tile in range(2):
        for expert in range(EXPERTS):
            dqall[pl.ds(expert * HEAD, HEAD), tokens_of(tile)] = expand(
                slot_ref, dqc, tile, expert
            ).astype(BF16)
    total = jnp.zeros((TOK, D), F32)
    for away, wq in enumerate((wq0, wq1, wq2, wq3)):
        owner = lax.rem(x + GROUPS - away, GROUPS)
        total = total + tn(dqall[block(owner, OWN), :], wq[...])
    rows_ref[...] = total
    for away in range(GROUPS):
        owner = lax.rem(x + away, GROUPS)
        grad = nn(dqall[block(owner, OWN), :], hid_ref[...]).astype(BF16)

        @pl.when(core == 0)
        def _():
            keep_ref[away] = grad[0:HALF]
            send_ref[away] = grad[HALF:OWN]

        @pl.when(core == 1)
        def _():
            keep_ref[away] = grad[HALF:OWN]
            send_ref[away] = grad[0:HALF]


def finish(
    place_ref,
    tok_ref,
    hid_ref,
    gm_ref,
    rows_ref,
    gl_ref,
    wr_ref,
    wkv_ref,
    gain_ref,
    own_ref,
    pair1_ref,
    pair2_ref,
    pair3_ref,
    small_ref,
    out_ref,
    keep_ref,
    send_ref,
):
    core = place_ref[1]
    pairs = (
        own_ref[...]
        + pair1_ref[...].astype(F32)
        + pair2_ref[...].astype(F32)
        + pair3_ref[...].astype(F32)
    ).astype(BF16)
    high, low = split_two(gl_ref[...])
    grad = rows_ref[...] + nt(pairs, wkv_ref[...])
    grad = grad + tn(high, wr_ref[...]) + tn(low, wr_ref[...])
    rows = tok_ref[...].astype(F32)
    scale = scale_of(rows)
    unit = rows * scale
    inner = grad * gain_ref[...]
    gain_grad = jnp.sum(grad * unit, axis=0, keepdims=True)
    out_ref[...] = (
        gm_ref[...] + scale * (inner - unit * jnp.mean(inner * unit, axis=-1, keepdims=True))
    ).astype(BF16)
    shared = jnp.concatenate(
        [tn(pairs, hid_ref[...]), small_ref[0:25], gain_grad, small_ref[26:32]], axis=0
    )

    @pl.when(core == 0)
    def _():
        keep_ref[...] = shared[0 : SMALL // 2].astype(BF16)
        send_ref[...] = shared[SMALL // 2 : SMALL].astype(BF16)

    @pl.when(core == 1)
    def _():
        keep_ref[...] = shared[SMALL // 2 : SMALL].astype(BF16)
        send_ref[...] = shared[0 : SMALL // 2].astype(BF16)


def unpack(place_ref, mine_ref, other_ref, up_ref, down_ref):
    mine = pl.program_id(0) // 4 == place_ref[1]

    def put(ref):
        for group in range(2):
            up_ref[:, 128 * group : 128 * group + 128] = (
                ref[:, pl.ds(32 * group, 32), :].astype(F32).reshape(D, 128)
            )
        for group in range(4):
            down_ref[:, 128 * group : 128 * group + 128] = (
                ref[:, pl.ds(64 + 16 * group, 16), :].astype(F32).reshape(CHUNK, 128)
            )

    @pl.when(mine)
    def _():
        put(mine_ref)

    @pl.when(jnp.logical_not(mine))
    def _():
        put(other_ref)


def shape(dims, dtype=BF16):
    return jax.ShapeDtypeStruct(dims, dtype)


VMEM = pl.BlockSpec(memory_space=pltpu.VMEM)
SMEM = pl.BlockSpec(memory_space=pltpu.SMEM)


def turn(size, step):
    return [(index, (index + step) % size) for index in range(size)]


def swap(value):
    return lax.ppermute(value, "core", turn(2, 1))


def around(value, axis):
    return [lax.ppermute(value, axis, turn(4, step)) for step in (1, 2, 3)]


def total_over(value, axis):
    one, two, three = around(value, axis)
    return (
        (value.astype(F32) + two.astype(F32)) + (one.astype(F32) + three.astype(F32))
    ).astype(BF16)


def both(mine, other, core):
    first = jnp.where(core == 0, mine, other)
    second = jnp.where(core == 0, other, mine)
    return first, second


def shards(
    tokens,
    expert_ids,
    cotangent,
    gain_heads,
    key_value_weight,
    router_weight,
    query_weight,
    output_weight,
    gain_feed,
    up_weight,
    down_weight,
):
    x = lax.axis_index("x")
    core = lax.axis_index("core")
    place = jnp.stack([x, core]).astype(jnp.int32)
    tok = tokens[0]
    cot = cotangent[0]
    wq = jnp.swapaxes(query_weight, 1, 2).reshape(OWN, D)
    wo = output_weight.reshape(OWN, D)
    wr = router_weight.T
    gain1 = gain_heads.reshape(1, D)
    gain2 = gain_feed.reshape(1, D)
    wqs = [wq] + around(wq, "x")

    hidden, kv, gates, slots = pl.pallas_call(
        prepare,
        out_shape=(
            shape((TOK, D)),
            shape((TOK, 2 * HEAD)),
            shape((EXPERTS, TOK), F32),
            shape((EXPERTS, TOK), jnp.int32),
        ),
        in_specs=[VMEM] * 5,
        out_specs=(VMEM,) * 4,
        name="prepare",
    )(tok, expert_ids[0].T, gain1, key_value_weight, wr)
    kvs = [kv] + around(kv, "x")
    wos = [wo] + around(wo, "x")

    qc, mixed, lse, kv_all = pl.pallas_call(
        attend,
        out_shape=(
            shape((HEAD, ROUTES)),
            shape((HEAD, ROUTES)),
            shape((1, ROUTES), F32),
            shape((LENGTH, 2 * HEAD)),
        ),
        in_specs=[SMEM] + [VMEM] * 10,
        out_specs=(VMEM,) * 4,
        scratch_shapes=[
            pltpu.VMEM((EXPERTS * HEAD, TOK), F32),
            pltpu.VMEM((LENGTH, HEAD), BF16),
            pltpu.VMEM((TILES, HEAD, TILE), BF16),
            pltpu.VMEM((1, LANES), F32),
            pltpu.VMEM((1, LANES), F32),
            pltpu.VMEM((HEAD, LANES), F32),
        ],
        compiler_params=pltpu.CompilerParams(vmem_limit_bytes=40 * MIB),
        name="attend",
    )(place, hidden, slots, *wqs, *kvs)

    result, grad_middle, gt, delta, grad_logits, small, keep, send = pl.pallas_call(
        middle_part,
        out_shape=(
            shape((TOK, D)),
            shape((TOK, D), F32),
            shape((HEAD, ROUTES)),
            shape((1, ROUTES), F32),
            shape((EXPERTS, TOK), F32),
            shape((32, D), F32),
            shape((64, 176, 128)),
            shape((64, 176, 128)),
        ),
        in_specs=[SMEM] + [VMEM] * 13,
        out_specs=(VMEM,) * 8,
        scratch_shapes=[
            pltpu.VMEM((EXPERTS * HEAD, TOK), BF16),
            pltpu.VMEM((TOK, D), BF16),
            pltpu.VMEM((D, TOK), BF16),
            pltpu.VMEM((TOK, D), F32),
            pltpu.VMEM((TOK, D), F32),
            pltpu.VMEM((TOK, D), F32),
            pltpu.VMEM((TOK, D), BF16),
            pltpu.VMEM((EXPERTS * HEAD, TOK), F32),
            pltpu.VMEM((EXPERTS, TOK), F32),
        ],
        compiler_params=pltpu.CompilerParams(vmem_limit_bytes=50 * MIB),
        name="middle_part",
    )(
        place,
        tok,
        cot,
        mixed,
        slots,
        gates,
        hidden,
        *wos,
        gain2,
        up_weight,
        down_weight,
    )

    chips = ("x", "y", "z")
    paired = (keep.astype(F32) + swap(send).astype(F32)).astype(BF16)
    pieces = lax.all_to_all(paired, chips, split_axis=0, concat_axis=0, tiled=True)

    own_pair, pair1, pair2, pair3, grad_rows, keep_q, send_q = pl.pallas_call(
        attend_back,
        out_shape=(
            shape((TOK, 2 * HEAD), F32),
            shape((TOK, 2 * HEAD)),
            shape((TOK, 2 * HEAD)),
            shape((TOK, 2 * HEAD)),
            shape((TOK, D), F32),
            shape((GROUPS, HALF, D)),
            shape((GROUPS, HALF, D)),
        ),
        in_specs=[SMEM] + [VMEM] * 11,
        out_specs=(VMEM,) * 7,
        scratch_shapes=[
            pltpu.VMEM((LENGTH, HEAD), BF16),
            pltpu.VMEM((LENGTH, HEAD), BF16),
            pltpu.VMEM((TILES, HEAD, TILE), BF16),
            pltpu.VMEM((ROUTES, HEAD), BF16),
            pltpu.VMEM((ROUTES, HEAD), BF16),
            pltpu.VMEM((LENGTH, HEAD), F32),
            pltpu.VMEM((LENGTH, HEAD), F32),
            pltpu.VMEM((HEAD, LANES), F32),
            pltpu.VMEM((HEAD, ROUTES), BF16),
            pltpu.VMEM((EXPERTS * HEAD, TOK), BF16),
            pltpu.VMEM((TILE, LANES), BF16),
            pltpu.VMEM((TILE, LANES), BF16),
        ],
        compiler_params=pltpu.CompilerParams(vmem_limit_bytes=40 * MIB),
        name="attend_back",
    )(place, qc, gt, lse, delta, kv_all, slots, hidden, *wqs)

    arrived = [
        lax.ppermute(pair, "x", turn(4, step))
        for step, pair in ((1, pair1), (2, pair2), (3, pair3))
    ]
    paired_q = (keep_q.astype(F32) + swap(send_q).astype(F32)).astype(BF16)
    parts = [lax.ppermute(paired_q[step], "x", turn(4, step)) for step in (1, 2, 3)]
    query_part = (
        paired_q[0].astype(F32)
        + parts[0].astype(F32)
        + parts[1].astype(F32)
        + parts[2].astype(F32)
    ).astype(BF16)
    query_part = total_over(total_over(query_part, "y"), "z")
    query_grad = jnp.concatenate(both(query_part, swap(query_part), core), axis=0)

    piece = jnp.sum(pieces.reshape(64, 176, 128).astype(F32), axis=0).astype(BF16)
    spread = lax.all_to_all(
        jnp.broadcast_to(piece[None], (64, 176, 128)), chips, split_axis=0, concat_axis=0, tiled=True
    )
    spread_other = swap(spread)
    half_spec = pl.BlockSpec((16, 176, 128), lambda index: (lax.rem(index, 4), 0, 0))
    grad_up, grad_down = pl.pallas_call(
        unpack,
        grid=(8,),
        out_shape=(shape((D, FF), F32), shape((FF, D), F32)),
        in_specs=[SMEM, half_spec, half_spec],
        out_specs=(
            pl.BlockSpec((D, CHUNK), lambda index: (0, index)),
            pl.BlockSpec((CHUNK, D), lambda index: (index, 0)),
        ),
        name="unpack",
    )(place, spread, spread_other)

    def output_half(value):
        value = lax.dynamic_slice(value, (16 * x, 128, 0), (16, 48, 128))
        return value.reshape(4, HALF, 128).swapaxes(0, 1).reshape(HALF, D)

    output_grad = jnp.concatenate(
        both(output_half(spread), output_half(spread_other), core), axis=0
    )

    grad_tokens, keep_s, send_s = pl.pallas_call(
        finish,
        out_shape=(
            shape((TOK, D)),
            shape((SMALL // 2, D)),
            shape((SMALL // 2, D)),
        ),
        in_specs=[SMEM] + [VMEM] * 13,
        out_specs=(VMEM,) * 3,
        compiler_params=pltpu.CompilerParams(vmem_limit_bytes=30 * MIB),
        name="finish",
    )(
        place,
        tok,
        hidden,
        grad_middle,
        grad_rows,
        grad_logits,
        wr,
        key_value_weight,
        gain1,
        own_pair,
        *arrived,
        small,
    )
    shared = (keep_s.astype(F32) + swap(send_s).astype(F32)).astype(BF16)
    for axis in chips:
        shared = total_over(shared, axis)
    shared = jnp.concatenate(both(shared, swap(shared), core), axis=0).astype(F32)
    return (
        result[None],
        grad_tokens[None],
        shared[153],
        shared[0:128].T,
        shared[128:152].T,
        query_grad.astype(F32).reshape(OWN // HEAD, HEAD, D).swapaxes(1, 2),
        output_grad.astype(F32).reshape(OWN // HEAD, HEAD, D),
        shared[152],
        grad_up,
        grad_down,
    )


def solution(mesh):
    grid = Mesh(mesh.devices.reshape(4, 4, 4, 2), ("x", "y", "z", "core"))
    dp = ("y", "z", "core")
    return jax.shard_map(
        shards,
        mesh=grid,
        in_specs=(
            P(dp, "x", None),
            P(dp, "x", None),
            P(dp, "x", None),
            P(),
            P(),
            P(),
            P("x", None, None),
            P("x", None, None),
            P(),
            P(),
            P(),
        ),
        out_specs=(
            P(dp, "x", None),
            P(dp, "x", None),
            P(),
            P(),
            P(),
            P("x", None, None),
            P("x", None, None),
            P(),
            P(),
            P(),
        ),
        check_vma=False,
    )
```

```python
from functools import partial

import jax
import jax.numpy as jnp
from jax import lax
from jax.experimental import pallas as pl
from jax.experimental.pallas import tpu as pltpu
from jax.sharding import Mesh, PartitionSpec as P

D = 512
HEAD = 64
EXPERTS = 24
TOPK = 8
FF = 2048
TOK = 512
GROUPS = 4
LENGTH = TOK * GROUPS
OWN = EXPERTS // GROUPS * HEAD
HALF = OWN // 2
TILE = 256
LANES = TOPK * TILE
TILES = LENGTH // TILE
ROUTES = TOK * TOPK
CHUNK = 256
SMALL = 160
PIECE = 48
EXTRA = 2 * PIECE + 16

EPSILON = 1e-06
CURVE_SCALE = 0.7978845608028654
CURVE_CUBIC = 0.044715
SCORE = HEAD**-0.5
SCORE2 = SCORE * 1.4426950408889634
LOW = -1e30

F32 = jnp.float32
BF16 = jnp.bfloat16
MIB = 1 << 20


def nn(a, b):
    return lax.dot_general(a, b, (((1,), (0,)), ((), ())), preferred_element_type=F32)


def nt(a, b):
    return lax.dot_general(a, b, (((1,), (1,)), ((), ())), preferred_element_type=F32)


def tn(a, b):
    return lax.dot_general(a, b, (((0,), (0,)), ((), ())), preferred_element_type=F32)


def split_two(value):
    high = value.astype(BF16)
    return high, (value - high.astype(F32)).astype(BF16)


def scale_of(rows):
    return lax.rsqrt(jnp.mean(rows * rows, axis=-1, keepdims=True) + EPSILON)


def lanes_of(tile, slot):
    return pl.ds(tile * LANES + slot * TILE, TILE)


def tokens_of(tile):
    return pl.ds(tile * TILE, TILE)


def block(index, size):
    return pl.ds(pl.multiple_of(index * size, size), size)


def slots_of(expert):
    return range(max(0, expert - (EXPERTS - TOPK)), min(TOPK - 1, expert) + 1)


def pairs_first(tok_ref, gain_ref, wkv_ref, first_ref, kv_ref):
    rows = tok_ref[...].astype(F32)
    first = (rows * scale_of(rows) * gain_ref[...]).astype(BF16)
    first_ref[...] = first[0:TILE]
    kv_ref[...] = nn(first, wkv_ref[...]).astype(BF16)


def prepare(
    first_ref,
    carried_ref,
    ids_ref,
    gain_ref,
    wr_ref,
    after1,
    after2,
    after3,
    hid_ref,
    turned_ref,
    gates_ref,
    slot_ref,
):
    rows = carried_ref[0:TILE].astype(F32)
    high = rows * scale_of(rows) * gain_ref[...]
    turned_ref[:, 0:TILE] = first_ref[...].astype(F32).T.astype(BF16)
    turned_ref[:, TILE:TOK] = high.T.astype(BF16)
    hidden = jnp.concatenate([first_ref[...], high.astype(BF16)], axis=0)
    hid_ref[...] = hidden
    logits = nt(wr_ref[...], hidden)
    ids = jnp.concatenate(
        [ids_ref[:, 0:TILE], carried_ref[TILE : TILE + 8, 0:TILE].astype(jnp.int32)], axis=1
    )
    names = lax.broadcasted_iota(jnp.int32, (EXPERTS, TOK), 0)
    chosen = names == ids[0:1]
    for route in range(1, TOPK):
        chosen = chosen | (names == ids[route : route + 1])
    count = jnp.where(chosen, 1.0, 0.0)
    below = lax.broadcasted_iota(jnp.int32, (EXPERTS, EXPERTS), 0) > lax.broadcasted_iota(
        jnp.int32, (EXPERTS, EXPERTS), 1
    )
    rank = nn(jnp.where(below, 1.0, 0.0).astype(BF16), count.astype(BF16))
    slot_ref[...] = jnp.where(chosen, rank, -1.0).astype(jnp.int32)
    peak = jnp.max(jnp.where(chosen, logits, -3e38), axis=0, keepdims=True)
    raised = jnp.where(chosen, jnp.exp(logits - peak), 0.0)
    gates_ref[...] = raised / jnp.sum(raised, axis=0, keepdims=True)


def compact(slot_ref, dense_ref, tile, slot):
    value = jnp.zeros((HEAD, TILE), F32)
    for expert in range(slot, slot + EXPERTS - TOPK + 1):
        here = slot_ref[pl.ds(expert, 1), tokens_of(tile)] == slot
        value = jnp.where(here, dense_ref[pl.ds(expert * HEAD, HEAD), tokens_of(tile)], value)
    return value


def expand(slot_ref, packed_ref, tile, expert):
    row = slot_ref[pl.ds(expert, 1), tokens_of(tile)]
    value = jnp.zeros((HEAD, TILE), F32)
    for slot in slots_of(expert):
        value = jnp.where(row == slot, packed_ref[:, lanes_of(tile, slot)].astype(F32), value)
    return value


def causal():
    return lax.broadcasted_iota(jnp.int32, (TILE, TILE), 0) <= lax.broadcasted_iota(
        jnp.int32, (TILE, TILE), 1
    )


def staged(count, *stages):
    for time in range(count + len(stages) - 1):
        for late, stage in enumerate(stages):
            if 0 <= time - late < count:
                stage(time - late)


def own_blocks(x):
    return 2 * x, 7 - 2 * x


def attend(
    turned_ref,
    slot_ref,
    mine_ref,
    other_ref,
    kv0,
    kv1,
    kv2,
    kv3,
    qc_ref,
    mixed_ref,
    lse_ref,
    kv_ref,
    qall,
    keys,
    vt,
    peak,
    acc,
    scores,
    shares,
):
    x = lax.axis_index("x")
    core = lax.axis_index("core")
    owners = [lax.rem(x + GROUPS - away, GROUPS) for away in range(GROUPS)]
    for owner, kv in zip(owners, (kv0, kv1, kv2, kv3)):
        turned = kv[:, HEAD : 2 * HEAD].astype(F32).T.astype(BF16)
        kv_ref[block(owner, TOK), :] = kv[...]
        keys[block(owner, TOK), :] = kv[:, 0:HEAD]
        vt[owner, 0:HEAD, :] = turned
        vt[owner, HEAD : HEAD + 16, :] = jnp.ones((16, 2 * TILE), BF16)
    for owner in range(GROUPS):
        qall[block(2 * owner + core, HALF), :] = nn(mine_ref[owner], turned_ref[...])
        qall[block(2 * owner + 1 - core, HALF), :] = nn(other_ref[owner], turned_ref[...])
    for tile in range(2):
        for slot in range(TOPK):
            qc_ref[:, lanes_of(tile, slot)] = compact(slot_ref, qall, tile, slot).astype(BF16)

    wide = 2 * TILE
    later = lax.broadcasted_iota(jnp.int32, (TILE, wide), 0) <= (
        lax.broadcasted_iota(jnp.int32, (TILE, wide), 1) & (TILE - 1)
    )
    later_two = lax.broadcasted_iota(jnp.int32, (wide, wide), 0) <= TILE + (
        lax.broadcasted_iota(jnp.int32, (wide, wide), 1) & (TILE - 1)
    )

    def step(tile, start, size, values, mask):
        fades = {}

        def multiply(unit):
            at = pl.ds(unit * wide, wide)
            route = pl.ds(tile * LANES + unit * wide, wide)
            scores[0:size, at] = nn(keys[pl.ds(start, size), :], qc_ref[:, route])

        def lift(unit):
            at = pl.ds(unit * wide, wide)
            value = scores[0:size, at]
            if mask is not None:
                value = jnp.where(mask, value, LOW)
            top = jnp.max(value, axis=0, keepdims=True)
            if mask is None:
                before = peak[:, at]
                top = jnp.maximum(before, top)
                fades[unit] = jnp.exp2((before - top) * SCORE2)
            shares[0:size, at] = jnp.exp2((value - top) * SCORE2).astype(BF16)
            peak[:, at] = top

        def gather(unit):
            at = pl.ds(unit * wide, wide)
            part = nn(values, shares[0:size, at])
            if mask is None:
                part = acc[:, at] * fades[unit] + part
            acc[:, at] = part

        staged(LANES // wide, multiply, lift, gather)

    for tile in range(2):
        if tile == 0:
            start = pl.multiple_of(2 * x * TILE, TILE)
            step(tile, start, TILE, vt[x, :, 0:TILE], later)
            count = x
        else:
            start = pl.multiple_of((3 - x) * wide, wide)
            step(tile, start, wide, vt[3 - x], later_two)
            count = 3 - x

        @pl.loop(0, count)
        def _(index):
            step(tile, pl.multiple_of(index * wide, wide), wide, vt[index], None)

        here = pl.ds(tile * LANES, LANES)
        total = acc[HEAD : HEAD + 1, :]
        mixed_ref[:, here] = (acc[0:HEAD, :] / total).astype(BF16)
        lse_ref[:, here] = peak[...] * SCORE2 + jnp.log2(total)


def feed_part(
    tok_ref,
    high_ref,
    cot_ref,
    cot_high_ref,
    mixed_ref,
    slot_ref,
    gates_ref,
    gain_ref,
    wo_hbm,
    up_hbm,
    down_hbm,
    out_ref,
    out_high_ref,
    middle_ref,
    back_ref,
    dense_ref,
    keep_hbm,
    send_hbm,
    feed,
    feed_t,
    cot,
    result,
    wo_ref,
    up_ref,
    down_ref,
    staging,
    sems,
    out_sems,
):
    core = lax.axis_index("core")
    sources = ((wo_hbm, wo_ref), (up_hbm, up_ref), (down_hbm, down_ref))
    loads = [
        pltpu.make_async_copy(source, target, sems.at[index])
        for index, (source, target) in enumerate(sources)
    ]
    for load in loads:
        load.start()
    for tile in range(2):
        for expert in range(EXPERTS):
            value = expand(slot_ref, mixed_ref, tile, expert)
            gate = gates_ref[pl.ds(expert, 1), tokens_of(tile)]
            dense_ref[pl.ds(expert * HEAD, HEAD), tokens_of(tile)] = (value * gate).astype(BF16)
    cot[0:TILE] = cot_ref[0:TILE]
    cot[TILE:TOK] = cot_high_ref[...]
    total = jnp.concatenate([tok_ref[0:TILE], high_ref[0:TILE]], axis=0).astype(F32)
    loads[0].wait()
    total = total + tn(dense_ref[...], wo_ref[...])
    middle_ref[...] = total
    feed32 = total * scale_of(total) * gain_ref[...]
    feed[...] = feed32.astype(BF16)
    feed_t[...] = feed32.T.astype(BF16)
    result[...] = total
    back_ref[...] = jnp.zeros_like(back_ref)
    loads[1].wait()
    loads[2].wait()

    def out_copy(index, target):
        return pltpu.make_async_copy(
            staging.at[index],
            target.at[pl.ds(pl.multiple_of(lax.rem(index, 4) * 16, 16), 16)],
            out_sems.at[index],
        )

    @pl.loop(0, FF // CHUNK)
    def _(index):
        up = up_ref[:, block(index, CHUNK)]
        down = down_ref[block(index, CHUNK), :]
        before = nn(feed[...], up)
        square = before * before
        curve = jnp.tanh(CURVE_SCALE * before * (1.0 + CURVE_CUBIC * square))
        rise = 0.5 * (1.0 + curve)
        active = (before * rise).astype(BF16)
        slope = rise + 0.5 * before * (1.0 - curve * curve) * (
            CURVE_SCALE * (1.0 + 3.0 * CURVE_CUBIC * square)
        )
        result[...] += nn(active, down)
        grad_before = (nt(cot[...], down) * slope).astype(BF16)
        back_ref[...] += nt(grad_before, up)
        grad_up = nn(feed_t[...], grad_before).astype(BF16).reshape(16, 32, CHUNK)
        grad_down = tn(active, cot[...]).astype(BF16).reshape(16, 16, D)
        for group in range(2):
            staging[index, :, pl.ds(32 * group, 32), :] = grad_up[
                :, :, 128 * group : 128 * group + 128
            ]
        for group in range(4):
            staging[index, :, pl.ds(64 + 16 * group, 16), :] = grad_down[
                :, :, 128 * group : 128 * group + 128
            ]
        mine = index // 4 == core

        @pl.when(mine)
        def _():
            out_copy(index, keep_hbm).start()

        @pl.when(jnp.logical_not(mine))
        def _():
            out_copy(index, send_hbm).start()

    out_ref[...] = result[...].astype(BF16)
    out_high_ref[...] = result[TILE:TOK].astype(BF16)
    for index in range(FF // CHUNK):
        out_copy(index, keep_hbm).wait()


def put_pieces(grad, owner, core, keep_ref, send_ref):
    def put(ref, half):
        part = grad[half * HALF : (half + 1) * HALF].reshape(4, PIECE, D)
        for group in range(4):
            ref[pl.ds(owner * 16 + 4 * group, 4), :, :] = part[
                :, :, 128 * group : 128 * group + 128
            ]

    @pl.when(core == 0)
    def _():
        put(keep_ref, 0)
        put(send_ref, 1)

    @pl.when(core == 1)
    def _():
        put(keep_ref, 1)
        put(send_ref, 0)


def norm_part(
    cot_ref,
    cot_high_ref,
    middle_ref,
    back_ref,
    dense_ref,
    gain_ref,
    gm_ref,
    turned_ref,
    gain_grad_ref,
    keep_ref,
    send_ref,
    gm16,
):
    core = lax.axis_index("core")
    total = middle_ref[...]
    scale = scale_of(total)
    unit = total * scale
    grad = back_ref[...]
    inner = grad * gain_ref[...]
    gain_grad_ref[...] = jnp.sum(grad * unit, axis=0, keepdims=True)
    cot = jnp.concatenate([cot_ref[0:TILE], cot_high_ref[...]], axis=0).astype(F32)
    grad_middle = cot + scale * (inner - unit * jnp.mean(inner * unit, axis=-1, keepdims=True))
    gm_ref[...] = grad_middle
    gm16[...] = grad_middle.astype(BF16)
    turned_ref[...] = grad_middle.T.astype(BF16)
    for owner in range(GROUPS):
        grad_out = nn(dense_ref[pl.ds(owner * OWN, OWN), :], gm16[...]).astype(BF16)
        put_pieces(grad_out, owner, core, keep_ref, send_ref)


def route_part(
    turned_ref,
    mixed_ref,
    slot_ref,
    gates_ref,
    hid_ref,
    wo_ref,
    gain_grad_ref,
    gt_ref,
    delta_ref,
    gl_ref,
    small_ref,
    gdense,
    sums,
):
    gdense[...] = nn(wo_ref[...], turned_ref[...])
    sums[...] = jnp.zeros_like(sums)
    for tile in range(2):
        for slot in range(TOPK):
            at = lanes_of(tile, slot)
            value = jnp.zeros((HEAD, TILE), F32)
            gate = jnp.zeros((1, TILE), F32)
            for expert in range(slot, slot + EXPERTS - TOPK + 1):
                here = slot_ref[pl.ds(expert, 1), tokens_of(tile)] == slot
                value = jnp.where(
                    here, gdense[pl.ds(expert * HEAD, HEAD), tokens_of(tile)], value
                )
                gate = jnp.where(here, gates_ref[pl.ds(expert, 1), tokens_of(tile)], gate)
            mixed = mixed_ref[:, at].astype(F32)
            dots = jnp.sum(mixed * value, axis=0, keepdims=True)
            rounded = (value * gate).astype(BF16)
            gt_ref[:, at] = rounded
            delta_ref[:, at] = jnp.sum(mixed * rounded.astype(F32), axis=0, keepdims=True)
            for expert in range(slot, slot + EXPERTS - TOPK + 1):
                here = slot_ref[pl.ds(expert, 1), tokens_of(tile)] == slot
                sums[pl.ds(expert, 1), tokens_of(tile)] += jnp.where(here, dots, 0.0)
    gates = gates_ref[...]
    dots = sums[...]
    grad_logits = gates * (dots - jnp.sum(gates * dots, axis=0, keepdims=True))
    gl_ref[...] = grad_logits
    high, low = split_two(grad_logits)
    small_ref[...] = jnp.concatenate(
        [
            nn(high, hid_ref[...]) + nn(low, hid_ref[...]),
            gain_grad_ref[...],
            jnp.zeros((7, D), F32),
        ],
        axis=0,
    )


def attend_back(
    qc_ref,
    gt_ref,
    lse_ref,
    delta_ref,
    kv_ref,
    after_ref,
    pair0,
    pair1,
    pair2,
    pair3,
    dqc,
    keys,
    values,
    kt,
    dkeys,
    dvalues,
    dq,
    scores,
    grads,
    shares,
    slopes,
):
    x = lax.axis_index("x")
    keys[...] = kv_ref[:, 0:HEAD]
    values[...] = kv_ref[:, HEAD : 2 * HEAD]
    for tile in range(TILES):
        kt[tile] = kv_ref[pl.ds(tile * TILE, TILE), 0:HEAD].astype(F32).T.astype(BF16)
    dkeys[...] = jnp.zeros_like(dkeys)
    dvalues[...] = jnp.zeros_like(dvalues)
    later = causal()
    for tile in range(2):
        last = own_blocks(x)[tile]
        dq[...] = jnp.zeros_like(dq)

        def step(index, masked):
            at = block(index, TILE)
            sums = {}

            def multiply(slot):
                here = pl.ds(slot * TILE, TILE)
                route = lanes_of(tile, slot)
                scores[:, here] = nn(keys[at, :], qc_ref[:, route])
                grads[:, here] = nn(values[at, :], gt_ref[:, route])

            def lift(slot):
                here = pl.ds(slot * TILE, TILE)
                route = lanes_of(tile, slot)
                value = jnp.exp2(scores[:, here] * SCORE2 - lse_ref[:, route])
                if masked:
                    value = jnp.where(later, value, 0.0)
                shares[:, here] = value.astype(BF16)
                slopes[:, here] = (value * (grads[:, here] - delta_ref[:, route])).astype(BF16)

            def gather(slot):
                here = pl.ds(slot * TILE, TILE)
                route = lanes_of(tile, slot)
                dq[:, here] += nn(kt[index], slopes[:, here])
                one = nt(qc_ref[:, route], slopes[:, here])
                two = nt(gt_ref[:, route], shares[:, here])
                if slot:
                    one, two = sums[0] + one, sums[1] + two
                sums[0], sums[1] = one, two

            staged(TOPK, multiply, lift, gather)
            dkeys[index] += sums[0]
            dvalues[index] += sums[1]

        step(last, True)

        @pl.loop(0, last)
        def _(index):
            step(index, False)

        dqc[:, pl.ds(tile * LANES, LANES)] = (dq[...] * SCORE).astype(BF16)

    def pair(low, high):
        return jnp.concatenate(
            [
                jnp.concatenate([dkeys[low], dkeys[high]], axis=1) * SCORE,
                jnp.concatenate([dvalues[low], dvalues[high]], axis=1),
            ],
            axis=0,
        ).astype(BF16)

    for away, ref in enumerate((pair0, pair1, pair2, pair3)):
        ref[...] = pair(*own_blocks(lax.rem(x + away, GROUPS)))


def query_part(
    dqc,
    slot_ref,
    hid_ref,
    small_ref,
    wr_ref,
    mine_ref,
    other_ref,
    dqall,
    gain_ref,
    keep_ref,
    send_ref,
):
    core = lax.axis_index("core")
    for tile in range(2):
        for expert in range(EXPERTS):
            dqall[pl.ds(expert * HEAD, HEAD), tokens_of(tile)] = expand(
                slot_ref, dqc, tile, expert
            ).astype(BF16)
    gain = jnp.sum(
        small_ref[0:EXPERTS] * wr_ref[...].astype(F32), axis=0, keepdims=True
    )
    for owner in range(GROUPS):
        grad = nn(dqall[pl.ds(owner * OWN, OWN), :], hid_ref[...])
        put_pieces(grad.astype(BF16), owner, core, keep_ref, send_ref)
        one, two = mine_ref[owner].astype(F32), other_ref[owner].astype(F32)
        first, last = jnp.where(core == 0, one, two), jnp.where(core == 0, two, one)
        gain = gain + jnp.sum(grad[0:HALF] * first, axis=0, keepdims=True)
        gain = gain + jnp.sum(grad[HALF:OWN] * last, axis=0, keepdims=True)
    gain_ref[...] = gain


def finish(
    tok_ref,
    high_ref,
    gm_ref,
    dqall,
    gl_ref,
    wr_ref,
    mine_ref,
    other_ref,
    pairs_ref,
    wkv_ref,
    gain_ref,
    out_ref,
    out_high_ref,
):
    core = lax.axis_index("core")
    high, low = split_two(gl_ref[...])
    grad = tn(high, wr_ref[...]) + tn(low, wr_ref[...])
    for owner in range(GROUPS):
        grad = grad + tn(dqall[block(2 * owner + core, HALF), :], mine_ref[owner])
        grad = grad + tn(dqall[block(2 * owner + 1 - core, HALF), :], other_ref[owner])
    grad = grad + lax.dot_general(
        pairs_ref[...], wkv_ref[...], (((0,), (1,)), ((), ())), preferred_element_type=F32
    )
    rows = jnp.concatenate([tok_ref[0:TILE], high_ref[0:TILE]], axis=0).astype(F32)
    scale = scale_of(rows)
    unit = rows * scale
    inner = grad * gain_ref[...]
    result = (
        gm_ref[...] + scale * (inner - unit * jnp.mean(inner * unit, axis=-1, keepdims=True))
    ).astype(BF16)
    out_ref[...] = result
    out_high_ref[...] = result[TILE:TOK]


def added(near, one, two, three):
    return (
        (near.astype(F32) + two.astype(F32)) + (one.astype(F32) + three.astype(F32))
    ).astype(BF16)


def pair_feed(keep_ref, arrived_ref, keep_o, arrived_o, out_ref):
    out_ref[:, 0:128, :] = (keep_ref[...].astype(F32) + arrived_ref[...].astype(F32)).astype(BF16)
    out_ref[:, 128:176, :] = (keep_o[...].astype(F32) + arrived_o[...].astype(F32)).astype(BF16)


def merge(
    pieces_ref,
    keep_q,
    arrived_q,
    near,
    one,
    two,
    three,
    hid_ref,
    small_ref,
    gain_rows,
    wkv_ref,
    gain_ref,
    out_ref,
    part_ref,
    pair_ref,
):
    pair = added(near[...], one[...], two[...], three[...])
    pair_ref[...] = pair
    grad_kv = nn(pair, hid_ref[...])
    gain_grad = (
        gain_rows[...]
        + jnp.sum(grad_kv * wkv_ref[...].astype(F32).T, axis=0, keepdims=True)
    ) / gain_ref[...]
    last = jnp.concatenate([small_ref[0:25], gain_grad, small_ref[26:32]], axis=0)
    shared = jnp.concatenate([grad_kv, last], axis=0).astype(BF16)
    total = pieces_ref[0].astype(F32)
    for index in range(1, 64):
        total = total + pieces_ref[index].astype(F32)
    total = total.astype(BF16)
    part_ref[...] = total[128:176]
    for index in range(64):
        out_ref[index, 0:128] = total[0:128]
    out_ref[:, 128:176, :] = (keep_q[...].astype(F32) + arrived_q[...].astype(F32)).astype(BF16)
    for index in range(64):
        row, group = index // 4, index % 4
        if 16 * row < SMALL:
            value = shared[16 * row : 16 * row + 16, 128 * group : 128 * group + 128]
        else:
            value = jnp.zeros((16, 128), BF16)
        out_ref[index, 176:192] = value


def collect(spread, part_ref, feed_hbm, out_ref, feed, rest, sems):
    loads = [
        pltpu.make_async_copy(spread.at[:, pl.ds(0, 128), :], feed, sems.at[0]),
        pltpu.make_async_copy(spread.at[:, pl.ds(128, 64), :], rest, sems.at[1]),
    ]
    copy = pltpu.make_async_copy(feed, feed_hbm, sems.at[2])
    for load in loads:
        load.start()
    loads[0].wait()
    copy.start()
    loads[1].wait()
    total = rest[0].astype(F32)
    for index in range(1, 64):
        total = total + rest[index].astype(F32)
    total = total.astype(BF16)
    for index in range(16):
        out_ref[index, 0:PIECE] = part_ref[...]
        out_ref[index, PIECE:EXTRA] = total
    copy.wait()


def small_part(pieces_ref, other_ref, out_ref):
    for row in range(4):
        for group in range(4):
            at = 4 * row + group
            mine = pieces_ref[at, 2 * PIECE : EXTRA, :].astype(F32)
            other = other_ref[at, 2 * PIECE : EXTRA, :].astype(F32)
            out_ref[16 * row : 16 * row + 16, 128 * group : 128 * group + 128] = (
                mine + other
            ).astype(BF16)


def unpack(at_ref, half_ref, *refs):
    up_ref, down_ref = refs[-2:]
    for group in range(2):
        up_ref[:, 128 * group : 128 * group + 128] = (
            half_ref[:, pl.ds(32 * group, 32), :].astype(F32).reshape(D, 128)
        )
    for group in range(4):
        down_ref[:, 128 * group : 128 * group + 128] = (
            half_ref[:, pl.ds(64 + 16 * group, 16), :].astype(F32).reshape(CHUNK, 128)
        )


def assemble(mine_ref, other_ref, output_ref, query_ref):
    core = lax.axis_index("core")
    for ref, half in ((mine_ref, core), (other_ref, 1 - core)):
        for column in range(4):
            for row in range(4):
                rows = pl.ds(pl.multiple_of(half * HALF + row * PIECE, 16), PIECE)
                for index, target in enumerate((output_ref, query_ref)):
                    target[rows, pl.ds(128 * column, 128)] = ref[
                        4 * column + row, pl.ds(PIECE * index, PIECE), :
                    ].astype(F32)


def share_out(near, one, two, three, kv_ref, router_ref, heads_ref, feed_ref, shared):
    x = lax.axis_index("x")
    for away, value in enumerate((near, one, two, three)):
        shared[block(lax.rem(x + GROUPS - away, GROUPS), 64), :] = value[...].astype(F32)
    kv_ref[...] = shared[0:128].T
    router_ref[...] = shared[128:152]
    feed_ref[...] = shared[152:153]
    heads_ref[...] = shared[153:154]


def shape(dims, dtype=BF16):
    return jax.ShapeDtypeStruct(dims, dtype)


VMEM = pl.BlockSpec(memory_space=pltpu.VMEM)
SMEM = pl.BlockSpec(memory_space=pltpu.SMEM)
HBM = pl.BlockSpec(memory_space=pltpu.HBM)


def nothing(*refs):
    pass


def after(value, *others):
    return pl.pallas_call(
        nothing,
        out_shape=shape(value.shape, value.dtype),
        in_specs=[HBM] * (1 + len(others)),
        out_specs=HBM,
        input_output_aliases={0: 0},
        name="after",
    )(value, *others)


def call(kernel, micros, inputs, outputs, scratch=(), far=(), far_out=(), limit=60):
    near = [index for index in range(len(inputs)) if index not in far]
    count, ends = len(inputs), len(inputs) + len(outputs)

    def body(*refs):
        sources, results, own = list(refs[:count]), refs[count:ends], refs[ends:]
        buffers, sems = own[len(scratch) : -1], own[-1]
        loads = []
        for index, (source, buffer) in enumerate(zip(near, buffers)):
            loads.append(pltpu.make_async_copy(sources[source], buffer, sems.at[index]))
            sources[source] = buffer
        for load in loads:
            load.start()
        for load in loads:
            load.wait()
        kernel(*sources, *results, *own[: len(scratch)])

    return pl.pallas_call(
        body,
        out_shape=outputs,
        in_specs=[HBM for index in range(count)],
        out_specs=tuple(HBM if index in far_out else VMEM for index in range(len(outputs))),
        scratch_shapes=[
            *scratch,
            *[pltpu.VMEM(inputs[index].shape, inputs[index].dtype) for index in near],
            pltpu.SemaphoreType.DMA((len(near),)),
        ],
        compiler_params=pltpu.CompilerParams(vmem_limit_bytes=limit * MIB),
        cost_estimate=pl.CostEstimate(
            flops=int(micros * 1e9), bytes_accessed=1 << 20, transcendentals=0
        ),
        name=kernel.__name__,
    )(*inputs)


def turn(size, step):
    return [(index, (index + step) % size) for index in range(size)]


def swap(value):
    return lax.ppermute(value, "core", turn(2, 1))


def mirror(value):
    return lax.ppermute(value, "x", [(0, 3), (3, 0), (1, 2), (2, 1)])


def around(value, axis):
    return [lax.ppermute(value, axis, turn(4, step)) for step in (1, 2, 3)]


def vmem(dims, dtype=F32):
    return pltpu.VMEM(dims, dtype)


def shards(
    tokens,
    expert_ids,
    cotangent,
    gain_heads,
    key_value_weight,
    router_weight,
    query_weight,
    output_weight,
    gain_feed,
    up_weight,
    down_weight,
):
    x = lax.axis_index("x")
    core = lax.axis_index("core")
    chips = ("x", "y", "z")
    tok = tokens[0]
    cot = cotangent[0]
    ids = expert_ids[0].T
    wq = jnp.swapaxes(query_weight, 1, 2).reshape(OWN, D)
    wr = router_weight.T
    wkv = key_value_weight
    gain1 = gain_heads.reshape(1, D)
    gain2 = gain_feed.reshape(1, D)

    carried = jnp.concatenate(
        [
            tok[TILE:TOK],
            jnp.pad(ids[:, TILE:TOK].astype(BF16), ((0, 8), (0, D - TILE))),
        ],
        axis=0,
    )
    carried = mirror(carried)
    mine = lax.dynamic_slice(wq, (core * HALF, 0), (HALF, D))
    mine = lax.all_to_all(
        jnp.broadcast_to(mine[None], (GROUPS, HALF, D)), "x", split_axis=0, concat_axis=0, tiled=True
    )
    wo = lax.all_gather(output_weight.reshape(OWN, D), "x", axis=0, tiled=True)
    first, kv = call(
        pairs_first,
        2,
        (tok, gain1, wkv),
        (shape((TILE, D)), shape((TOK, 2 * HEAD))),
    )
    kvs = [kv] + around(kv, "x")
    hidden, turned, gates, slots = call(
        prepare,
        3,
        (first, carried, ids, gain1, wr, *kvs[1:]),
        (
            shape((TOK, D)),
            shape((D, TOK)),
            shape((EXPERTS, TOK), F32),
            shape((EXPERTS, TOK), jnp.int32),
        ),
        far=(5, 6, 7),
    )
    mine = after(mine, slots)
    wqs = (mine, swap(mine))
    cot_high = mirror(after(cot[TILE:TOK], slots))

    qc, mixed, lse, kv_all = call(
        attend,
        15,
        (turned, slots, *wqs, *kvs),
        (
            shape((HEAD, ROUTES)),
            shape((HEAD, ROUTES)),
            shape((1, ROUTES), F32),
            shape((LENGTH, 2 * HEAD)),
        ),
        [
            vmem((EXPERTS * HEAD, TOK)),
            vmem((LENGTH, HEAD), BF16),
            vmem((GROUPS, HEAD + 16, 2 * TILE), BF16),
            vmem((1, LANES)),
            vmem((HEAD + 16, LANES)),
            vmem((2 * TILE, LANES)),
            vmem((2 * TILE, LANES), BF16),
        ],
    )

    result, out_high, middle, back, dense, keep, send = call(
        feed_part,
        17,
        (
            tok,
            carried,
            cot,
            cot_high,
            mixed,
            slots,
            gates,
            gain2,
            wo,
            up_weight,
            down_weight,
        ),
        (
            shape((TOK, D)),
            shape((TILE, D)),
            shape((TOK, D), F32),
            shape((TOK, D), F32),
            shape((EXPERTS * HEAD, TOK)),
            shape((64, 128, 128)),
            shape((64, 128, 128)),
        ),
        [
            vmem((TOK, D), BF16),
            vmem((D, TOK), BF16),
            vmem((TOK, D), BF16),
            vmem((TOK, D)),
            vmem((EXPERTS * HEAD, D), BF16),
            vmem((D, FF), BF16),
            vmem((FF, D), BF16),
            vmem((8, 16, 128, 128), BF16),
            pltpu.SemaphoreType.DMA((3,)),
            pltpu.SemaphoreType.DMA((8,)),
        ],
        far=(9, 10, 11),
        far_out=(5, 6),
    )
    arrived = swap(send)
    out_back = mirror(out_high)

    grad_middle, turned_gm, gain_grad, keep_o, send_o = call(
        norm_part,
        4,
        (cot, cot_high, middle, back, dense, gain2),
        (
            shape((TOK, D), F32),
            shape((D, TOK)),
            shape((1, D), F32),
            shape((64, PIECE, 128)),
            shape((64, PIECE, 128)),
        ),
        [vmem((TOK, D), BF16)],
    )
    gt, delta, grad_logits, small = call(
        route_part,
        6,
        (turned_gm, mixed, slots, gates, hidden, wo, gain_grad),
        (
            shape((HEAD, ROUTES)),
            shape((1, ROUTES), F32),
            shape((EXPERTS, TOK), F32),
            shape((32, D), F32),
        ),
        [vmem((EXPERTS * HEAD, TOK)), vmem((EXPERTS, TOK))],
    )
    arrived_o = swap(send_o)
    full_spec = pl.BlockSpec((16, 128, 128), lambda index: (index, 0, 0))
    out_spec = pl.BlockSpec((16, PIECE, 128), lambda index: (index, 0, 0))
    paired = pl.pallas_call(
        pair_feed,
        grid=(4,),
        out_shape=shape((64, 176, 128)),
        in_specs=[full_spec, full_spec, out_spec, out_spec],
        out_specs=pl.BlockSpec((16, 176, 128), lambda index: (index, 0, 0)),
        compiler_params=pltpu.CompilerParams(vmem_limit_bytes=60 * MIB),
        name="pair_feed",
    )(keep, arrived, keep_o, arrived_o)
    pieces = lax.all_to_all(paired, chips, split_axis=0, concat_axis=0, tiled=True)

    pair, *others, dqc = call(
        attend_back,
        20,
        (qc, gt, lse, delta, kv_all, out_back),
        (
            *[shape((2 * HEAD, TOK))] * GROUPS,
            shape((HEAD, ROUTES)),
        ),
        [
            vmem((LENGTH, HEAD), BF16),
            vmem((LENGTH, HEAD), BF16),
            vmem((TILES, HEAD, TILE), BF16),
            vmem((TILES, HEAD, TILE)),
            vmem((TILES, HEAD, TILE)),
            vmem((HEAD, LANES)),
            vmem((TILE, LANES)),
            vmem((TILE, LANES)),
            vmem((TILE, LANES), BF16),
            vmem((TILE, LANES), BF16),
        ],
        far=(5,),
    )
    arrived_pairs = [
        lax.ppermute(value, "x", turn(4, step + 1)) for step, value in enumerate(others)
    ]
    dqall, gain_rows, keep_q, send_q = call(
        query_part,
        6,
        (dqc, slots, hidden, small, wr, *wqs),
        (
            shape((EXPERTS * HEAD, TOK)),
            shape((1, D), F32),
            shape((64, PIECE, 128)),
            shape((64, PIECE, 128)),
        ),
    )
    arrived_q = swap(send_q)
    merged, part, pair_sum = call(
        merge,
        5,
        (
            pieces,
            keep_q,
            arrived_q,
            pair,
            *arrived_pairs,
            hidden,
            small,
            gain_rows,
            wkv,
            gain1,
        ),
        (shape((64, 192, 128)), shape((PIECE, 128)), shape((2 * HEAD, TOK))),
    )
    grad_whole, grad_high = call(
        finish,
        3,
        (tok, carried, grad_middle, dqall, grad_logits, wr, *wqs, pair_sum, wkv, gain1),
        (shape((TOK, D)), shape((TILE, D))),
    )
    spread = lax.all_to_all(merged, chips, split_axis=0, concat_axis=0, tiled=True)
    spread = after(spread, grad_high)
    grad_tokens = lax.dynamic_update_slice(grad_whole, mirror(grad_high), (TILE, 0))
    result = lax.dynamic_update_slice(result, out_back, (TILE, 0))
    feed_spread, part = call(
        collect,
        3,
        (spread, part),
        (shape((64, 128, 128)), shape((16, EXTRA, 128))),
        [
            vmem((64, 128, 128), BF16),
            vmem((64, 64, 128), BF16),
            pltpu.SemaphoreType.DMA((3,)),
        ],
        far=(0,),
        far_out=(0,),
    )
    feed_other = swap(feed_spread)
    part = lax.all_to_all(part, ("y", "z"), split_axis=0, concat_axis=0, tiled=True)

    def unpacked(value, half, *earlier):
        half_spec = pl.BlockSpec((16, 128, 128), lambda index, at: (index, 0, 0))
        return pl.pallas_call(
            unpack,
            grid_spec=pltpu.PrefetchScalarGridSpec(
                num_scalar_prefetch=1,
                grid=(4,),
                in_specs=[half_spec] + [HBM] * len(earlier),
                out_specs=(
                    pl.BlockSpec((D, CHUNK), lambda index, at: (0, 4 * at[0] + index)),
                    pl.BlockSpec((CHUNK, D), lambda index, at: (4 * at[0] + index, 0)),
                ),
            ),
            out_shape=(shape((D, FF), F32), shape((FF, D), F32)),
            input_output_aliases={2: 0, 3: 1} if earlier else {},
            compiler_params=pltpu.CompilerParams(vmem_limit_bytes=60 * MIB),
            name="unpack",
        )(half.reshape(1), value, *earlier)

    grads = unpacked(feed_spread, core)
    part = after(part, grads[0])
    part_other = swap(part)
    (shared,) = call(small_part, 1, (part, part_other), (shape((64, D)),))
    shareds = [shared] + around(shared, "x")
    grad_up, grad_down = unpacked(feed_other, 1 - core, *grads)

    output_grad, query_grad = call(
        assemble,
        2,
        (part, part_other),
        (shape((OWN, D), F32), shape((OWN, D), F32)),
    )
    kv_grad, router_grad, gain_heads_grad, gain_feed_grad = call(
        share_out,
        1,
        shareds,
        (shape((D, 2 * HEAD), F32), shape((EXPERTS, D), F32))
        + (shape((1, D), F32),) * 2,
        [vmem((256, D))],
    )

    return (
        result[None],
        grad_tokens[None],
        gain_heads_grad.reshape(D),
        kv_grad,
        router_grad.T,
        query_grad.reshape(OWN // HEAD, HEAD, D).swapaxes(1, 2),
        output_grad.reshape(OWN // HEAD, HEAD, D),
        gain_feed_grad.reshape(D),
        grad_up,
        grad_down,
    )


def solution(mesh):
    grid = Mesh(mesh.devices.reshape(4, 4, 4, 2), ("x", "y", "z", "core"))
    dp = ("y", "z", "core")
    return jax.shard_map(
        shards,
        mesh=grid,
        in_specs=(
            P(dp, "x", None),
            P(dp, "x", None),
            P(dp, "x", None),
            P(),
            P(),
            P(),
            P("x", None, None),
            P("x", None, None),
            P(),
            P(),
            P(),
        ),
        out_specs=(
            P(dp, "x", None),
            P(dp, "x", None),
            P(),
            P(),
            P(),
            P("x", None, None),
            P("x", None, None),
            P(),
            P(),
            P(),
        ),
        check_vma=False,
    )
```

```python
import math

import jax
import jax.numpy as jnp
from jax import lax
from jax.experimental import pallas as pl
from jax.experimental.pallas import tpu as pltpu
from jax.sharding import Mesh, PartitionSpec as P

D = 512
HEAD = 64
EXPERTS = 24
TOPK = 8
FF = 2048
TOK = 512
GROUPS = 4
LENGTH = TOK * GROUPS
OWN = EXPERTS // GROUPS * HEAD
HALF = OWN // 2
TILE = 256
LANES = TOPK * TILE
TILES = LENGTH // TILE
ROUTES = TOK * TOPK
CHUNK = 256
SMALL = 160
PIECE = 48
EXTRA = 3 * PIECE

EPSILON = 1e-06
CURVE_SCALE = 0.7978845608028654
CURVE_CUBIC = 0.044715
SCORE = HEAD**-0.5
SCORE2 = SCORE * 1.4426950408889634
LOW = -1e30

F32 = jnp.float32
BF16 = jnp.bfloat16
MIB = 1 << 20
LIMIT = 62 * MIB - (1 << 18)


def nn(a, b):
    return lax.dot_general(a, b, (((1,), (0,)), ((), ())), preferred_element_type=F32)


def nt(a, b):
    return lax.dot_general(a, b, (((1,), (1,)), ((), ())), preferred_element_type=F32)


def tn(a, b):
    return lax.dot_general(a, b, (((0,), (0,)), ((), ())), preferred_element_type=F32)


def split_two(value):
    high = value.astype(BF16)
    return high, (value - high.astype(F32)).astype(BF16)


def scale_of(rows):
    return lax.rsqrt(jnp.mean(rows * rows, axis=-1, keepdims=True) + EPSILON)


def lanes_of(tile, slot):
    return pl.ds(tile * LANES + slot * TILE, TILE)


def tokens_of(tile):
    return pl.ds(tile * TILE, TILE)


def block(index, size):
    return pl.ds(pl.multiple_of(index * size, size), size)


def slots_of(expert):
    return range(max(0, expert - (EXPERTS - TOPK)), min(TOPK - 1, expert) + 1)


def pairs_first(tok_ref, gain_ref, wkv_ref, first_ref, kv_ref):
    rows = tok_ref[...].astype(F32)
    first = (rows * scale_of(rows) * gain_ref[...]).astype(BF16)
    first_ref[...] = first[0:TILE]
    kv_ref[...] = nn(first, wkv_ref[...]).astype(BF16)


def prepare(
    first_ref,
    carried_ref,
    ids_ref,
    gain_ref,
    wr_ref,
    cot_ref,
    after1,
    after2,
    after3,
    cot_high_ref,
    hid_ref,
    turned_ref,
    gates_ref,
    slot_ref,
):
    cot_high_ref[...] = cot_ref[TILE:TOK]
    rows = carried_ref[0:TILE].astype(F32)
    high = rows * scale_of(rows) * gain_ref[...]
    turned_ref[:, 0:TILE] = first_ref[...].astype(F32).T.astype(BF16)
    turned_ref[:, TILE:TOK] = high.T.astype(BF16)
    hidden = jnp.concatenate([first_ref[...], high.astype(BF16)], axis=0)
    hid_ref[...] = hidden
    logits = nt(wr_ref[...], hidden)
    ids = jnp.concatenate(
        [ids_ref[:, 0:TILE], carried_ref[TILE : TILE + 8, 0:TILE].astype(jnp.int32)], axis=1
    )
    names = lax.broadcasted_iota(jnp.int32, (EXPERTS, TOK), 0)
    chosen = names == ids[0:1]
    for route in range(1, TOPK):
        chosen = chosen | (names == ids[route : route + 1])
    count = jnp.where(chosen, 1.0, 0.0)
    below = lax.broadcasted_iota(jnp.int32, (EXPERTS, EXPERTS), 0) > lax.broadcasted_iota(
        jnp.int32, (EXPERTS, EXPERTS), 1
    )
    rank = nn(jnp.where(below, 1.0, 0.0).astype(BF16), count.astype(BF16))
    slot_ref[...] = jnp.where(chosen, rank, -1.0).astype(jnp.int32)
    peak = jnp.max(jnp.where(chosen, logits, -3e38), axis=0, keepdims=True)
    raised = jnp.where(chosen, jnp.exp(logits - peak), 0.0)
    gates_ref[...] = raised / jnp.sum(raised, axis=0, keepdims=True)


def compact(slot_ref, dense_ref, tile, slot):
    value = jnp.zeros((HEAD, TILE), F32)
    for expert in range(slot, slot + EXPERTS - TOPK + 1):
        here = slot_ref[pl.ds(expert, 1), tokens_of(tile)] == slot
        value = jnp.where(here, dense_ref[pl.ds(expert * HEAD, HEAD), tokens_of(tile)], value)
    return value


def expand(slot_ref, packed_ref, tile, expert):
    row = slot_ref[pl.ds(expert, 1), tokens_of(tile)]
    value = jnp.zeros((HEAD, TILE), F32)
    for slot in slots_of(expert):
        value = jnp.where(row == slot, packed_ref[:, lanes_of(tile, slot)].astype(F32), value)
    return value


def causal():
    return lax.broadcasted_iota(jnp.int32, (TILE, TILE), 0) <= lax.broadcasted_iota(
        jnp.int32, (TILE, TILE), 1
    )


def staged(count, *stages):
    for time in range(count + len(stages) - 1):
        for late, stage in enumerate(stages):
            if 0 <= time - late < count:
                stage(time - late)


def own_blocks(x):
    return 2 * x, 7 - 2 * x


def attend(
    turned_ref,
    slot_ref,
    gates_ref,
    mine_ref,
    other_ref,
    kv0,
    kv1,
    kv2,
    kv3,
    qc_ref,
    mixed_ref,
    lse_ref,
    kv_ref,
    dense_ref,
    qall,
    keys,
    vt,
    peak,
    acc,
    scores,
    shares,
):
    x = lax.axis_index("x")
    core = lax.axis_index("core")
    owners = [lax.rem(x + GROUPS - away, GROUPS) for away in range(GROUPS)]
    for owner, kv in zip(owners, (kv0, kv1, kv2, kv3)):
        turned = kv[:, HEAD : 2 * HEAD].astype(F32).T.astype(BF16)
        kv_ref[block(owner, TOK), :] = kv[...]
        keys[block(owner, TOK), :] = kv[:, 0:HEAD]
        vt[owner, 0:HEAD, :] = turned
        vt[owner, HEAD : HEAD + 16, :] = jnp.ones((16, 2 * TILE), BF16)
    for owner in range(GROUPS):
        qall[block(2 * owner + core, HALF), :] = nn(mine_ref[owner], turned_ref[...])
        qall[block(2 * owner + 1 - core, HALF), :] = nn(other_ref[owner], turned_ref[...])
    for tile in range(2):
        for slot in range(TOPK):
            qc_ref[:, lanes_of(tile, slot)] = compact(slot_ref, qall, tile, slot).astype(BF16)

    wide = 2 * TILE
    later = lax.broadcasted_iota(jnp.int32, (TILE, wide), 0) <= (
        lax.broadcasted_iota(jnp.int32, (TILE, wide), 1) & (TILE - 1)
    )
    later_two = lax.broadcasted_iota(jnp.int32, (wide, wide), 0) <= TILE + (
        lax.broadcasted_iota(jnp.int32, (wide, wide), 1) & (TILE - 1)
    )

    def step(tile, start, size, values, mask):
        fades = {}

        def multiply(unit):
            at = pl.ds(unit * wide, wide)
            route = pl.ds(tile * LANES + unit * wide, wide)
            scores[0:size, at] = nn(keys[pl.ds(start, size), :], qc_ref[:, route])

        def lift(unit):
            at = pl.ds(unit * wide, wide)
            value = scores[0:size, at]
            if mask is not None:
                value = jnp.where(mask, value, LOW)
            top = jnp.max(value, axis=0, keepdims=True)
            if mask is None:
                before = peak[:, at]
                top = jnp.maximum(before, top)
                fades[unit] = jnp.exp2((before - top) * SCORE2)
            shares[0:size, at] = jnp.exp2((value - top) * SCORE2).astype(BF16)
            peak[:, at] = top

        def gather(unit):
            at = pl.ds(unit * wide, wide)
            part = nn(values, shares[0:size, at])
            if mask is None:
                part = acc[:, at] * fades[unit] + part
            acc[:, at] = part

        staged(LANES // wide, multiply, lift, gather)

    for tile in range(2):
        if tile == 0:
            start = pl.multiple_of(2 * x * TILE, TILE)
            step(tile, start, TILE, vt[x, :, 0:TILE], later)
            count = x
        else:
            start = pl.multiple_of((3 - x) * wide, wide)
            step(tile, start, wide, vt[3 - x], later_two)
            count = 3 - x

        @pl.loop(0, count)
        def _(index):
            step(tile, pl.multiple_of(index * wide, wide), wide, vt[index], None)

        here = pl.ds(tile * LANES, LANES)
        total = acc[HEAD : HEAD + 1, :]
        mixed_ref[:, here] = (acc[0:HEAD, :] / total).astype(BF16)
        lse_ref[:, here] = peak[...] * SCORE2 + jnp.log2(total)
    for tile in range(2):
        for expert in range(EXPERTS):
            value = expand(slot_ref, mixed_ref, tile, expert)
            gate = gates_ref[pl.ds(expert, 1), tokens_of(tile)]
            dense_ref[pl.ds(expert * HEAD, HEAD), tokens_of(tile)] = (value * gate).astype(BF16)


def feed_part(
    arrive,
    tok_ref,
    high_ref,
    cot_ref,
    cot_high_ref,
    dense_ref,
    gain_ref,
    wo_hbm,
    up_hbm,
    down_hbm,
    out_ref,
    out_high_ref,
    middle_ref,
    back_ref,
    keep_hbm,
    send_hbm,
    feed,
    feed_t,
    cot,
    result,
    wo_ref,
    up_ref,
    down_ref,
    staging,
    sems,
    out_sems,
):
    core = lax.axis_index("core")
    sources = ((wo_hbm, wo_ref), (up_hbm, up_ref), (down_hbm, down_ref))
    loads = [
        pltpu.make_async_copy(source, target, sems.at[index])
        for index, (source, target) in enumerate(sources)
    ]
    for load in loads:
        load.start()
    arrive()
    cot[0:TILE] = cot_ref[0:TILE]
    cot[TILE:TOK] = cot_high_ref[...]
    total = jnp.concatenate([tok_ref[0:TILE], high_ref[0:TILE]], axis=0).astype(F32)
    loads[0].wait()
    total = total + tn(dense_ref[...], wo_ref[...])
    middle_ref[...] = total
    feed32 = total * scale_of(total) * gain_ref[...]
    feed[...] = feed32.astype(BF16)
    feed_t[...] = feed32.T.astype(BF16)
    result[...] = total
    back_ref[...] = jnp.zeros_like(back_ref)
    loads[1].wait()
    loads[2].wait()

    def out_copy(index, target):
        return pltpu.make_async_copy(
            staging.at[index],
            target.at[pl.ds(pl.multiple_of(lax.rem(index, 4) * 16, 16), 16)],
            out_sems.at[index],
        )

    @pl.loop(0, FF // CHUNK // 4)
    def _(turn_index):
        held = {}

        def multiply(unit):
            index = 4 * turn_index + unit
            up = up_ref[:, block(index, CHUNK)]
            down = down_ref[block(index, CHUNK), :]
            held[unit] = (up, down, nn(feed[...], up), nt(cot[...], down))

        def lift(unit):
            up, down, before, grad_active = held[unit]
            square = before * before
            curve = jnp.tanh(CURVE_SCALE * before * (1.0 + CURVE_CUBIC * square))
            rise = 0.5 * (1.0 + curve)
            slope = rise + 0.5 * before * (1.0 - curve * curve) * (
                CURVE_SCALE * (1.0 + 3.0 * CURVE_CUBIC * square)
            )
            active = (before * rise).astype(BF16)
            held[unit] = (up, down, active, (grad_active * slope).astype(BF16))

        def gather(unit):
            index = 4 * turn_index + unit
            up, down, active, grad_before = held[unit]
            result[...] += nn(active, down)
            back_ref[...] += nt(grad_before, up)
            grad_up = nn(feed_t[...], grad_before).astype(BF16).reshape(16, 32, CHUNK)
            grad_down = tn(active, cot[...]).astype(BF16).reshape(16, 16, D)
            for group in range(2):
                staging[index, :, pl.ds(32 * group, 32), :] = grad_up[
                    :, :, 128 * group : 128 * group + 128
                ]
            for group in range(4):
                staging[index, :, pl.ds(64 + 16 * group, 16), :] = grad_down[
                    :, :, 128 * group : 128 * group + 128
                ]

        staged(4, multiply, lift, gather)
        mine = turn_index == core

        @pl.when(mine)
        def _():
            for unit in range(4):
                out_copy(4 * turn_index + unit, keep_hbm).start()

        @pl.when(jnp.logical_not(mine))
        def _():
            for unit in range(4):
                out_copy(4 * turn_index + unit, send_hbm).start()

    out_ref[...] = result[...].astype(BF16)
    out_high_ref[...] = result[TILE:TOK].astype(BF16)
    for index in range(FF // CHUNK):
        out_copy(index, keep_hbm).wait()


def put_pieces(grad, owner, core, keep_ref, send_ref):
    def put(ref, half):
        part = grad[half * HALF : (half + 1) * HALF].reshape(4, PIECE, D)
        for group in range(4):
            ref[pl.ds(owner * 16 + 4 * group, 4), :, :] = part[
                :, :, 128 * group : 128 * group + 128
            ]

    @pl.when(core == 0)
    def _():
        put(keep_ref, 0)
        put(send_ref, 1)

    @pl.when(core == 1)
    def _():
        put(keep_ref, 1)
        put(send_ref, 0)


def norm_part(
    cot_ref,
    cot_high_ref,
    middle_ref,
    back_ref,
    dense_ref,
    gain_ref,
    gm_ref,
    turned_ref,
    gain_grad_ref,
    keep_ref,
    send_ref,
    gm16,
):
    core = lax.axis_index("core")
    total = middle_ref[...]
    scale = scale_of(total)
    unit = total * scale
    grad = back_ref[...]
    inner = grad * gain_ref[...]
    gain_grad_ref[...] = jnp.sum(grad * unit, axis=0, keepdims=True)
    cot = jnp.concatenate([cot_ref[0:TILE], cot_high_ref[...]], axis=0).astype(F32)
    grad_middle = cot + scale * (inner - unit * jnp.mean(inner * unit, axis=-1, keepdims=True))
    gm_ref[...] = grad_middle
    gm16[...] = grad_middle.astype(BF16)
    turned_ref[...] = grad_middle.T.astype(BF16)
    for owner in range(GROUPS):
        grad_out = nn(dense_ref[pl.ds(owner * OWN, OWN), :], gm16[...]).astype(BF16)
        put_pieces(grad_out, owner, core, keep_ref, send_ref)


def route_part(
    turned_ref,
    mixed_ref,
    slot_ref,
    gates_ref,
    hid_ref,
    wo_ref,
    gain_grad_ref,
    after_ref,
    gt_ref,
    delta_ref,
    gl_ref,
    small_ref,
    gdense,
    sums,
):
    gdense[...] = nn(wo_ref[...], turned_ref[...])
    sums[...] = jnp.zeros_like(sums)
    for tile in range(2):
        for slot in range(TOPK):
            at = lanes_of(tile, slot)
            value = jnp.zeros((HEAD, TILE), F32)
            gate = jnp.zeros((1, TILE), F32)
            for expert in range(slot, slot + EXPERTS - TOPK + 1):
                here = slot_ref[pl.ds(expert, 1), tokens_of(tile)] == slot
                value = jnp.where(
                    here, gdense[pl.ds(expert * HEAD, HEAD), tokens_of(tile)], value
                )
                gate = jnp.where(here, gates_ref[pl.ds(expert, 1), tokens_of(tile)], gate)
            mixed = mixed_ref[:, at].astype(F32)
            dots = jnp.sum(mixed * value, axis=0, keepdims=True)
            rounded = (value * gate).astype(BF16)
            gt_ref[:, at] = rounded
            delta_ref[:, at] = jnp.sum(mixed * rounded.astype(F32), axis=0, keepdims=True)
            for expert in range(slot, slot + EXPERTS - TOPK + 1):
                here = slot_ref[pl.ds(expert, 1), tokens_of(tile)] == slot
                sums[pl.ds(expert, 1), tokens_of(tile)] += jnp.where(here, dots, 0.0)
    gates = gates_ref[...]
    dots = sums[...]
    grad_logits = gates * (dots - jnp.sum(gates * dots, axis=0, keepdims=True))
    gl_ref[...] = grad_logits
    high, low = split_two(grad_logits)
    small_ref[...] = jnp.concatenate(
        [
            nn(high, hid_ref[...]) + nn(low, hid_ref[...]),
            gain_grad_ref[...],
            jnp.zeros((7, D), F32),
        ],
        axis=0,
    )


def attend_back(
    qc_ref,
    gt_ref,
    lse_ref,
    delta_ref,
    kv_ref,
    after_ref,
    pair0,
    pair1,
    pair2,
    pair3,
    dqc,
    keys,
    values,
    kt,
    dkeys,
    dvalues,
    dq,
    scores,
    grads,
    shares,
    slopes,
):
    x = lax.axis_index("x")
    keys[...] = kv_ref[:, 0:HEAD]
    values[...] = kv_ref[:, HEAD : 2 * HEAD]
    for tile in range(TILES):
        kt[tile] = kv_ref[pl.ds(tile * TILE, TILE), 0:HEAD].astype(F32).T.astype(BF16)
    dkeys[...] = jnp.zeros_like(dkeys)
    dvalues[...] = jnp.zeros_like(dvalues)
    later = causal()
    for tile in range(2):
        last = own_blocks(x)[tile]
        dq[...] = jnp.zeros_like(dq)

        def step(index, masked):
            at = block(index, TILE)
            sums = {}

            def multiply(slot):
                here = pl.ds(slot * TILE, TILE)
                route = lanes_of(tile, slot)
                scores[:, here] = nn(keys[at, :], qc_ref[:, route])
                grads[:, here] = nn(values[at, :], gt_ref[:, route])

            def lift(slot):
                here = pl.ds(slot * TILE, TILE)
                route = lanes_of(tile, slot)
                value = jnp.exp2(scores[:, here] * SCORE2 - lse_ref[:, route])
                if masked:
                    value = jnp.where(later, value, 0.0)
                shares[:, here] = value.astype(BF16)
                slopes[:, here] = (value * (grads[:, here] - delta_ref[:, route])).astype(BF16)

            def gather(slot):
                here = pl.ds(slot * TILE, TILE)
                route = lanes_of(tile, slot)
                dq[:, here] += nn(kt[index], slopes[:, here])
                one = nt(qc_ref[:, route], slopes[:, here])
                two = nt(gt_ref[:, route], shares[:, here])
                if slot:
                    one, two = sums[0] + one, sums[1] + two
                sums[0], sums[1] = one, two

            staged(TOPK, multiply, lift, gather)
            dkeys[index] += sums[0]
            dvalues[index] += sums[1]

        step(last, True)

        @pl.loop(0, last)
        def _(index):
            step(index, False)

        dqc[:, pl.ds(tile * LANES, LANES)] = (dq[...] * SCORE).astype(BF16)

    def pair(low, high):
        return jnp.concatenate(
            [
                jnp.concatenate([dkeys[low], dkeys[high]], axis=1) * SCORE,
                jnp.concatenate([dvalues[low], dvalues[high]], axis=1),
            ],
            axis=0,
        ).astype(BF16)

    for away, ref in enumerate((pair0, pair1, pair2, pair3)):
        ref[...] = pair(*own_blocks(lax.rem(x + away, GROUPS)))


def query_part(
    dqc,
    slot_ref,
    hid_ref,
    small_ref,
    wr_ref,
    mine_ref,
    other_ref,
    dqall,
    gain_ref,
    keep_ref,
    send_ref,
):
    core = lax.axis_index("core")
    for tile in range(2):
        for expert in range(EXPERTS):
            dqall[pl.ds(expert * HEAD, HEAD), tokens_of(tile)] = expand(
                slot_ref, dqc, tile, expert
            ).astype(BF16)
    gain = jnp.sum(
        small_ref[0:EXPERTS] * wr_ref[...].astype(F32), axis=0, keepdims=True
    )
    for owner in range(GROUPS):
        grad = nn(dqall[pl.ds(owner * OWN, OWN), :], hid_ref[...])
        put_pieces(grad.astype(BF16), owner, core, keep_ref, send_ref)
        one, two = mine_ref[owner].astype(F32), other_ref[owner].astype(F32)
        first, last = jnp.where(core == 0, one, two), jnp.where(core == 0, two, one)
        gain = gain + jnp.sum(grad[0:HALF] * first, axis=0, keepdims=True)
        gain = gain + jnp.sum(grad[HALF:OWN] * last, axis=0, keepdims=True)
    gain_ref[...] = gain


def finish(
    tok_ref,
    high_ref,
    gm_ref,
    dqall,
    gl_ref,
    wr_ref,
    mine_ref,
    other_ref,
    pairs_ref,
    wkv_ref,
    gain_ref,
    out_ref,
    out_high_ref,
):
    core = lax.axis_index("core")
    high, low = split_two(gl_ref[...])
    grad = tn(high, wr_ref[...]) + tn(low, wr_ref[...])
    for owner in range(GROUPS):
        grad = grad + tn(dqall[block(2 * owner + core, HALF), :], mine_ref[owner])
        grad = grad + tn(dqall[block(2 * owner + 1 - core, HALF), :], other_ref[owner])
    grad = grad + lax.dot_general(
        pairs_ref[...], wkv_ref[...], (((0,), (1,)), ((), ())), preferred_element_type=F32
    )
    rows = jnp.concatenate([tok_ref[0:TILE], high_ref[0:TILE]], axis=0).astype(F32)
    scale = scale_of(rows)
    unit = rows * scale
    inner = grad * gain_ref[...]
    result = (
        gm_ref[...] + scale * (inner - unit * jnp.mean(inner * unit, axis=-1, keepdims=True))
    ).astype(BF16)
    out_ref[...] = result
    out_high_ref[...] = result[TILE:TOK]


def added(near, one, two, three):
    return (
        (near.astype(F32) + two.astype(F32)) + (one.astype(F32) + three.astype(F32))
    ).astype(BF16)


def pair_feed(arrive, keep, arrived, keep_o, arrived_o, out_hbm, one, two, three, four, out, sems):
    arrive()
    parts = [pl.ds(16 * index, 16) for index in range(4)]
    loads = []
    for index, part in enumerate(parts):
        loads.append(
            [
                pltpu.make_async_copy(source.at[part], target.at[part], sems.at[index, place])
                for place, (source, target) in enumerate(
                    ((keep, one), (arrived, two), (keep_o, three), (arrived_o, four))
                )
            ]
        )
        for load in loads[-1]:
            load.start()
    stores = []
    for index, part in enumerate(parts):
        for load in loads[index]:
            load.wait()
        out[part, 0:128, :] = (one[part].astype(F32) + two[part].astype(F32)).astype(BF16)
        out[part, 128:176, :] = (three[part].astype(F32) + four[part].astype(F32)).astype(BF16)
        stores.append(pltpu.make_async_copy(out.at[part], out_hbm.at[part], sems.at[index, 4]))
        stores[-1].start()
    for store in stores:
        store.wait()


def merge(
    arrive,
    pieces_hbm,
    keep_hbm,
    arrived_hbm,
    near,
    one,
    two,
    three,
    hid_ref,
    small_ref,
    gain_rows,
    wkv_ref,
    gain_ref,
    out_hbm,
    part_ref,
    pair_ref,
    pieces,
    keep_q,
    arrived_q,
    feed,
    rest,
    sems,
):
    parts = [pl.ds(16 * index, 16) for index in range(4)]
    first = [
        pltpu.make_async_copy(keep_hbm, keep_q, sems.at[0]),
        pltpu.make_async_copy(arrived_hbm, arrived_q, sems.at[1]),
    ]
    loads = [
        pltpu.make_async_copy(pieces_hbm.at[part], pieces.at[part], sems.at[2 + index])
        for index, part in enumerate(parts)
    ]
    for load in first + loads:
        load.start()
    arrive()
    pair = added(near[...], one[...], two[...], three[...])
    pair_ref[...] = pair
    grad_kv = nn(pair, hid_ref[...])
    gain_grad = (
        gain_rows[...]
        + jnp.sum(grad_kv * wkv_ref[...].astype(F32).T, axis=0, keepdims=True)
    ) / gain_ref[...]
    last = jnp.concatenate([small_ref[0:25], gain_grad, small_ref[26:32]], axis=0)
    shared = jnp.concatenate([grad_kv, last], axis=0).astype(BF16)
    for piece in range(16):
        for place in range(3):
            row, group = divmod(3 * piece + place, 4)
            if 16 * row < SMALL:
                value = shared[16 * row : 16 * row + 16, 128 * group : 128 * group + 128]
            else:
                value = jnp.zeros((16, 128), BF16)
            for far in range(GROUPS):
                rest[16 * far + piece, 48 + 16 * place : 64 + 16 * place] = value
    for load in first:
        load.wait()
    rest[:, 0:48, :] = (keep_q[...].astype(F32) + arrived_q[...].astype(F32)).astype(BF16)
    stores = [pltpu.make_async_copy(rest, out_hbm.at[:, pl.ds(128, 96), :], sems.at[6])]
    stores[0].start()
    total = jnp.zeros((176, 128), F32)
    for index in range(4):
        loads[index].wait()
        for piece in range(16 * index, 16 * index + 16):
            total = total + pieces[piece].astype(F32)
    total = total.astype(BF16)
    part_ref[...] = total[128:176]
    for index in range(64):
        feed[index] = total[0:128]
    stores.append(pltpu.make_async_copy(feed, out_hbm.at[:, pl.ds(0, 128), :], sems.at[7]))
    stores[1].start()
    for store in stores:
        store.wait()


def collect(spread, part_ref, out_ref, rest, sems):
    load = pltpu.make_async_copy(spread.at[:, pl.ds(128, 96), :], rest, sems.at[0])
    load.start()
    load.wait()
    total = rest[0].astype(F32)
    for index in range(1, 64):
        total = total + rest[index].astype(F32)
    total = total.astype(BF16)
    for index in range(16):
        out_ref[index, 0:PIECE] = part_ref[...]
        out_ref[index, PIECE:EXTRA] = total


def unpack(at_ref, half_ref, *refs):
    up_ref, down_ref = refs[-2:]
    for group in range(2):
        up_ref[:, 128 * group : 128 * group + 128] = (
            half_ref[:, pl.ds(32 * group, 32), :].astype(F32).reshape(D, 128)
        )
    for group in range(4):
        down_ref[:, 128 * group : 128 * group + 128] = (
            half_ref[:, pl.ds(64 + 16 * group, 16), :].astype(F32).reshape(CHUNK, 128)
        )


def assemble(mine_ref, other_ref, output_ref, query_ref, kv_ref, router_ref, heads_ref, feed_ref, shared):
    core = lax.axis_index("core")
    for ref, half in ((mine_ref, core), (other_ref, 1 - core)):
        for column in range(4):
            for row in range(4):
                rows = pl.ds(pl.multiple_of(half * HALF + row * PIECE, 16), PIECE)
                for index, target in enumerate((output_ref, query_ref)):
                    target[rows, pl.ds(128 * column, 128)] = ref[
                        4 * column + row, pl.ds(PIECE * index, PIECE), :
                    ].astype(F32)
    for piece in range(14):
        for place in range(3):
            row, group = divmod(3 * piece + place, 4)
            if 16 * row < SMALL:
                at = pl.ds(2 * PIECE + 16 * place, 16)
                shared[16 * row : 16 * row + 16, 128 * group : 128 * group + 128] = mine_ref[
                    piece, at, :
                ].astype(F32) + other_ref[piece, at, :].astype(F32)
    kv_ref[...] = shared[0:128].T
    router_ref[...] = shared[128:152]
    feed_ref[...] = shared[152:153]
    heads_ref[...] = shared[153:154]


def shape(dims, dtype=BF16):
    return jax.ShapeDtypeStruct(dims, dtype)


VMEM = pl.BlockSpec(memory_space=pltpu.VMEM)
SMEM = pl.BlockSpec(memory_space=pltpu.SMEM)
HBM = pl.BlockSpec(memory_space=pltpu.HBM)
ANY = pl.BlockSpec(memory_space=pl.ANY)


def nothing(*refs):
    pass


def after(value, *others):
    return pl.pallas_call(
        nothing,
        out_shape=shape(value.shape, value.dtype),
        in_specs=[ANY] * (1 + len(others)),
        out_specs=ANY,
        input_output_aliases={0: 0},
        name="after",
    )(value, *others)


def size_of(value):
    return math.prod(value.shape) * jnp.dtype(value.dtype).itemsize


def call(kernel, micros, inputs, outputs, scratch=(), far=(), far_out=(), sent=(), own_loads=False):
    near = [index for index in range(len(inputs)) if index not in far]
    count, ends = len(inputs), len(inputs) + len(outputs)

    def body(*refs):
        sources, results, own = list(refs[:count]), refs[count:ends], refs[ends:]
        buffers, sems = own[len(scratch) : -1], own[-1]
        loads = []
        for index, (source, buffer) in enumerate(zip(near, buffers)):
            loads.append(pltpu.make_async_copy(sources[source], buffer, sems.at[index]))
            sources[source] = buffer
        def arrive():
            for load in loads:
                load.wait()

        for load in loads:
            load.start()
        if own_loads:
            kernel(arrive, *sources, *results, *own[: len(scratch)])
        else:
            arrive()
            kernel(*sources, *results, *own[: len(scratch)])

    buffers = [pltpu.VMEM(inputs[index].shape, inputs[index].dtype) for index in near]
    limit = LIMIT - sum(size_of(inputs[index]) for index in sent)
    return pl.pallas_call(
        body,
        out_shape=outputs,
        in_specs=[ANY if index in sent else HBM for index in range(count)],
        out_specs=tuple(HBM if index in far_out else VMEM for index in range(len(outputs))),
        scratch_shapes=[
            *scratch,
            *buffers,
            pltpu.SemaphoreType.DMA((len(near),)),
        ],
        compiler_params=pltpu.CompilerParams(vmem_limit_bytes=limit),
        cost_estimate=pl.CostEstimate(
            flops=int(micros * 1e9), bytes_accessed=(1 << 20) if micros else 0, transcendentals=0
        ),
        name=kernel.__name__,
    )(*inputs)


def turn(size, step):
    return [(index, (index + step) % size) for index in range(size)]


def swap(value):
    return lax.ppermute(value, "core", turn(2, 1))


def mirror(value):
    return lax.ppermute(value, "x", [(0, 3), (3, 0), (1, 2), (2, 1)])


def around(value, axis):
    return [lax.ppermute(value, axis, turn(4, step)) for step in (1, 2, 3)]


def vmem(dims, dtype=F32):
    return pltpu.VMEM(dims, dtype)


def shards(
    tokens,
    expert_ids,
    cotangent,
    gain_heads,
    key_value_weight,
    router_weight,
    query_weight,
    output_weight,
    gain_feed,
    up_weight,
    down_weight,
):
    x = lax.axis_index("x")
    core = lax.axis_index("core")
    chips = ("x", "y", "z")
    tok = tokens[0]
    cot = cotangent[0]
    ids = expert_ids[0].T
    wq = jnp.swapaxes(query_weight, 1, 2).reshape(OWN, D)
    wr = router_weight.T
    wkv = key_value_weight
    gain1 = gain_heads.reshape(1, D)
    gain2 = gain_feed.reshape(1, D)

    carried = jnp.concatenate(
        [
            tok[TILE:TOK],
            jnp.pad(ids[:, TILE:TOK].astype(BF16), ((0, 8), (0, D - TILE))),
        ],
        axis=0,
    )
    carried = mirror(carried)
    mine = lax.dynamic_slice(wq, (core * HALF, 0), (HALF, D))
    mine = lax.all_to_all(
        jnp.broadcast_to(mine[None], (GROUPS, HALF, D)), "x", split_axis=0, concat_axis=0, tiled=True
    )
    wo = lax.all_gather(output_weight.reshape(OWN, D), "x", axis=0, tiled=True)
    first, kv = call(
        pairs_first,
        2,
        (tok, gain1, wkv),
        (shape((TILE, D)), shape((TOK, 2 * HEAD))),
    )
    kvs = [kv] + around(kv, "x")
    cot_high, hidden, turned, gates, slots = call(
        prepare,
        3,
        (first, carried, ids, gain1, wr, cot, *kvs[1:]),
        (
            shape((TILE, D)),
            shape((TOK, D)),
            shape((D, TOK)),
            shape((EXPERTS, TOK), F32),
            shape((EXPERTS, TOK), jnp.int32),
        ),
        far=(6, 7, 8),
        sent=(1, 6, 7, 8),
    )
    mine = after(mine, slots)
    wqs = (mine, swap(mine))
    cot_high = mirror(cot_high)

    qc, mixed, lse, kv_all, dense = call(
        attend,
        14,
        (turned, slots, gates, *wqs, *kvs),
        (
            shape((HEAD, ROUTES)),
            shape((HEAD, ROUTES)),
            shape((1, ROUTES), F32),
            shape((LENGTH, 2 * HEAD)),
            shape((EXPERTS * HEAD, TOK)),
        ),
        [
            vmem((EXPERTS * HEAD, TOK)),
            vmem((LENGTH, HEAD), BF16),
            vmem((GROUPS, HEAD + 16, 2 * TILE), BF16),
            vmem((1, LANES)),
            vmem((HEAD + 16, LANES)),
            vmem((2 * TILE, LANES)),
            vmem((2 * TILE, LANES), BF16),
        ],
        sent=(3, 4, 6, 7, 8),
    )

    result, out_high, middle, back, keep, send = call(
        feed_part,
        17,
        (tok, carried, cot, cot_high, dense, gain2, wo, up_weight, down_weight),
        (
            shape((TOK, D)),
            shape((TILE, D)),
            shape((TOK, D), F32),
            shape((TOK, D), F32),
            shape((64, 128, 128)),
            shape((64, 128, 128)),
        ),
        [
            vmem((TOK, D), BF16),
            vmem((D, TOK), BF16),
            vmem((TOK, D), BF16),
            vmem((TOK, D)),
            vmem((EXPERTS * HEAD, D), BF16),
            vmem((D, FF), BF16),
            vmem((FF, D), BF16),
            vmem((8, 16, 128, 128), BF16),
            pltpu.SemaphoreType.DMA((3,)),
            pltpu.SemaphoreType.DMA((8,)),
        ],
        far=(6, 7, 8),
        far_out=(4, 5),
        sent=(3, 6),
        own_loads=True,
    )
    arrived = swap(send)
    out_back = mirror(out_high)

    grad_middle, turned_gm, gain_grad, keep_o, send_o = call(
        norm_part,
        4,
        (cot, cot_high, middle, back, dense, gain2),
        (
            shape((TOK, D), F32),
            shape((D, TOK)),
            shape((1, D), F32),
            shape((64, PIECE, 128)),
            shape((64, PIECE, 128)),
        ),
        [vmem((TOK, D), BF16)],
        sent=(1,),
    )
    arrived_o = swap(send_o)
    (paired,) = call(
        pair_feed,
        4,
        (keep, arrived, keep_o, arrived_o),
        (shape((64, 176, 128)),),
        [
            vmem((64, 128, 128), BF16),
            vmem((64, 128, 128), BF16),
            vmem((64, PIECE, 128), BF16),
            vmem((64, PIECE, 128), BF16),
            vmem((64, 176, 128), BF16),
            pltpu.SemaphoreType.DMA((4, 5)),
        ],
        far=(0, 1, 2, 3),
        far_out=(0,),
        sent=(1, 3),
        own_loads=True,
    )
    gt, delta, grad_logits, small = call(
        route_part,
        6,
        (turned_gm, mixed, slots, gates, hidden, wo, gain_grad, paired),
        (
            shape((HEAD, ROUTES)),
            shape((1, ROUTES), F32),
            shape((EXPERTS, TOK), F32),
            shape((32, D), F32),
        ),
        [vmem((EXPERTS * HEAD, TOK)), vmem((EXPERTS, TOK))],
        far=(7,),
        sent=(5,),
    )
    pieces = lax.all_to_all(paired, chips, split_axis=0, concat_axis=0, tiled=True)

    pair, *others, dqc = call(
        attend_back,
        20,
        (qc, gt, lse, delta, kv_all, out_back),
        (
            *[shape((2 * HEAD, TOK))] * GROUPS,
            shape((HEAD, ROUTES)),
        ),
        [
            vmem((LENGTH, HEAD), BF16),
            vmem((LENGTH, HEAD), BF16),
            vmem((TILES, HEAD, TILE), BF16),
            vmem((TILES, HEAD, TILE)),
            vmem((TILES, HEAD, TILE)),
            vmem((HEAD, LANES)),
            vmem((TILE, LANES)),
            vmem((TILE, LANES)),
            vmem((TILE, LANES), BF16),
            vmem((TILE, LANES), BF16),
        ],
        far=(5,),
        sent=(5,),
    )
    arrived_pairs = [
        lax.ppermute(value, "x", turn(4, step + 1)) for step, value in enumerate(others)
    ]
    dqall, gain_rows, keep_q, send_q = call(
        query_part,
        6,
        (dqc, slots, hidden, small, wr, *wqs),
        (
            shape((EXPERTS * HEAD, TOK)),
            shape((1, D), F32),
            shape((64, PIECE, 128)),
            shape((64, PIECE, 128)),
        ),
        sent=(5, 6),
    )
    arrived_q = swap(send_q)
    merged, part, pair_sum = call(
        merge,
        5,
        (
            pieces,
            keep_q,
            arrived_q,
            pair,
            *arrived_pairs,
            hidden,
            small,
            gain_rows,
            wkv,
            gain1,
        ),
        (shape((64, 224, 128)), shape((PIECE, 128)), shape((2 * HEAD, TOK))),
        [
            vmem((64, 176, 128), BF16),
            vmem((64, PIECE, 128), BF16),
            vmem((64, PIECE, 128), BF16),
            vmem((64, 128, 128), BF16),
            vmem((64, 96, 128), BF16),
            pltpu.SemaphoreType.DMA((8,)),
        ],
        far=(0, 1, 2),
        far_out=(0,),
        own_loads=True,
        sent=(0, 2, 4, 5, 6),
    )
    grad_whole, grad_high = call(
        finish,
        3,
        (tok, carried, grad_middle, dqall, grad_logits, wr, *wqs, pair_sum, wkv, gain1),
        (shape((TOK, D)), shape((TILE, D))),
    )
    spread = lax.all_to_all(merged, chips, split_axis=0, concat_axis=0, tiled=True)
    result = lax.dynamic_update_slice(result, out_back, (TILE, 0))
    spread = after(spread, grad_high, result)
    grad_back = mirror(grad_high)
    grad_tokens = lax.dynamic_update_slice(grad_whole, grad_back, (TILE, 0))
    (part,) = call(
        collect,
        0,
        (spread, part),
        (shape((16, EXTRA, 128)),),
        [vmem((64, 96, 128), BF16), pltpu.SemaphoreType.DMA((1,))],
        far=(0,),
        sent=(0,),
    )
    feed_other = swap(spread)
    part = after(part, grad_back)
    part = lax.all_to_all(part, ("y", "z"), split_axis=0, concat_axis=0, tiled=True)

    def unpacked(value, half, *earlier, extra=()):
        half_spec = pl.BlockSpec((16, 128, 128), lambda index, at: (index, 0, 0))
        return pl.pallas_call(
            unpack,
            grid_spec=pltpu.PrefetchScalarGridSpec(
                num_scalar_prefetch=1,
                grid=(4,),
                in_specs=[half_spec] + [HBM] * len(earlier) + [ANY] * len(extra),
                out_specs=(
                    pl.BlockSpec((D, CHUNK), lambda index, at: (0, 4 * at[0] + index)),
                    pl.BlockSpec((CHUNK, D), lambda index, at: (4 * at[0] + index, 0)),
                ),
            ),
            out_shape=(shape((D, FF), F32), shape((FF, D), F32)),
            input_output_aliases={2: 0, 3: 1} if earlier else {},
            compiler_params=pltpu.CompilerParams(vmem_limit_bytes=LIMIT - 2 * MIB),
            name="unpack",
        )(half.reshape(1), value, *earlier, *extra)

    grads = unpacked(spread, core)
    grad_up, grad_down = unpacked(feed_other, 1 - core, *grads)
    part = after(part, grad_up)
    part_other = swap(part)
    output_grad, query_grad, kv_grad, router_grad, gain_heads_grad, gain_feed_grad = call(
        assemble,
        4,
        (part, part_other),
        (
            shape((OWN, D), F32),
            shape((OWN, D), F32),
            shape((D, 2 * HEAD), F32),
            shape((EXPERTS, D), F32),
            shape((1, D), F32),
            shape((1, D), F32),
        ),
        [vmem((SMALL, D))],
        sent=(0, 1),
    )
    return (
        result[None],
        grad_tokens[None],
        gain_heads_grad.reshape(D),
        kv_grad,
        router_grad.T,
        query_grad.reshape(OWN // HEAD, HEAD, D).swapaxes(1, 2),
        output_grad.reshape(OWN // HEAD, HEAD, D),
        gain_feed_grad.reshape(D),
        grad_up,
        grad_down,
    )


def solution(mesh):
    grid = Mesh(mesh.devices.reshape(4, 4, 4, 2), ("x", "y", "z", "core"))
    dp = ("y", "z", "core")
    return jax.shard_map(
        shards,
        mesh=grid,
        in_specs=(
            P(dp, "x", None),
            P(dp, "x", None),
            P(dp, "x", None),
            P(),
            P(),
            P(),
            P("x", None, None),
            P("x", None, None),
            P(),
            P(),
            P(),
        ),
        out_specs=(
            P(dp, "x", None),
            P(dp, "x", None),
            P(),
            P(),
            P(),
            P("x", None, None),
            P("x", None, None),
            P(),
            P(),
            P(),
        ),
        check_vma=False,
    )
```

```python
import math

import jax
import jax.numpy as jnp
from jax import lax
from jax.experimental import pallas as pl
from jax.experimental.pallas import tpu as pltpu
from jax.sharding import Mesh, PartitionSpec as P

D = 512
HEAD = 64
EXPERTS = 24
TOPK = 8
FF = 2048
TOK = 512
GROUPS = 4
LENGTH = TOK * GROUPS
OWN = EXPERTS // GROUPS * HEAD
HALF = OWN // 2
TILE = 256
LANES = TOPK * TILE
TILES = LENGTH // TILE
ROUTES = TOK * TOPK
CHUNK = 256
SMALL = 160
PIECE = 48
EXTRA = 3 * PIECE

EPSILON = 1e-06
CURVE_SCALE = 0.7978845608028654
CURVE_CUBIC = 0.044715
SCORE = HEAD**-0.5
SCORE2 = SCORE * 1.4426950408889634
LOW = -1e30

F32 = jnp.float32
BF16 = jnp.bfloat16
MIB = 1 << 20
LIMIT = 62 * MIB - (1 << 18)


def nn(a, b):
    return lax.dot_general(a, b, (((1,), (0,)), ((), ())), preferred_element_type=F32)


def nt(a, b):
    return lax.dot_general(a, b, (((1,), (1,)), ((), ())), preferred_element_type=F32)


def tn(a, b):
    return lax.dot_general(a, b, (((0,), (0,)), ((), ())), preferred_element_type=F32)


def split_two(value):
    high = value.astype(BF16)
    return high, (value - high.astype(F32)).astype(BF16)


def scale_of(rows):
    return lax.rsqrt(jnp.mean(rows * rows, axis=-1, keepdims=True) + EPSILON)


def lanes_of(tile, slot):
    return pl.ds(tile * LANES + slot * TILE, TILE)


def tokens_of(tile):
    return pl.ds(tile * TILE, TILE)


def block(index, size):
    return pl.ds(pl.multiple_of(index * size, size), size)


def slots_of(expert):
    return range(max(0, expert - (EXPERTS - TOPK)), min(TOPK - 1, expert) + 1)


def pairs_first(tok_ref, gain_ref, wkv_ref, first_ref, kv_ref):
    rows = tok_ref[...].astype(F32)
    first = (rows * scale_of(rows) * gain_ref[...]).astype(BF16)
    first_ref[...] = first[0:TILE]
    kv_ref[...] = nn(first, wkv_ref[...]).astype(BF16)


def prepare(
    first_ref,
    carried_ref,
    ids_ref,
    gain_ref,
    wr_ref,
    cot_ref,
    after1,
    after2,
    after3,
    cot_high_ref,
    hid_ref,
    turned_ref,
    gates_ref,
    slot_ref,
):
    cot_high_ref[...] = cot_ref[TILE:TOK]
    rows = carried_ref[0:TILE].astype(F32)
    high = rows * scale_of(rows) * gain_ref[...]
    turned_ref[:, 0:TILE] = first_ref[...].astype(F32).T.astype(BF16)
    turned_ref[:, TILE:TOK] = high.T.astype(BF16)
    hidden = jnp.concatenate([first_ref[...], high.astype(BF16)], axis=0)
    hid_ref[...] = hidden
    logits = nt(wr_ref[...], hidden)
    ids = jnp.concatenate(
        [ids_ref[:, 0:TILE], carried_ref[TILE : TILE + 8, 0:TILE].astype(jnp.int32)], axis=1
    )
    names = lax.broadcasted_iota(jnp.int32, (EXPERTS, TOK), 0)
    chosen = names == ids[0:1]
    for route in range(1, TOPK):
        chosen = chosen | (names == ids[route : route + 1])
    count = jnp.where(chosen, 1.0, 0.0)
    below = lax.broadcasted_iota(jnp.int32, (EXPERTS, EXPERTS), 0) > lax.broadcasted_iota(
        jnp.int32, (EXPERTS, EXPERTS), 1
    )
    rank = nn(jnp.where(below, 1.0, 0.0).astype(BF16), count.astype(BF16))
    slot_ref[...] = jnp.where(chosen, rank, -1.0).astype(jnp.int32)
    peak = jnp.max(jnp.where(chosen, logits, -3e38), axis=0, keepdims=True)
    raised = jnp.where(chosen, jnp.exp(logits - peak), 0.0)
    gates_ref[...] = raised / jnp.sum(raised, axis=0, keepdims=True)


def compact(slot_ref, dense_ref, tile, slot):
    value = jnp.zeros((HEAD, TILE), F32)
    for expert in range(slot, slot + EXPERTS - TOPK + 1):
        here = slot_ref[pl.ds(expert, 1), tokens_of(tile)] == slot
        value = jnp.where(here, dense_ref[pl.ds(expert * HEAD, HEAD), tokens_of(tile)], value)
    return value


def expand(slot_ref, packed_ref, tile, expert):
    row = slot_ref[pl.ds(expert, 1), tokens_of(tile)]
    value = jnp.zeros((HEAD, TILE), F32)
    for slot in slots_of(expert):
        value = jnp.where(row == slot, packed_ref[:, lanes_of(tile, slot)].astype(F32), value)
    return value


def causal():
    return lax.broadcasted_iota(jnp.int32, (TILE, TILE), 0) <= lax.broadcasted_iota(
        jnp.int32, (TILE, TILE), 1
    )


def staged(count, *stages):
    for time in range(count + len(stages) - 1):
        for late, stage in enumerate(stages):
            if 0 <= time - late < count:
                stage(time - late)


def own_blocks(x):
    return 2 * x, 7 - 2 * x


def attend(
    turned_ref,
    slot_ref,
    gates_ref,
    mine_ref,
    other_ref,
    kv0,
    kv1,
    kv2,
    kv3,
    qc_ref,
    mixed_ref,
    lse_ref,
    kv_ref,
    dense_ref,
    qall,
    keys,
    vt,
    peak,
    acc,
    scores,
    shares,
):
    x = lax.axis_index("x")
    core = lax.axis_index("core")
    owners = [lax.rem(x + GROUPS - away, GROUPS) for away in range(GROUPS)]
    for owner, kv in zip(owners, (kv0, kv1, kv2, kv3)):
        turned = kv[:, HEAD : 2 * HEAD].astype(F32).T.astype(BF16)
        kv_ref[block(owner, TOK), :] = kv[...]
        keys[block(owner, TOK), :] = kv[:, 0:HEAD]
        vt[owner, 0:HEAD, :] = turned
        vt[owner, HEAD : HEAD + 16, :] = jnp.ones((16, 2 * TILE), BF16)
    for owner in range(GROUPS):
        qall[block(2 * owner + core, HALF), :] = nn(mine_ref[owner], turned_ref[...])
        qall[block(2 * owner + 1 - core, HALF), :] = nn(other_ref[owner], turned_ref[...])
    for tile in range(2):
        for slot in range(TOPK):
            qc_ref[:, lanes_of(tile, slot)] = compact(slot_ref, qall, tile, slot).astype(BF16)

    wide = 2 * TILE
    later = lax.broadcasted_iota(jnp.int32, (TILE, wide), 0) <= (
        lax.broadcasted_iota(jnp.int32, (TILE, wide), 1) & (TILE - 1)
    )
    later_two = lax.broadcasted_iota(jnp.int32, (wide, wide), 0) <= TILE + (
        lax.broadcasted_iota(jnp.int32, (wide, wide), 1) & (TILE - 1)
    )

    def step(tile, start, size, values, mask):
        fades = {}

        def multiply(unit):
            at = pl.ds(unit * wide, wide)
            route = pl.ds(tile * LANES + unit * wide, wide)
            scores[0:size, at] = nn(keys[pl.ds(start, size), :], qc_ref[:, route])

        def lift(unit):
            at = pl.ds(unit * wide, wide)
            value = scores[0:size, at]
            if mask is not None:
                value = jnp.where(mask, value, LOW)
            top = jnp.max(value, axis=0, keepdims=True)
            if mask is None:
                before = peak[:, at]
                top = jnp.maximum(before, top)
                fades[unit] = jnp.exp2((before - top) * SCORE2)
            shares[0:size, at] = jnp.exp2((value - top) * SCORE2).astype(BF16)
            peak[:, at] = top

        def gather(unit):
            at = pl.ds(unit * wide, wide)
            part = nn(values, shares[0:size, at])
            if mask is None:
                part = acc[:, at] * fades[unit] + part
            acc[:, at] = part

        staged(LANES // wide, multiply, lift, gather)

    for tile in range(2):
        if tile == 0:
            start = pl.multiple_of(2 * x * TILE, TILE)
            step(tile, start, TILE, vt[x, :, 0:TILE], later)
            count = x
        else:
            start = pl.multiple_of((3 - x) * wide, wide)
            step(tile, start, wide, vt[3 - x], later_two)
            count = 3 - x

        @pl.loop(0, count)
        def _(index):
            step(tile, pl.multiple_of(index * wide, wide), wide, vt[index], None)

        here = pl.ds(tile * LANES, LANES)
        total = acc[HEAD : HEAD + 1, :]
        mixed_ref[:, here] = (acc[0:HEAD, :] / total).astype(BF16)
        lse_ref[:, here] = peak[...] * SCORE2 + jnp.log2(total)
    for tile in range(2):
        for expert in range(EXPERTS):
            value = expand(slot_ref, mixed_ref, tile, expert)
            gate = gates_ref[pl.ds(expert, 1), tokens_of(tile)]
            dense_ref[pl.ds(expert * HEAD, HEAD), tokens_of(tile)] = (value * gate).astype(BF16)


def feed_part(
    arrive,
    tok_ref,
    high_ref,
    cot_ref,
    cot_high_ref,
    dense_ref,
    gain_ref,
    wo_hbm,
    up_hbm,
    down_hbm,
    out_ref,
    out_high_ref,
    middle_ref,
    back_ref,
    keep_hbm,
    send_hbm,
    feed,
    feed_t,
    cot,
    result,
    wo_ref,
    up_ref,
    down_ref,
    staging,
    sems,
    out_sems,
):
    core = lax.axis_index("core")
    sources = ((wo_hbm, wo_ref), (up_hbm, up_ref), (down_hbm, down_ref))
    loads = [
        pltpu.make_async_copy(source, target, sems.at[index])
        for index, (source, target) in enumerate(sources)
    ]
    for load in loads:
        load.start()
    arrive()
    cot[0:TILE] = cot_ref[0:TILE]
    cot[TILE:TOK] = cot_high_ref[...]
    total = jnp.concatenate([tok_ref[0:TILE], high_ref[0:TILE]], axis=0).astype(F32)
    loads[0].wait()
    total = total + tn(dense_ref[...], wo_ref[...])
    middle_ref[...] = total
    feed32 = total * scale_of(total) * gain_ref[...]
    feed[...] = feed32.astype(BF16)
    feed_t[...] = feed32.T.astype(BF16)
    result[...] = total
    back_ref[...] = jnp.zeros_like(back_ref)
    loads[1].wait()
    loads[2].wait()

    def out_copy(index, target):
        return pltpu.make_async_copy(
            staging.at[index],
            target.at[pl.ds(pl.multiple_of(lax.rem(index, 4) * 16, 16), 16)],
            out_sems.at[index],
        )

    @pl.loop(0, FF // CHUNK // 4)
    def _(turn_index):
        held = {}

        def multiply(unit):
            index = 4 * turn_index + unit
            up = up_ref[:, block(index, CHUNK)]
            down = down_ref[block(index, CHUNK), :]
            held[unit] = (up, down, nn(feed[...], up), nt(cot[...], down))

        def lift(unit):
            up, down, before, grad_active = held[unit]
            square = before * before
            curve = jnp.tanh(CURVE_SCALE * before * (1.0 + CURVE_CUBIC * square))
            rise = 0.5 * (1.0 + curve)
            slope = rise + 0.5 * before * (1.0 - curve * curve) * (
                CURVE_SCALE * (1.0 + 3.0 * CURVE_CUBIC * square)
            )
            active = (before * rise).astype(BF16)
            held[unit] = (up, down, active, (grad_active * slope).astype(BF16))

        def gather(unit):
            index = 4 * turn_index + unit
            up, down, active, grad_before = held[unit]
            result[...] += nn(active, down)
            back_ref[...] += nt(grad_before, up)
            grad_up = nn(feed_t[...], grad_before).astype(BF16).reshape(16, 32, CHUNK)
            grad_down = tn(active, cot[...]).astype(BF16).reshape(16, 16, D)
            for group in range(2):
                staging[index, :, pl.ds(32 * group, 32), :] = grad_up[
                    :, :, 128 * group : 128 * group + 128
                ]
            for group in range(4):
                staging[index, :, pl.ds(64 + 16 * group, 16), :] = grad_down[
                    :, :, 128 * group : 128 * group + 128
                ]

        staged(4, multiply, lift, gather)
        mine = turn_index == core

        @pl.when(mine)
        def _():
            for unit in range(4):
                out_copy(4 * turn_index + unit, keep_hbm).start()

        @pl.when(jnp.logical_not(mine))
        def _():
            for unit in range(4):
                out_copy(4 * turn_index + unit, send_hbm).start()

    out_ref[...] = result[...].astype(BF16)
    out_high_ref[...] = result[TILE:TOK].astype(BF16)
    for index in range(FF // CHUNK):
        out_copy(index, keep_hbm).wait()


def put_pieces(grad, owner, core, keep_ref, send_ref):
    def put(ref, half):
        part = grad[half * HALF : (half + 1) * HALF].reshape(4, PIECE, D)
        for group in range(4):
            ref[pl.ds(owner * 16 + 4 * group, 4), :, :] = part[
                :, :, 128 * group : 128 * group + 128
            ]

    @pl.when(core == 0)
    def _():
        put(keep_ref, 0)
        put(send_ref, 1)

    @pl.when(core == 1)
    def _():
        put(keep_ref, 1)
        put(send_ref, 0)


def norm_part(
    cot_ref,
    cot_high_ref,
    middle_ref,
    back_ref,
    dense_ref,
    gain_ref,
    gm_ref,
    turned_ref,
    gain_grad_ref,
    keep_ref,
    send_ref,
    gm16,
):
    core = lax.axis_index("core")
    total = middle_ref[...]
    scale = scale_of(total)
    unit = total * scale
    grad = back_ref[...]
    inner = grad * gain_ref[...]
    gain_grad_ref[...] = jnp.sum(grad * unit, axis=0, keepdims=True)
    cot = jnp.concatenate([cot_ref[0:TILE], cot_high_ref[...]], axis=0).astype(F32)
    grad_middle = cot + scale * (inner - unit * jnp.mean(inner * unit, axis=-1, keepdims=True))
    gm_ref[...] = grad_middle
    gm16[...] = grad_middle.astype(BF16)
    turned_ref[...] = grad_middle.T.astype(BF16)
    for owner in range(GROUPS):
        grad_out = nn(dense_ref[pl.ds(owner * OWN, OWN), :], gm16[...]).astype(BF16)
        put_pieces(grad_out, owner, core, keep_ref, send_ref)


def route_part(
    turned_ref,
    mixed_ref,
    slot_ref,
    gates_ref,
    hid_ref,
    wo_ref,
    gain_grad_ref,
    after_ref,
    gt_ref,
    delta_ref,
    gl_ref,
    small_ref,
    gdense,
    sums,
):
    gdense[...] = nn(wo_ref[...], turned_ref[...])
    sums[...] = jnp.zeros_like(sums)
    for tile in range(2):
        for slot in range(TOPK):
            at = lanes_of(tile, slot)
            value = jnp.zeros((HEAD, TILE), F32)
            gate = jnp.zeros((1, TILE), F32)
            for expert in range(slot, slot + EXPERTS - TOPK + 1):
                here = slot_ref[pl.ds(expert, 1), tokens_of(tile)] == slot
                value = jnp.where(
                    here, gdense[pl.ds(expert * HEAD, HEAD), tokens_of(tile)], value
                )
                gate = jnp.where(here, gates_ref[pl.ds(expert, 1), tokens_of(tile)], gate)
            mixed = mixed_ref[:, at].astype(F32)
            dots = jnp.sum(mixed * value, axis=0, keepdims=True)
            rounded = (value * gate).astype(BF16)
            gt_ref[:, at] = rounded
            delta_ref[:, at] = jnp.sum(mixed * rounded.astype(F32), axis=0, keepdims=True)
            for expert in range(slot, slot + EXPERTS - TOPK + 1):
                here = slot_ref[pl.ds(expert, 1), tokens_of(tile)] == slot
                sums[pl.ds(expert, 1), tokens_of(tile)] += jnp.where(here, dots, 0.0)
    gates = gates_ref[...]
    dots = sums[...]
    grad_logits = gates * (dots - jnp.sum(gates * dots, axis=0, keepdims=True))
    gl_ref[...] = grad_logits
    high, low = split_two(grad_logits)
    small_ref[...] = jnp.concatenate(
        [
            nn(high, hid_ref[...]) + nn(low, hid_ref[...]),
            gain_grad_ref[...],
            jnp.zeros((7, D), F32),
        ],
        axis=0,
    )


def attend_back(
    qc_ref,
    gt_ref,
    lse_ref,
    delta_ref,
    kv_ref,
    after_ref,
    pair0,
    pair1,
    pair2,
    pair3,
    dqc,
    keys,
    values,
    kt,
    dkeys,
    dvalues,
    dq,
    scores,
    grads,
    shares,
    slopes,
):
    x = lax.axis_index("x")
    keys[...] = kv_ref[:, 0:HEAD]
    values[...] = kv_ref[:, HEAD : 2 * HEAD]
    for tile in range(TILES):
        kt[tile] = kv_ref[pl.ds(tile * TILE, TILE), 0:HEAD].astype(F32).T.astype(BF16)
    dkeys[...] = jnp.zeros_like(dkeys)
    dvalues[...] = jnp.zeros_like(dvalues)
    later = causal()
    for tile in range(2):
        last = own_blocks(x)[tile]
        dq[...] = jnp.zeros_like(dq)

        def step(index, masked):
            at = block(index, TILE)
            sums = {}

            def multiply(slot):
                here = pl.ds(slot * TILE, TILE)
                route = lanes_of(tile, slot)
                scores[:, here] = nn(keys[at, :], qc_ref[:, route])
                grads[:, here] = nn(values[at, :], gt_ref[:, route])

            def lift(slot):
                here = pl.ds(slot * TILE, TILE)
                route = lanes_of(tile, slot)
                value = jnp.exp2(scores[:, here] * SCORE2 - lse_ref[:, route])
                if masked:
                    value = jnp.where(later, value, 0.0)
                shares[:, here] = value.astype(BF16)
                slopes[:, here] = (value * (grads[:, here] - delta_ref[:, route])).astype(BF16)

            def gather(slot):
                here = pl.ds(slot * TILE, TILE)
                route = lanes_of(tile, slot)
                dq[:, here] += nn(kt[index], slopes[:, here])
                one = nt(qc_ref[:, route], slopes[:, here])
                two = nt(gt_ref[:, route], shares[:, here])
                if slot:
                    one, two = sums[0] + one, sums[1] + two
                sums[0], sums[1] = one, two

            staged(TOPK, multiply, lift, gather)
            dkeys[index] += sums[0]
            dvalues[index] += sums[1]

        step(last, True)

        @pl.loop(0, last)
        def _(index):
            step(index, False)

        dqc[:, pl.ds(tile * LANES, LANES)] = (dq[...] * SCORE).astype(BF16)

    def pair(low, high):
        return jnp.concatenate(
            [
                jnp.concatenate([dkeys[low], dkeys[high]], axis=1) * SCORE,
                jnp.concatenate([dvalues[low], dvalues[high]], axis=1),
            ],
            axis=0,
        ).astype(BF16)

    for away, ref in enumerate((pair0, pair1, pair2, pair3)):
        ref[...] = pair(*own_blocks(lax.rem(x + away, GROUPS)))


def query_part(
    dqc,
    slot_ref,
    hid_ref,
    small_ref,
    wr_ref,
    mine_ref,
    other_ref,
    dqall,
    gain_ref,
    keep_ref,
    send_ref,
):
    core = lax.axis_index("core")
    for tile in range(2):
        for expert in range(EXPERTS):
            dqall[pl.ds(expert * HEAD, HEAD), tokens_of(tile)] = expand(
                slot_ref, dqc, tile, expert
            ).astype(BF16)
    gain = jnp.sum(
        small_ref[0:EXPERTS] * wr_ref[...].astype(F32), axis=0, keepdims=True
    )
    for owner in range(GROUPS):
        grad = nn(dqall[pl.ds(owner * OWN, OWN), :], hid_ref[...])
        put_pieces(grad.astype(BF16), owner, core, keep_ref, send_ref)
        one, two = mine_ref[owner].astype(F32), other_ref[owner].astype(F32)
        first, last = jnp.where(core == 0, one, two), jnp.where(core == 0, two, one)
        gain = gain + jnp.sum(grad[0:HALF] * first, axis=0, keepdims=True)
        gain = gain + jnp.sum(grad[HALF:OWN] * last, axis=0, keepdims=True)
    gain_ref[...] = gain


def finish(
    tok_ref,
    high_ref,
    gm_ref,
    dqall,
    gl_ref,
    wr_ref,
    mine_ref,
    other_ref,
    pairs_ref,
    wkv_ref,
    gain_ref,
    out_ref,
    out_high_ref,
):
    core = lax.axis_index("core")
    high, low = split_two(gl_ref[...])
    grad = tn(high, wr_ref[...]) + tn(low, wr_ref[...])
    for owner in range(GROUPS):
        grad = grad + tn(dqall[block(2 * owner + core, HALF), :], mine_ref[owner])
        grad = grad + tn(dqall[block(2 * owner + 1 - core, HALF), :], other_ref[owner])
    grad = grad + lax.dot_general(
        pairs_ref[...], wkv_ref[...], (((0,), (1,)), ((), ())), preferred_element_type=F32
    )
    rows = jnp.concatenate([tok_ref[0:TILE], high_ref[0:TILE]], axis=0).astype(F32)
    scale = scale_of(rows)
    unit = rows * scale
    inner = grad * gain_ref[...]
    result = (
        gm_ref[...] + scale * (inner - unit * jnp.mean(inner * unit, axis=-1, keepdims=True))
    ).astype(BF16)
    out_ref[...] = result
    out_high_ref[...] = result[TILE:TOK]


def added(near, one, two, three):
    return (
        (near.astype(F32) + two.astype(F32)) + (one.astype(F32) + three.astype(F32))
    ).astype(BF16)


def pair_feed(arrive, keep, arrived, keep_o, arrived_o, out_hbm, one, two, three, four, out, sems):
    arrive()
    parts = [pl.ds(16 * index, 16) for index in range(4)]
    loads = []
    for index, part in enumerate(parts):
        loads.append(
            [
                pltpu.make_async_copy(source.at[part], target.at[part], sems.at[index, place])
                for place, (source, target) in enumerate(
                    ((keep, one), (arrived, two), (keep_o, three), (arrived_o, four))
                )
            ]
        )
        for load in loads[-1]:
            load.start()
    stores = []
    for index, part in enumerate(parts):
        for load in loads[index]:
            load.wait()
        out[part, 0:128, :] = (one[part].astype(F32) + two[part].astype(F32)).astype(BF16)
        out[part, 128:176, :] = (three[part].astype(F32) + four[part].astype(F32)).astype(BF16)
        stores.append(pltpu.make_async_copy(out.at[part], out_hbm.at[part], sems.at[index, 4]))
        stores[-1].start()
    for store in stores:
        store.wait()


def merge(
    arrive,
    pieces_hbm,
    keep_hbm,
    arrived_hbm,
    near,
    one,
    two,
    three,
    hid_ref,
    small_ref,
    gain_rows,
    wkv_ref,
    gain_ref,
    out_hbm,
    part_ref,
    pair_ref,
    pieces,
    keep_q,
    arrived_q,
    feed,
    rest,
    sems,
):
    parts = [pl.ds(16 * index, 16) for index in range(4)]
    first = [
        pltpu.make_async_copy(keep_hbm, keep_q, sems.at[0]),
        pltpu.make_async_copy(arrived_hbm, arrived_q, sems.at[1]),
    ]
    loads = [
        pltpu.make_async_copy(pieces_hbm.at[part], pieces.at[part], sems.at[2 + index])
        for index, part in enumerate(parts)
    ]
    for load in first + loads:
        load.start()
    arrive()
    pair = added(near[...], one[...], two[...], three[...])
    pair_ref[...] = pair
    grad_kv = nn(pair, hid_ref[...])
    gain_grad = (
        gain_rows[...]
        + jnp.sum(grad_kv * wkv_ref[...].astype(F32).T, axis=0, keepdims=True)
    ) / gain_ref[...]
    last = jnp.concatenate([small_ref[0:25], gain_grad, small_ref[26:32]], axis=0)
    shared = jnp.concatenate([grad_kv, last], axis=0).astype(BF16)
    for piece in range(16):
        for place in range(3):
            row, group = divmod(3 * piece + place, 4)
            if 16 * row < SMALL:
                value = shared[16 * row : 16 * row + 16, 128 * group : 128 * group + 128]
            else:
                value = jnp.zeros((16, 128), BF16)
            for far in range(GROUPS):
                rest[16 * far + piece, 48 + 16 * place : 64 + 16 * place] = value
    for load in first:
        load.wait()
    rest[:, 0:48, :] = (keep_q[...].astype(F32) + arrived_q[...].astype(F32)).astype(BF16)
    stores = [pltpu.make_async_copy(rest, out_hbm.at[:, pl.ds(128, 96), :], sems.at[6])]
    stores[0].start()
    total = jnp.zeros((176, 128), F32)
    for index in range(4):
        loads[index].wait()
        for piece in range(16 * index, 16 * index + 16):
            total = total + pieces[piece].astype(F32)
    total = total.astype(BF16)
    part_ref[...] = total[128:176]
    for index in range(64):
        feed[index] = total[0:128]
    stores.append(pltpu.make_async_copy(feed, out_hbm.at[:, pl.ds(0, 128), :], sems.at[7]))
    stores[1].start()
    for store in stores:
        store.wait()


def collect(spread, part_ref, out_ref, rest, sems):
    load = pltpu.make_async_copy(spread.at[:, pl.ds(128, 96), :], rest, sems.at[0])
    load.start()
    load.wait()
    total = rest[0].astype(F32)
    for index in range(1, 64):
        total = total + rest[index].astype(F32)
    total = total.astype(BF16)
    for index in range(16):
        out_ref[index, 0:PIECE] = part_ref[...]
        out_ref[index, PIECE:EXTRA] = total


def unpack(at_ref, half_ref, *refs):
    up_ref, down_ref = refs[-2:]
    for group in range(2):
        up_ref[:, 128 * group : 128 * group + 128] = (
            half_ref[:, pl.ds(32 * group, 32), :].astype(F32).reshape(D, 128)
        )
    for group in range(4):
        down_ref[:, 128 * group : 128 * group + 128] = (
            half_ref[:, pl.ds(64 + 16 * group, 16), :].astype(F32).reshape(CHUNK, 128)
        )


def assemble(mine_ref, other_ref, output_ref, query_ref, kv_ref, router_ref, heads_ref, feed_ref, shared):
    core = lax.axis_index("core")
    for ref, half in ((mine_ref, core), (other_ref, 1 - core)):
        for column in range(4):
            for row in range(4):
                rows = pl.ds(pl.multiple_of(half * HALF + row * PIECE, 16), PIECE)
                for index, target in enumerate((output_ref, query_ref)):
                    target[rows, pl.ds(128 * column, 128)] = ref[
                        4 * column + row, pl.ds(PIECE * index, PIECE), :
                    ].astype(F32)
    for piece in range(14):
        for place in range(3):
            row, group = divmod(3 * piece + place, 4)
            if 16 * row < SMALL:
                at = pl.ds(2 * PIECE + 16 * place, 16)
                shared[16 * row : 16 * row + 16, 128 * group : 128 * group + 128] = mine_ref[
                    piece, at, :
                ].astype(F32) + other_ref[piece, at, :].astype(F32)
    kv_ref[...] = shared[0:128].T
    router_ref[...] = shared[128:152]
    feed_ref[...] = shared[152:153]
    heads_ref[...] = shared[153:154]


def shape(dims, dtype=BF16):
    return jax.ShapeDtypeStruct(dims, dtype)


VMEM = pl.BlockSpec(memory_space=pltpu.VMEM)
SMEM = pl.BlockSpec(memory_space=pltpu.SMEM)
HBM = pl.BlockSpec(memory_space=pltpu.HBM)
ANY = pl.BlockSpec(memory_space=pl.ANY)


def nothing(*refs):
    pass


def after(value, *others):
    return pl.pallas_call(
        nothing,
        out_shape=shape(value.shape, value.dtype),
        in_specs=[ANY] * (1 + len(others)),
        out_specs=ANY,
        input_output_aliases={0: 0},
        name="after",
    )(value, *others)


def size_of(value):
    return math.prod(value.shape) * jnp.dtype(value.dtype).itemsize


def call(kernel, micros, inputs, outputs, scratch=(), far=(), far_out=(), sent=(), own_loads=False):
    near = [index for index in range(len(inputs)) if index not in far]
    count, ends = len(inputs), len(inputs) + len(outputs)

    def body(*refs):
        sources, results, own = list(refs[:count]), refs[count:ends], refs[ends:]
        buffers, sems = own[len(scratch) : -1], own[-1]
        loads = []
        for index, (source, buffer) in enumerate(zip(near, buffers)):
            loads.append(pltpu.make_async_copy(sources[source], buffer, sems.at[index]))
            sources[source] = buffer
        def arrive():
            for load in loads:
                load.wait()

        for load in loads:
            load.start()
        if own_loads:
            kernel(arrive, *sources, *results, *own[: len(scratch)])
        else:
            arrive()
            kernel(*sources, *results, *own[: len(scratch)])

    buffers = [pltpu.VMEM(inputs[index].shape, inputs[index].dtype) for index in near]
    limit = LIMIT - sum(size_of(inputs[index]) for index in sent)
    return pl.pallas_call(
        body,
        out_shape=outputs,
        in_specs=[ANY if index in sent else HBM for index in range(count)],
        out_specs=tuple(HBM if index in far_out else VMEM for index in range(len(outputs))),
        scratch_shapes=[
            *scratch,
            *buffers,
            pltpu.SemaphoreType.DMA((len(near),)),
        ],
        compiler_params=pltpu.CompilerParams(vmem_limit_bytes=limit),
        cost_estimate=pl.CostEstimate(
            flops=int(micros * 1e9), bytes_accessed=(1 << 20) if micros else 0, transcendentals=0
        ),
        name=kernel.__name__,
    )(*inputs)


def turn(size, step):
    return [(index, (index + step) % size) for index in range(size)]


def swap(value):
    return lax.ppermute(value, "core", turn(2, 1))


def mirror(value):
    return lax.ppermute(value, "x", [(0, 3), (3, 0), (1, 2), (2, 1)])


def around(value, axis):
    return [lax.ppermute(value, axis, turn(4, step)) for step in (1, 2, 3)]


def vmem(dims, dtype=F32):
    return pltpu.VMEM(dims, dtype)


def shards(
    tokens,
    expert_ids,
    cotangent,
    gain_heads,
    key_value_weight,
    router_weight,
    query_weight,
    output_weight,
    gain_feed,
    up_weight,
    down_weight,
):
    x = lax.axis_index("x")
    core = lax.axis_index("core")
    chips = ("x", "y", "z")
    tok = tokens[0]
    cot = cotangent[0]
    ids = expert_ids[0].T
    wq = jnp.swapaxes(query_weight, 1, 2).reshape(OWN, D)
    wr = router_weight.T
    wkv = key_value_weight
    gain1 = gain_heads.reshape(1, D)
    gain2 = gain_feed.reshape(1, D)

    carried = jnp.concatenate(
        [
            tok[TILE:TOK],
            jnp.pad(ids[:, TILE:TOK].astype(BF16), ((0, 8), (0, D - TILE))),
        ],
        axis=0,
    )
    carried = mirror(carried)
    mine = lax.dynamic_slice(wq, (core * HALF, 0), (HALF, D))
    mine = lax.all_to_all(
        jnp.broadcast_to(mine[None], (GROUPS, HALF, D)), "x", split_axis=0, concat_axis=0, tiled=True
    )
    first, kv = call(
        pairs_first,
        2,
        (tok, gain1, wkv),
        (shape((TILE, D)), shape((TOK, 2 * HEAD))),
    )
    kvs = [kv] + around(kv, "x")
    cot_high, hidden, turned, gates, slots = call(
        prepare,
        3,
        (first, carried, ids, gain1, wr, cot, *kvs[1:]),
        (
            shape((TILE, D)),
            shape((TOK, D)),
            shape((D, TOK)),
            shape((EXPERTS, TOK), F32),
            shape((EXPERTS, TOK), jnp.int32),
        ),
        far=(6, 7, 8),
        sent=(1, 6, 7, 8),
    )
    mine = after(mine, slots)
    wqs = (mine, swap(mine))
    wo = after(
        jnp.broadcast_to(output_weight.reshape(1, OWN, D), (GROUPS, OWN, D)), wqs[1]
    )
    wo = lax.all_to_all(wo, "x", split_axis=0, concat_axis=0, tiled=True)
    wo = wo.reshape(EXPERTS * HEAD, D)
    cot_high = mirror(cot_high)

    qc, mixed, lse, kv_all, dense = call(
        attend,
        14,
        (turned, slots, gates, *wqs, *kvs),
        (
            shape((HEAD, ROUTES)),
            shape((HEAD, ROUTES)),
            shape((1, ROUTES), F32),
            shape((LENGTH, 2 * HEAD)),
            shape((EXPERTS * HEAD, TOK)),
        ),
        [
            vmem((EXPERTS * HEAD, TOK)),
            vmem((LENGTH, HEAD), BF16),
            vmem((GROUPS, HEAD + 16, 2 * TILE), BF16),
            vmem((1, LANES)),
            vmem((HEAD + 16, LANES)),
            vmem((2 * TILE, LANES)),
            vmem((2 * TILE, LANES), BF16),
        ],
        sent=(3, 4, 6, 7, 8),
    )

    result, out_high, middle, back, keep, send = call(
        feed_part,
        17,
        (tok, carried, cot, cot_high, dense, gain2, wo, up_weight, down_weight),
        (
            shape((TOK, D)),
            shape((TILE, D)),
            shape((TOK, D), F32),
            shape((TOK, D), F32),
            shape((64, 128, 128)),
            shape((64, 128, 128)),
        ),
        [
            vmem((TOK, D), BF16),
            vmem((D, TOK), BF16),
            vmem((TOK, D), BF16),
            vmem((TOK, D)),
            vmem((EXPERTS * HEAD, D), BF16),
            vmem((D, FF), BF16),
            vmem((FF, D), BF16),
            vmem((8, 16, 128, 128), BF16),
            pltpu.SemaphoreType.DMA((3,)),
            pltpu.SemaphoreType.DMA((8,)),
        ],
        far=(6, 7, 8),
        far_out=(4, 5),
        sent=(3, 6),
        own_loads=True,
    )
    arrived = swap(send)
    out_back = mirror(out_high)

    grad_middle, turned_gm, gain_grad, keep_o, send_o = call(
        norm_part,
        4,
        (cot, cot_high, middle, back, dense, gain2),
        (
            shape((TOK, D), F32),
            shape((D, TOK)),
            shape((1, D), F32),
            shape((64, PIECE, 128)),
            shape((64, PIECE, 128)),
        ),
        [vmem((TOK, D), BF16)],
        sent=(1,),
    )
    arrived_o = swap(send_o)
    (paired,) = call(
        pair_feed,
        4,
        (keep, arrived, keep_o, arrived_o),
        (shape((64, 176, 128)),),
        [
            vmem((64, 128, 128), BF16),
            vmem((64, 128, 128), BF16),
            vmem((64, PIECE, 128), BF16),
            vmem((64, PIECE, 128), BF16),
            vmem((64, 176, 128), BF16),
            pltpu.SemaphoreType.DMA((4, 5)),
        ],
        far=(0, 1, 2, 3),
        far_out=(0,),
        sent=(1, 3),
        own_loads=True,
    )
    gt, delta, grad_logits, small = call(
        route_part,
        6,
        (turned_gm, mixed, slots, gates, hidden, wo, gain_grad, paired),
        (
            shape((HEAD, ROUTES)),
            shape((1, ROUTES), F32),
            shape((EXPERTS, TOK), F32),
            shape((32, D), F32),
        ),
        [vmem((EXPERTS * HEAD, TOK)), vmem((EXPERTS, TOK))],
        far=(7,),
        sent=(5,),
    )
    pieces = lax.all_to_all(paired, chips, split_axis=0, concat_axis=0, tiled=True)

    pair, *others, dqc = call(
        attend_back,
        20,
        (qc, gt, lse, delta, kv_all, out_back),
        (
            *[shape((2 * HEAD, TOK))] * GROUPS,
            shape((HEAD, ROUTES)),
        ),
        [
            vmem((LENGTH, HEAD), BF16),
            vmem((LENGTH, HEAD), BF16),
            vmem((TILES, HEAD, TILE), BF16),
            vmem((TILES, HEAD, TILE)),
            vmem((TILES, HEAD, TILE)),
            vmem((HEAD, LANES)),
            vmem((TILE, LANES)),
            vmem((TILE, LANES)),
            vmem((TILE, LANES), BF16),
            vmem((TILE, LANES), BF16),
        ],
        far=(5,),
        sent=(5,),
    )
    arrived_pairs = [
        lax.ppermute(value, "x", turn(4, step + 1)) for step, value in enumerate(others)
    ]
    dqall, gain_rows, keep_q, send_q = call(
        query_part,
        6,
        (dqc, slots, hidden, small, wr, *wqs),
        (
            shape((EXPERTS * HEAD, TOK)),
            shape((1, D), F32),
            shape((64, PIECE, 128)),
            shape((64, PIECE, 128)),
        ),
        sent=(5, 6),
    )
    arrived_q = swap(send_q)
    merged, part, pair_sum = call(
        merge,
        5,
        (
            pieces,
            keep_q,
            arrived_q,
            pair,
            *arrived_pairs,
            hidden,
            small,
            gain_rows,
            wkv,
            gain1,
        ),
        (shape((64, 224, 128)), shape((PIECE, 128)), shape((2 * HEAD, TOK))),
        [
            vmem((64, 176, 128), BF16),
            vmem((64, PIECE, 128), BF16),
            vmem((64, PIECE, 128), BF16),
            vmem((64, 128, 128), BF16),
            vmem((64, 96, 128), BF16),
            pltpu.SemaphoreType.DMA((8,)),
        ],
        far=(0, 1, 2),
        far_out=(0,),
        own_loads=True,
        sent=(0, 2, 4, 5, 6),
    )
    grad_whole, grad_high = call(
        finish,
        3,
        (tok, carried, grad_middle, dqall, grad_logits, wr, *wqs, pair_sum, wkv, gain1),
        (shape((TOK, D)), shape((TILE, D))),
    )
    spread = lax.all_to_all(merged, chips, split_axis=0, concat_axis=0, tiled=True)
    result = lax.dynamic_update_slice(result, out_back, (TILE, 0))
    grad_back = mirror(grad_high)
    spread = after(spread, grad_back, result)
    grad_tokens = lax.dynamic_update_slice(grad_whole, grad_back, (TILE, 0))
    (part,) = call(
        collect,
        0,
        (spread, part),
        (shape((16, EXTRA, 128)),),
        [vmem((64, 96, 128), BF16), pltpu.SemaphoreType.DMA((1,))],
        far=(0,),
        sent=(0,),
    )
    feed_other = swap(spread)
    part = lax.all_to_all(part, ("y", "z"), split_axis=0, concat_axis=0, tiled=True)

    def unpacked(value, half, *earlier, extra=()):
        half_spec = pl.BlockSpec((16, 128, 128), lambda index, at: (index, 0, 0))
        return pl.pallas_call(
            unpack,
            grid_spec=pltpu.PrefetchScalarGridSpec(
                num_scalar_prefetch=1,
                grid=(4,),
                in_specs=[half_spec] + [HBM] * len(earlier) + [ANY] * len(extra),
                out_specs=(
                    pl.BlockSpec((D, CHUNK), lambda index, at: (0, 4 * at[0] + index)),
                    pl.BlockSpec((CHUNK, D), lambda index, at: (4 * at[0] + index, 0)),
                ),
            ),
            out_shape=(shape((D, FF), F32), shape((FF, D), F32)),
            input_output_aliases={2: 0, 3: 1} if earlier else {},
            compiler_params=pltpu.CompilerParams(vmem_limit_bytes=LIMIT - 2 * MIB),
            name="unpack",
        )(half.reshape(1), value, *earlier, *extra)

    grads = unpacked(spread, core)
    grad_up, grad_down = unpacked(feed_other, 1 - core, *grads)
    part = after(part, grad_up)
    part_other = swap(part)
    output_grad, query_grad, kv_grad, router_grad, gain_heads_grad, gain_feed_grad = call(
        assemble,
        4,
        (part, part_other),
        (
            shape((OWN, D), F32),
            shape((OWN, D), F32),
            shape((D, 2 * HEAD), F32),
            shape((EXPERTS, D), F32),
            shape((1, D), F32),
            shape((1, D), F32),
        ),
        [vmem((SMALL, D))],
        sent=(0, 1),
    )
    return (
        result[None],
        grad_tokens[None],
        gain_heads_grad.reshape(D),
        kv_grad,
        router_grad.T,
        query_grad.reshape(OWN // HEAD, HEAD, D).swapaxes(1, 2),
        output_grad.reshape(OWN // HEAD, HEAD, D),
        gain_feed_grad.reshape(D),
        grad_up,
        grad_down,
    )


def solution(mesh):
    grid = Mesh(mesh.devices.reshape(4, 4, 4, 2), ("x", "y", "z", "core"))
    dp = ("y", "z", "core")
    return jax.shard_map(
        shards,
        mesh=grid,
        in_specs=(
            P(dp, "x", None),
            P(dp, "x", None),
            P(dp, "x", None),
            P(),
            P(),
            P(),
            P("x", None, None),
            P("x", None, None),
            P(),
            P(),
            P(),
        ),
        out_specs=(
            P(dp, "x", None),
            P(dp, "x", None),
            P(),
            P(),
            P(),
            P("x", None, None),
            P("x", None, None),
            P(),
            P(),
            P(),
        ),
        check_vma=False,
    )
```

```python
import math

import jax
import jax.numpy as jnp
from jax import lax
from jax.experimental import pallas as pl
from jax.experimental.pallas import tpu as pltpu
from jax.sharding import Mesh, PartitionSpec as P

D = 512
HEAD = 64
EXPERTS = 24
TOPK = 8
FF = 2048
TOK = 512
GROUPS = 4
LENGTH = TOK * GROUPS
OWN = EXPERTS // GROUPS * HEAD
HALF = OWN // 2
TILE = 256
LANES = TOPK * TILE
TILES = LENGTH // TILE
ROUTES = TOK * TOPK
CHUNK = 256
SMALL = 160
PIECE = 48
EXTRA = 3 * PIECE

EPSILON = 1e-06
CURVE_SCALE = 0.7978845608028654
CURVE_CUBIC = 0.044715
SCORE = HEAD**-0.5
SCORE2 = SCORE * 1.4426950408889634
LOW = -1e30

F32 = jnp.float32
BF16 = jnp.bfloat16
MIB = 1 << 20
LIMIT = 62 * MIB - (1 << 18)


def nn(a, b):
    return lax.dot_general(a, b, (((1,), (0,)), ((), ())), preferred_element_type=F32)


def nt(a, b):
    return lax.dot_general(a, b, (((1,), (1,)), ((), ())), preferred_element_type=F32)


def tn(a, b):
    return lax.dot_general(a, b, (((0,), (0,)), ((), ())), preferred_element_type=F32)


def split_two(value):
    high = value.astype(BF16)
    return high, (value - high.astype(F32)).astype(BF16)


def scale_of(rows):
    return lax.rsqrt(jnp.mean(rows * rows, axis=-1, keepdims=True) + EPSILON)


def lanes_of(tile, slot):
    return pl.ds(tile * LANES + slot * TILE, TILE)


def tokens_of(tile):
    return pl.ds(tile * TILE, TILE)


def block(index, size):
    return pl.ds(pl.multiple_of(index * size, size), size)


def slots_of(expert):
    return range(max(0, expert - (EXPERTS - TOPK)), min(TOPK - 1, expert) + 1)


def pairs_first(tok_ref, gain_ref, wkv_ref, first_ref, kv_ref):
    rows = tok_ref[...].astype(F32)
    first = (rows * scale_of(rows) * gain_ref[...]).astype(BF16)
    first_ref[...] = first[0:TILE]
    kv_ref[...] = nn(first, wkv_ref[...]).astype(BF16)


def prepare(
    first_ref,
    carried_ref,
    ids_ref,
    gain_ref,
    wr_ref,
    cot_ref,
    after1,
    after2,
    after3,
    after4,
    cot_high_ref,
    hid_ref,
    turned_ref,
    gates_ref,
    slot_ref,
):
    cot_high_ref[...] = cot_ref[TILE:TOK]
    rows = carried_ref[0:TILE].astype(F32)
    high = rows * scale_of(rows) * gain_ref[...]
    turned_ref[:, 0:TILE] = first_ref[...].astype(F32).T.astype(BF16)
    turned_ref[:, TILE:TOK] = high.T.astype(BF16)
    hidden = jnp.concatenate([first_ref[...], high.astype(BF16)], axis=0)
    hid_ref[...] = hidden
    logits = nt(wr_ref[...], hidden)[0:EXPERTS]
    ids = jnp.concatenate(
        [ids_ref[:, 0:TILE], carried_ref[TILE : TILE + 16, 0:TILE].astype(F32)[0:TOPK].astype(jnp.int32)], axis=1
    )
    names = lax.broadcasted_iota(jnp.int32, (EXPERTS, TOK), 0)
    chosen = names == ids[0:1]
    for route in range(1, TOPK):
        chosen = chosen | (names == ids[route : route + 1])
    count = jnp.where(chosen, 1.0, 0.0)
    below = lax.broadcasted_iota(jnp.int32, (EXPERTS, EXPERTS), 0) > lax.broadcasted_iota(
        jnp.int32, (EXPERTS, EXPERTS), 1
    )
    rank = nn(jnp.where(below, 1.0, 0.0).astype(BF16), count.astype(BF16))
    slot_ref[...] = jnp.where(chosen, rank, -1.0).astype(jnp.int32)
    peak = jnp.max(jnp.where(chosen, logits, -3e38), axis=0, keepdims=True)
    raised = jnp.where(chosen, jnp.exp(logits - peak), 0.0)
    gates_ref[...] = raised / jnp.sum(raised, axis=0, keepdims=True)


def compact(slot_ref, dense_ref, tile, slot):
    value = jnp.zeros((HEAD, TILE), F32)
    for expert in range(slot, slot + EXPERTS - TOPK + 1):
        here = slot_ref[pl.ds(expert, 1), tokens_of(tile)] == slot
        value = jnp.where(here, dense_ref[pl.ds(expert * HEAD, HEAD), tokens_of(tile)], value)
    return value


def expand(slot_ref, packed_ref, tile, expert):
    row = slot_ref[pl.ds(expert, 1), tokens_of(tile)]
    value = jnp.zeros((HEAD, TILE), F32)
    for slot in slots_of(expert):
        value = jnp.where(row == slot, packed_ref[:, lanes_of(tile, slot)].astype(F32), value)
    return value


def causal():
    return lax.broadcasted_iota(jnp.int32, (TILE, TILE), 0) <= lax.broadcasted_iota(
        jnp.int32, (TILE, TILE), 1
    )


def staged(count, *stages):
    for time in range(count + len(stages) - 1):
        for late, stage in enumerate(stages):
            if 0 <= time - late < count:
                stage(time - late)


def own_blocks(x):
    return 2 * x, 7 - 2 * x


def attend(
    arrive,
    turned_ref,
    slot_ref,
    gates_ref,
    mine_hbm,
    other_hbm,
    kv0,
    kv1,
    kv2,
    kv3,
    qc_ref,
    mixed_ref,
    lse_ref,
    kv_ref,
    dense_ref,
    qall,
    keys,
    vt,
    peak,
    acc,
    scores,
    shares,
    mine_ref,
    other_ref,
    sems,
):
    loads = (
        pltpu.make_async_copy(mine_hbm, mine_ref, sems.at[0]),
        pltpu.make_async_copy(other_hbm, other_ref, sems.at[1]),
    )
    for load in loads:
        load.start()
    arrive()
    x = lax.axis_index("x")
    core = lax.axis_index("core")
    owners = [lax.rem(x + GROUPS - away, GROUPS) for away in range(GROUPS)]
    for owner, kv in zip(owners, (kv0, kv1, kv2, kv3)):
        turned = kv[:, HEAD : 2 * HEAD].astype(F32).T.astype(BF16)
        kv_ref[block(owner, TOK), :] = kv[...]
        keys[block(owner, TOK), :] = kv[:, 0:HEAD]
        vt[owner, 0:HEAD, :] = turned
        vt[owner, HEAD : HEAD + 16, :] = jnp.ones((16, 2 * TILE), BF16)
    for load in loads:
        load.wait()
    for owner in range(GROUPS):
        qall[block(2 * owner + core, HALF), :] = nn(mine_ref[owner], turned_ref[...])
        qall[block(2 * owner + 1 - core, HALF), :] = nn(other_ref[owner], turned_ref[...])
    for tile in range(2):
        for slot in range(TOPK):
            qc_ref[:, lanes_of(tile, slot)] = compact(slot_ref, qall, tile, slot).astype(BF16)

    wide = 2 * TILE
    later = lax.broadcasted_iota(jnp.int32, (TILE, wide), 0) <= (
        lax.broadcasted_iota(jnp.int32, (TILE, wide), 1) & (TILE - 1)
    )
    later_two = lax.broadcasted_iota(jnp.int32, (wide, wide), 0) <= TILE + (
        lax.broadcasted_iota(jnp.int32, (wide, wide), 1) & (TILE - 1)
    )

    def step(tile, start, size, values, mask):
        fades = {}

        def multiply(unit):
            at = pl.ds(unit * wide, wide)
            route = pl.ds(tile * LANES + unit * wide, wide)
            scores[0:size, at] = nn(keys[pl.ds(start, size), :], qc_ref[:, route])

        def lift(unit):
            at = pl.ds(unit * wide, wide)
            value = scores[0:size, at]
            if mask is not None:
                value = jnp.where(mask, value, LOW)
            top = jnp.max(value, axis=0, keepdims=True)
            if mask is None:
                before = peak[:, at]
                top = jnp.maximum(before, top)
                fades[unit] = jnp.exp2((before - top) * SCORE2)
            shares[0:size, at] = jnp.exp2((value - top) * SCORE2).astype(BF16)
            peak[:, at] = top

        def gather(unit):
            at = pl.ds(unit * wide, wide)
            part = nn(values, shares[0:size, at])
            if mask is None:
                part = acc[:, at] * fades[unit] + part
            acc[:, at] = part

        staged(LANES // wide, multiply, lift, gather)

    for tile in range(2):
        if tile == 0:
            start = pl.multiple_of(2 * x * TILE, TILE)
            step(tile, start, TILE, vt[x, :, 0:TILE], later)
            count = x
        else:
            start = pl.multiple_of((3 - x) * wide, wide)
            step(tile, start, wide, vt[3 - x], later_two)
            count = 3 - x

        @pl.loop(0, count)
        def _(index):
            step(tile, pl.multiple_of(index * wide, wide), wide, vt[index], None)

        here = pl.ds(tile * LANES, LANES)
        total = acc[HEAD : HEAD + 1, :]
        mixed_ref[:, here] = (acc[0:HEAD, :] / total).astype(BF16)
        lse_ref[:, here] = peak[...] * SCORE2 + jnp.log2(total)
    for tile in range(2):
        for expert in range(EXPERTS):
            value = expand(slot_ref, mixed_ref, tile, expert)
            gate = gates_ref[pl.ds(expert, 1), tokens_of(tile)]
            dense_ref[pl.ds(expert * HEAD, HEAD), tokens_of(tile)] = (value * gate).astype(BF16)


def feed_part(
    arrive,
    tok_ref,
    high_ref,
    cot_ref,
    cot_high_ref,
    dense_ref,
    gain_ref,
    wo_hbm,
    up_hbm,
    down_hbm,
    out_ref,
    out_high_ref,
    middle_ref,
    back_ref,
    keep_hbm,
    send_hbm,
    feed,
    feed_t,
    cot,
    result,
    wo_ref,
    up_ref,
    down_ref,
    staging,
    sems,
    out_sems,
):
    core = lax.axis_index("core")
    sources = ((wo_hbm, wo_ref), (up_hbm, up_ref), (down_hbm, down_ref))
    loads = [
        pltpu.make_async_copy(source, target, sems.at[index])
        for index, (source, target) in enumerate(sources)
    ]
    for load in loads:
        load.start()
    arrive()
    cot[0:TILE] = cot_ref[0:TILE]
    cot[TILE:TOK] = cot_high_ref[...]
    total = jnp.concatenate([tok_ref[0:TILE], high_ref[0:TILE]], axis=0).astype(F32)
    loads[0].wait()
    total = total + tn(dense_ref[...], wo_ref[...])
    middle_ref[...] = total
    feed32 = total * scale_of(total) * gain_ref[...]
    feed[...] = feed32.astype(BF16)
    feed_t[...] = feed32.T.astype(BF16)
    result[...] = total
    back_ref[...] = jnp.zeros_like(back_ref)
    loads[1].wait()
    loads[2].wait()

    def out_copy(index, target):
        return pltpu.make_async_copy(
            staging.at[index],
            target.at[pl.ds(pl.multiple_of(lax.rem(index, 4) * 16, 16), 16)],
            out_sems.at[index],
        )

    @pl.loop(0, FF // CHUNK // 4)
    def _(turn_index):
        held = {}

        def multiply(unit):
            index = 4 * turn_index + unit
            up = up_ref[:, block(index, CHUNK)]
            down = down_ref[block(index, CHUNK), :]
            held[unit] = (up, down, nn(feed[...], up), nt(cot[...], down))

        def lift(unit):
            up, down, before, grad_active = held[unit]
            square = before * before
            curve = jnp.tanh(CURVE_SCALE * before * (1.0 + CURVE_CUBIC * square))
            rise = 0.5 * (1.0 + curve)
            slope = rise + 0.5 * before * (1.0 - curve * curve) * (
                CURVE_SCALE * (1.0 + 3.0 * CURVE_CUBIC * square)
            )
            active = (before * rise).astype(BF16)
            held[unit] = (up, down, active, (grad_active * slope).astype(BF16))

        def gather(unit):
            index = 4 * turn_index + unit
            up, down, active, grad_before = held[unit]
            result[...] += nn(active, down)
            back_ref[...] += nt(grad_before, up)
            grad_up = nn(feed_t[...], grad_before).astype(BF16).reshape(16, 32, CHUNK)
            grad_down = tn(active, cot[...]).astype(BF16).reshape(16, 16, D)
            for group in range(2):
                staging[index, :, pl.ds(32 * group, 32), :] = grad_up[
                    :, :, 128 * group : 128 * group + 128
                ]
            for group in range(4):
                staging[index, :, pl.ds(64 + 16 * group, 16), :] = grad_down[
                    :, :, 128 * group : 128 * group + 128
                ]

        staged(4, multiply, lift, gather)
        mine = turn_index == core

        @pl.when(mine)
        def _():
            for unit in range(4):
                out_copy(4 * turn_index + unit, keep_hbm).start()

        @pl.when(jnp.logical_not(mine))
        def _():
            for unit in range(4):
                out_copy(4 * turn_index + unit, send_hbm).start()

    out_ref[...] = result[...].astype(BF16)
    out_high_ref[...] = result[TILE:TOK].astype(BF16)
    for index in range(FF // CHUNK):
        out_copy(index, keep_hbm).wait()


def put_pieces(grad, owner, core, keep_ref, send_ref):
    def put(ref, half):
        part = grad[half * HALF : (half + 1) * HALF].reshape(4, PIECE, D)
        for group in range(4):
            ref[pl.ds(owner * 16 + 4 * group, 4), :, :] = part[
                :, :, 128 * group : 128 * group + 128
            ]

    @pl.when(core == 0)
    def _():
        put(keep_ref, 0)
        put(send_ref, 1)

    @pl.when(core == 1)
    def _():
        put(keep_ref, 1)
        put(send_ref, 0)


def norm_part(
    cot_ref,
    cot_high_ref,
    middle_ref,
    back_ref,
    dense_ref,
    gain_ref,
    gm_ref,
    turned_ref,
    gain_grad_ref,
    keep_ref,
    send_ref,
    gm16,
):
    core = lax.axis_index("core")
    total = middle_ref[...]
    scale = scale_of(total)
    unit = total * scale
    grad = back_ref[...]
    inner = grad * gain_ref[...]
    gain_grad_ref[...] = jnp.sum(grad * unit, axis=0, keepdims=True)
    cot = jnp.concatenate([cot_ref[0:TILE], cot_high_ref[...]], axis=0).astype(F32)
    grad_middle = cot + scale * (inner - unit * jnp.mean(inner * unit, axis=-1, keepdims=True))
    gm_ref[...] = grad_middle
    gm16[...] = grad_middle.astype(BF16)
    turned_ref[...] = grad_middle.T.astype(BF16)
    for owner in range(GROUPS):
        grad_out = nn(dense_ref[pl.ds(owner * OWN, OWN), :], gm16[...]).astype(BF16)
        put_pieces(grad_out, owner, core, keep_ref, send_ref)


def route_part(
    turned_ref,
    mixed_ref,
    slot_ref,
    gates_ref,
    hid_ref,
    wo_ref,
    gain_grad_ref,
    after_ref,
    gt_ref,
    delta_ref,
    gl_ref,
    small_ref,
    gdense,
    sums,
):
    gdense[...] = nn(wo_ref[...], turned_ref[...])
    sums[...] = jnp.zeros_like(sums)
    for tile in range(2):
        for slot in range(TOPK):
            at = lanes_of(tile, slot)
            value = jnp.zeros((HEAD, TILE), F32)
            gate = jnp.zeros((1, TILE), F32)
            for expert in range(slot, slot + EXPERTS - TOPK + 1):
                here = slot_ref[pl.ds(expert, 1), tokens_of(tile)] == slot
                value = jnp.where(
                    here, gdense[pl.ds(expert * HEAD, HEAD), tokens_of(tile)], value
                )
                gate = jnp.where(here, gates_ref[pl.ds(expert, 1), tokens_of(tile)], gate)
            mixed = mixed_ref[:, at].astype(F32)
            dots = jnp.sum(mixed * value, axis=0, keepdims=True)
            rounded = (value * gate).astype(BF16)
            gt_ref[:, at] = rounded
            delta_ref[:, at] = jnp.sum(mixed * rounded.astype(F32), axis=0, keepdims=True)
            for expert in range(slot, slot + EXPERTS - TOPK + 1):
                here = slot_ref[pl.ds(expert, 1), tokens_of(tile)] == slot
                sums[pl.ds(expert, 1), tokens_of(tile)] += jnp.where(here, dots, 0.0)
    gates = gates_ref[...]
    dots = sums[...]
    grad_logits = gates * (dots - jnp.sum(gates * dots, axis=0, keepdims=True))
    gl_ref[...] = grad_logits
    high, low = split_two(grad_logits)
    small_ref[...] = jnp.concatenate(
        [
            nn(high, hid_ref[...]) + nn(low, hid_ref[...]),
            gain_grad_ref[...],
            jnp.zeros((7, D), F32),
        ],
        axis=0,
    )


def attend_back(
    qc_ref,
    gt_ref,
    lse_ref,
    delta_ref,
    kv_ref,
    after_ref,
    pair0,
    pair1,
    pair2,
    pair3,
    dqc,
    keys,
    values,
    kt,
    dkeys,
    dvalues,
    dq,
    scores,
    grads,
    shares,
    slopes,
):
    x = lax.axis_index("x")
    keys[...] = kv_ref[:, 0:HEAD]
    values[...] = kv_ref[:, HEAD : 2 * HEAD]
    for tile in range(TILES):
        kt[tile] = kv_ref[pl.ds(tile * TILE, TILE), 0:HEAD].astype(F32).T.astype(BF16)
    dkeys[...] = jnp.zeros_like(dkeys)
    dvalues[...] = jnp.zeros_like(dvalues)
    later = causal()
    for tile in range(2):
        last = own_blocks(x)[tile]
        dq[...] = jnp.zeros_like(dq)

        def step(index, masked):
            at = block(index, TILE)
            sums = {}

            def multiply(slot):
                here = pl.ds(slot * TILE, TILE)
                route = lanes_of(tile, slot)
                scores[:, here] = nn(keys[at, :], qc_ref[:, route])
                grads[:, here] = nn(values[at, :], gt_ref[:, route])

            def lift(slot):
                here = pl.ds(slot * TILE, TILE)
                route = lanes_of(tile, slot)
                value = jnp.exp2(scores[:, here] * SCORE2 - lse_ref[:, route])
                if masked:
                    value = jnp.where(later, value, 0.0)
                shares[:, here] = value.astype(BF16)
                slopes[:, here] = (value * (grads[:, here] - delta_ref[:, route])).astype(BF16)

            def gather(slot):
                here = pl.ds(slot * TILE, TILE)
                route = lanes_of(tile, slot)
                dq[:, here] += nn(kt[index], slopes[:, here])
                one = nt(qc_ref[:, route], slopes[:, here])
                two = nt(gt_ref[:, route], shares[:, here])
                if slot:
                    one, two = sums[0] + one, sums[1] + two
                sums[0], sums[1] = one, two

            staged(TOPK, multiply, lift, gather)
            dkeys[index] += sums[0]
            dvalues[index] += sums[1]

        step(last, True)

        @pl.loop(0, last)
        def _(index):
            step(index, False)

        dqc[:, pl.ds(tile * LANES, LANES)] = (dq[...] * SCORE).astype(BF16)

    def pair(low, high):
        return jnp.concatenate(
            [
                jnp.concatenate([dkeys[low], dkeys[high]], axis=1) * SCORE,
                jnp.concatenate([dvalues[low], dvalues[high]], axis=1),
            ],
            axis=0,
        ).astype(BF16)

    for away, ref in enumerate((pair0, pair1, pair2, pair3)):
        ref[...] = pair(*own_blocks(lax.rem(x + away, GROUPS)))


def query_part(
    dqc,
    slot_ref,
    hid_ref,
    small_ref,
    wr_ref,
    mine_ref,
    other_ref,
    dqall,
    gain_ref,
    keep_ref,
    send_ref,
):
    core = lax.axis_index("core")
    for tile in range(2):
        for expert in range(EXPERTS):
            dqall[pl.ds(expert * HEAD, HEAD), tokens_of(tile)] = expand(
                slot_ref, dqc, tile, expert
            ).astype(BF16)
    gain = jnp.sum(
        small_ref[0:EXPERTS] * wr_ref[...].astype(F32)[0:EXPERTS], axis=0, keepdims=True
    )
    for owner in range(GROUPS):
        grad = nn(dqall[pl.ds(owner * OWN, OWN), :], hid_ref[...])
        put_pieces(grad.astype(BF16), owner, core, keep_ref, send_ref)
        one, two = mine_ref[owner].astype(F32), other_ref[owner].astype(F32)
        first, last = jnp.where(core == 0, one, two), jnp.where(core == 0, two, one)
        gain = gain + jnp.sum(grad[0:HALF] * first, axis=0, keepdims=True)
        gain = gain + jnp.sum(grad[HALF:OWN] * last, axis=0, keepdims=True)
    gain_ref[...] = gain


def back_part(
    qc_ref,
    gt_ref,
    lse_ref,
    delta_ref,
    kv_ref,
    after_ref,
    slot_ref,
    hid_ref,
    small_ref,
    wr_ref,
    mine_ref,
    other_ref,
    pair0,
    pair1,
    pair2,
    pair3,
    dqall,
    gain_ref,
    keep_ref,
    send_ref,
    dqc,
    *scratch,
):
    attend_back(
        qc_ref,
        gt_ref,
        lse_ref,
        delta_ref,
        kv_ref,
        after_ref,
        pair0,
        pair1,
        pair2,
        pair3,
        dqc,
        *scratch,
    )
    query_part(
        dqc,
        slot_ref,
        hid_ref,
        small_ref,
        wr_ref,
        mine_ref,
        other_ref,
        dqall,
        gain_ref,
        keep_ref,
        send_ref,
    )


def finish(
    tok_ref,
    high_ref,
    gm_ref,
    dqall,
    gl_ref,
    wr_ref,
    mine_ref,
    other_ref,
    pairs_ref,
    wkv_ref,
    gain_ref,
    out_ref,
    out_high_ref,
):
    core = lax.axis_index("core")
    high, low = split_two(jnp.concatenate([gl_ref[...], jnp.zeros((8, TOK), F32)], axis=0))
    grad = tn(high, wr_ref[...]) + tn(low, wr_ref[...])
    for owner in range(GROUPS):
        grad = grad + tn(dqall[block(2 * owner + core, HALF), :], mine_ref[owner])
        grad = grad + tn(dqall[block(2 * owner + 1 - core, HALF), :], other_ref[owner])
    grad = grad + lax.dot_general(
        pairs_ref[...], wkv_ref[...], (((0,), (1,)), ((), ())), preferred_element_type=F32
    )
    rows = jnp.concatenate([tok_ref[0:TILE], high_ref[0:TILE]], axis=0).astype(F32)
    scale = scale_of(rows)
    unit = rows * scale
    inner = grad * gain_ref[...]
    result = (
        gm_ref[...] + scale * (inner - unit * jnp.mean(inner * unit, axis=-1, keepdims=True))
    ).astype(BF16)
    out_ref[...] = result
    out_high_ref[...] = result[TILE:TOK]


def added(near, one, two, three):
    return (
        (near.astype(F32) + two.astype(F32)) + (one.astype(F32) + three.astype(F32))
    ).astype(BF16)


def pair_feed(arrive, keep, arrived, keep_o, arrived_o, out_hbm, one, two, three, four, out, sems):
    arrive()
    parts = [pl.ds(16 * index, 16) for index in range(4)]
    loads = []
    for index, part in enumerate(parts):
        loads.append(
            [
                pltpu.make_async_copy(source.at[part], target.at[part], sems.at[index, place])
                for place, (source, target) in enumerate(
                    ((keep, one), (arrived, two), (keep_o, three), (arrived_o, four))
                )
            ]
        )
        for load in loads[-1]:
            load.start()
    stores = []
    for index, part in enumerate(parts):
        for load in loads[index]:
            load.wait()
        out[part, 0:128, :] = (one[part].astype(F32) + two[part].astype(F32)).astype(BF16)
        out[part, 128:176, :] = (three[part].astype(F32) + four[part].astype(F32)).astype(BF16)
        stores.append(pltpu.make_async_copy(out.at[part], out_hbm.at[part], sems.at[index, 4]))
        stores[-1].start()
    for store in stores:
        store.wait()


def merge(
    arrive,
    pieces_hbm,
    keep_hbm,
    arrived_hbm,
    near,
    one,
    two,
    three,
    hid_ref,
    small_ref,
    gain_rows,
    wkv_ref,
    gain_ref,
    out_hbm,
    part_ref,
    pair_ref,
    pieces,
    keep_q,
    arrived_q,
    feed,
    rest,
    sems,
):
    parts = [pl.ds(16 * index, 16) for index in range(4)]
    first = [
        pltpu.make_async_copy(keep_hbm, keep_q, sems.at[0]),
        pltpu.make_async_copy(arrived_hbm, arrived_q, sems.at[1]),
    ]
    loads = [
        pltpu.make_async_copy(pieces_hbm.at[part], pieces.at[part], sems.at[2 + index])
        for index, part in enumerate(parts)
    ]
    for load in first + loads:
        load.start()
    arrive()
    pair = added(near[...], one[...], two[...], three[...])
    pair_ref[...] = pair
    grad_kv = nn(pair, hid_ref[...])
    gain_grad = (
        gain_rows[...]
        + jnp.sum(grad_kv * wkv_ref[...].astype(F32).T, axis=0, keepdims=True)
    ) / gain_ref[...]
    last = jnp.concatenate([small_ref[0:25], gain_grad, small_ref[26:32]], axis=0)
    shared = jnp.concatenate([grad_kv, last], axis=0).astype(BF16)
    for piece in range(16):
        for place in range(3):
            row, group = divmod(3 * piece + place, 4)
            if 16 * row < SMALL:
                value = shared[16 * row : 16 * row + 16, 128 * group : 128 * group + 128]
            else:
                value = jnp.zeros((16, 128), BF16)
            for far in range(GROUPS):
                rest[16 * far + piece, 48 + 16 * place : 64 + 16 * place] = value
    for load in first:
        load.wait()
    rest[:, 0:48, :] = (keep_q[...].astype(F32) + arrived_q[...].astype(F32)).astype(BF16)
    stores = [pltpu.make_async_copy(rest, out_hbm.at[:, pl.ds(128, 96), :], sems.at[6])]
    stores[0].start()
    total = jnp.zeros((176, 128), F32)
    for index in range(4):
        loads[index].wait()
        for piece in range(16 * index, 16 * index + 16):
            total = total + pieces[piece].astype(F32)
    total = total.astype(BF16)
    part_ref[...] = total[128:176]
    for index in range(64):
        feed[index] = total[0:128]
    stores.append(pltpu.make_async_copy(feed, out_hbm.at[:, pl.ds(0, 128), :], sems.at[7]))
    stores[1].start()
    for store in stores:
        store.wait()


def collect(spread, part_ref, out_ref, rest, sems):
    load = pltpu.make_async_copy(spread.at[:, pl.ds(128, 96), :], rest, sems.at[0])
    load.start()
    load.wait()
    total = rest[0].astype(F32)
    for index in range(1, 64):
        total = total + rest[index].astype(F32)
    total = total.astype(BF16)
    for index in range(16):
        out_ref[index, 0:PIECE] = part_ref[...]
        out_ref[index, PIECE:EXTRA] = total


def unpack(at_ref, half_ref, *refs):
    up_ref, down_ref = refs[-2:]
    for group in range(2):
        up_ref[:, 128 * group : 128 * group + 128] = (
            half_ref[:, pl.ds(32 * group, 32), :].astype(F32).reshape(D, 128)
        )
    for group in range(4):
        down_ref[:, 128 * group : 128 * group + 128] = (
            half_ref[:, pl.ds(64 + 16 * group, 16), :].astype(F32).reshape(CHUNK, 128)
        )


def assemble(mine_ref, other_ref, output_ref, query_ref, kv_ref, router_ref, heads_ref, feed_ref, shared):
    core = lax.axis_index("core")
    for ref, half in ((mine_ref, core), (other_ref, 1 - core)):
        for column in range(4):
            for row in range(4):
                rows = pl.ds(pl.multiple_of(half * HALF + row * PIECE, 16), PIECE)
                for index, target in enumerate((output_ref, query_ref)):
                    target[rows, pl.ds(128 * column, 128)] = ref[
                        4 * column + row, pl.ds(PIECE * index, PIECE), :
                    ].astype(F32)
    for piece in range(14):
        for place in range(3):
            row, group = divmod(3 * piece + place, 4)
            if 16 * row < SMALL:
                at = pl.ds(2 * PIECE + 16 * place, 16)
                shared[16 * row : 16 * row + 16, 128 * group : 128 * group + 128] = mine_ref[
                    piece, at, :
                ].astype(F32) + other_ref[piece, at, :].astype(F32)
    kv_ref[...] = shared[0:128].T
    router_ref[...] = shared[128:152]
    feed_ref[...] = shared[152:153]
    heads_ref[...] = shared[153:154]


def shape(dims, dtype=BF16):
    return jax.ShapeDtypeStruct(dims, dtype)


VMEM = pl.BlockSpec(memory_space=pltpu.VMEM)
SMEM = pl.BlockSpec(memory_space=pltpu.SMEM)
HBM = pl.BlockSpec(memory_space=pltpu.HBM)
ANY = pl.BlockSpec(memory_space=pl.ANY)


def nothing(*refs):
    pass


def after(value, *others):
    return pl.pallas_call(
        nothing,
        out_shape=shape(value.shape, value.dtype),
        in_specs=[ANY] * (1 + len(others)),
        out_specs=ANY,
        input_output_aliases={0: 0},
        name="after",
    )(value, *others)


def size_of(value):
    return math.prod(value.shape) * jnp.dtype(value.dtype).itemsize


def call(kernel, micros, inputs, outputs, scratch=(), far=(), far_out=(), sent=(), own_loads=False, limit=None):
    near = [index for index in range(len(inputs)) if index not in far]
    count, ends = len(inputs), len(inputs) + len(outputs)

    def body(*refs):
        sources, results, own = list(refs[:count]), refs[count:ends], refs[ends:]
        buffers, sems = own[len(scratch) : -1], own[-1]
        loads = []
        for index, (source, buffer) in enumerate(zip(near, buffers)):
            loads.append(pltpu.make_async_copy(sources[source], buffer, sems.at[index]))
            sources[source] = buffer
        def arrive():
            for load in loads:
                load.wait()

        for load in loads:
            load.start()
        if own_loads:
            kernel(arrive, *sources, *results, *own[: len(scratch)])
        else:
            arrive()
            kernel(*sources, *results, *own[: len(scratch)])

    buffers = [pltpu.VMEM(inputs[index].shape, inputs[index].dtype) for index in near]
    limit = limit or LIMIT - sum(size_of(inputs[index]) for index in sent)
    return pl.pallas_call(
        body,
        out_shape=outputs,
        in_specs=[ANY if index in sent else HBM for index in range(count)],
        out_specs=tuple(HBM if index in far_out else VMEM for index in range(len(outputs))),
        scratch_shapes=[
            *scratch,
            *buffers,
            pltpu.SemaphoreType.DMA((len(near),)),
        ],
        compiler_params=pltpu.CompilerParams(vmem_limit_bytes=limit),
        cost_estimate=pl.CostEstimate(
            flops=int(micros * 1e9), bytes_accessed=(1 << 20) if micros else 0, transcendentals=0
        ),
        name=kernel.__name__,
    )(*inputs)


def turn(size, step):
    return [(index, (index + step) % size) for index in range(size)]


def swap(value):
    return lax.ppermute(value, "core", turn(2, 1))


def mirror(value):
    return lax.ppermute(value, "x", [(0, 3), (3, 0), (1, 2), (2, 1)])


def around(value, axis):
    return [lax.ppermute(value, axis, turn(4, step)) for step in (1, 2, 3)]


def vmem(dims, dtype=F32):
    return pltpu.VMEM(dims, dtype)


def shards(
    tokens,
    expert_ids,
    cotangent,
    gain_heads,
    key_value_weight,
    router_weight,
    query_weight,
    output_weight,
    gain_feed,
    up_weight,
    down_weight,
):
    x = lax.axis_index("x")
    core = lax.axis_index("core")
    chips = ("x", "y", "z")
    tok = tokens[0]
    cot = cotangent[0]
    ids = expert_ids[0].T
    wq = jnp.swapaxes(query_weight, 1, 2).reshape(OWN, D)
    wr = jnp.pad(router_weight.T, ((0, 8), (0, 0)))
    wkv = key_value_weight
    gain1 = gain_heads.reshape(1, D)
    gain2 = gain_feed.reshape(1, D)

    carried = jnp.concatenate(
        [
            tok[TILE:TOK],
            jnp.pad(ids[:, TILE:TOK].astype(BF16), ((0, 8), (0, D - TILE))),
        ],
        axis=0,
    )
    carried = mirror(carried)
    mine = lax.dynamic_slice(wq, (core * HALF, 0), (HALF, D))
    mine = lax.all_to_all(
        jnp.broadcast_to(mine[None], (GROUPS, HALF, D)), "x", split_axis=0, concat_axis=0, tiled=True
    )
    first, kv = call(
        pairs_first,
        2,
        (tok, gain1, wkv),
        (shape((TILE, D)), shape((TOK, 2 * HEAD))),
    )
    kvs = [kv] + around(kv, "x")
    wo_copies = jnp.broadcast_to(output_weight.reshape(1, OWN, D), (GROUPS, OWN, D))
    cot_high, hidden, turned, gates, slots = call(
        prepare,
        3,
        (first, carried, ids, gain1, wr, cot, *kvs[1:], wo_copies),
        (
            shape((TILE, D)),
            shape((TOK, D)),
            shape((D, TOK)),
            shape((EXPERTS, TOK), F32),
            shape((EXPERTS, TOK), jnp.int32),
        ),
        far=(6, 7, 8, 9),
        sent=(1, 6, 7, 8),
    )
    mine = after(mine, slots)
    wqs = (mine, swap(mine))
    wo = after(wo_copies, wqs[1])
    wo = lax.all_to_all(wo, "x", split_axis=0, concat_axis=0, tiled=True)
    wo = wo.reshape(EXPERTS * HEAD, D)
    cot_high = mirror(cot_high)

    qc, mixed, lse, kv_all, dense = call(
        attend,
        14,
        (turned, slots, gates, *wqs, *kvs),
        (
            shape((HEAD, ROUTES)),
            shape((HEAD, ROUTES)),
            shape((1, ROUTES), F32),
            shape((LENGTH, 2 * HEAD)),
            shape((EXPERTS * HEAD, TOK)),
        ),
        [
            vmem((EXPERTS * HEAD, TOK)),
            vmem((LENGTH, HEAD), BF16),
            vmem((GROUPS, HEAD + 16, 2 * TILE), BF16),
            vmem((1, LANES)),
            vmem((HEAD + 16, LANES)),
            vmem((2 * TILE, LANES)),
            vmem((2 * TILE, LANES), BF16),
            vmem((GROUPS, HALF, D), BF16),
            vmem((GROUPS, HALF, D), BF16),
            pltpu.SemaphoreType.DMA((2,)),
        ],
        far=(3, 4),
        own_loads=True,
        sent=(3, 4, 6, 7, 8),
    )

    result, out_high, middle, back, keep, send = call(
        feed_part,
        17,
        (tok, carried, cot, cot_high, dense, gain2, wo, up_weight, down_weight),
        (
            shape((TOK, D)),
            shape((TILE, D)),
            shape((TOK, D), F32),
            shape((TOK, D), F32),
            shape((64, 128, 128)),
            shape((64, 128, 128)),
        ),
        [
            vmem((TOK, D), BF16),
            vmem((D, TOK), BF16),
            vmem((TOK, D), BF16),
            vmem((TOK, D)),
            vmem((EXPERTS * HEAD, D), BF16),
            vmem((D, FF), BF16),
            vmem((FF, D), BF16),
            vmem((8, 16, 128, 128), BF16),
            pltpu.SemaphoreType.DMA((3,)),
            pltpu.SemaphoreType.DMA((8,)),
        ],
        far=(6, 7, 8),
        far_out=(4, 5),
        sent=(3, 6),
        own_loads=True,
    )
    arrived = swap(send)
    out_back = mirror(out_high)

    grad_middle, turned_gm, gain_grad, keep_o, send_o = call(
        norm_part,
        4,
        (cot, cot_high, middle, back, dense, gain2),
        (
            shape((TOK, D), F32),
            shape((D, TOK)),
            shape((1, D), F32),
            shape((64, PIECE, 128)),
            shape((64, PIECE, 128)),
        ),
        [vmem((TOK, D), BF16)],
        sent=(1,),
    )
    arrived_o = swap(send_o)
    (paired,) = call(
        pair_feed,
        4,
        (keep, arrived, keep_o, arrived_o),
        (shape((64, 176, 128)),),
        [
            vmem((64, 128, 128), BF16),
            vmem((64, 128, 128), BF16),
            vmem((64, PIECE, 128), BF16),
            vmem((64, PIECE, 128), BF16),
            vmem((64, 176, 128), BF16),
            pltpu.SemaphoreType.DMA((4, 5)),
        ],
        far=(0, 1, 2, 3),
        far_out=(0,),
        sent=(1, 3),
        own_loads=True,
    )
    gt, delta, grad_logits, small = call(
        route_part,
        6,
        (turned_gm, mixed, slots, gates, hidden, wo, gain_grad, paired),
        (
            shape((HEAD, ROUTES)),
            shape((1, ROUTES), F32),
            shape((EXPERTS, TOK), F32),
            shape((32, D), F32),
        ),
        [vmem((EXPERTS * HEAD, TOK)), vmem((EXPERTS, TOK))],
        far=(7,),
        sent=(5,),
    )
    pieces = lax.all_to_all(paired, chips, split_axis=0, concat_axis=0, tiled=True)

    pair, *others, dqall, gain_rows, keep_q, send_q = call(
        back_part,
        20,
        (qc, gt, lse, delta, kv_all, out_back, slots, hidden, small, wr, *wqs),
        (
            *[shape((2 * HEAD, TOK))] * GROUPS,
            shape((EXPERTS * HEAD, TOK)),
            shape((1, D), F32),
            shape((64, PIECE, 128)),
            shape((64, PIECE, 128)),
        ),
        [
            vmem((HEAD, ROUTES), BF16),
            vmem((LENGTH, HEAD), BF16),
            vmem((LENGTH, HEAD), BF16),
            vmem((TILES, HEAD, TILE), BF16),
            vmem((TILES, HEAD, TILE)),
            vmem((TILES, HEAD, TILE)),
            vmem((HEAD, LANES)),
            vmem((TILE, LANES)),
            vmem((TILE, LANES)),
            vmem((TILE, LANES), BF16),
            vmem((TILE, LANES), BF16),
        ],
        far=(5,),
        sent=(5, 10, 11),
    )
    arrived_pairs = [
        lax.ppermute(value, "x", turn(4, step + 1)) for step, value in enumerate(others)
    ]
    arrived_q = swap(send_q)
    merged, part, pair_sum = call(
        merge,
        5,
        (
            pieces,
            keep_q,
            arrived_q,
            pair,
            *arrived_pairs,
            hidden,
            small,
            gain_rows,
            wkv,
            gain1,
        ),
        (shape((64, 224, 128)), shape((PIECE, 128)), shape((2 * HEAD, TOK))),
        [
            vmem((64, 176, 128), BF16),
            vmem((64, PIECE, 128), BF16),
            vmem((64, PIECE, 128), BF16),
            vmem((64, 128, 128), BF16),
            vmem((64, 96, 128), BF16),
            pltpu.SemaphoreType.DMA((8,)),
        ],
        far=(0, 1, 2),
        far_out=(0,),
        own_loads=True,
        sent=(0, 2, 4, 5, 6),
    )
    grad_whole, grad_high = call(
        finish,
        3,
        (tok, carried, grad_middle, dqall, grad_logits, wr, *wqs, pair_sum, wkv, gain1),
        (shape((TOK, D)), shape((TILE, D))),
    )
    spread = lax.all_to_all(merged, chips, split_axis=0, concat_axis=0, tiled=True)
    result = lax.dynamic_update_slice(result, out_back, (TILE, 0))
    grad_back = mirror(grad_high)
    spread = after(spread, grad_back, result)
    grad_tokens = lax.dynamic_update_slice(grad_whole, grad_back, (TILE, 0))
    (part,) = call(
        collect,
        0,
        (spread, part),
        (shape((16, EXTRA, 128)),),
        [vmem((64, 96, 128), BF16), pltpu.SemaphoreType.DMA((1,))],
        far=(0,),
        sent=(0,),
    )
    feed_other = swap(spread)
    part = lax.all_to_all(part, ("y", "z"), split_axis=0, concat_axis=0, tiled=True)

    def unpacked(value, half, *earlier, extra=()):
        half_spec = pl.BlockSpec((16, 128, 128), lambda index, at: (index, 0, 0))
        return pl.pallas_call(
            unpack,
            grid_spec=pltpu.PrefetchScalarGridSpec(
                num_scalar_prefetch=1,
                grid=(4,),
                in_specs=[half_spec] + [HBM] * len(earlier) + [ANY] * len(extra),
                out_specs=(
                    pl.BlockSpec((D, CHUNK), lambda index, at: (0, 4 * at[0] + index)),
                    pl.BlockSpec((CHUNK, D), lambda index, at: (4 * at[0] + index, 0)),
                ),
            ),
            out_shape=(shape((D, FF), F32), shape((FF, D), F32)),
            input_output_aliases={2: 0, 3: 1} if earlier else {},
            compiler_params=pltpu.CompilerParams(vmem_limit_bytes=LIMIT - 2 * MIB),
            name="unpack",
        )(half.reshape(1), value, *earlier, *extra)

    grads = unpacked(spread, core)
    grad_up, grad_down = unpacked(feed_other, 1 - core, *grads)
    part = after(part, grad_up)
    part_other = swap(part)
    output_grad, query_grad, kv_grad, router_grad, gain_heads_grad, gain_feed_grad = call(
        assemble,
        4,
        (part, part_other),
        (
            shape((OWN, D), F32),
            shape((OWN, D), F32),
            shape((D, 2 * HEAD), F32),
            shape((EXPERTS, D), F32),
            shape((1, D), F32),
            shape((1, D), F32),
        ),
        [vmem((SMALL, D))],
        sent=(0, 1),
        limit=20 * MIB,
    )
    return (
        result[None],
        grad_tokens[None],
        gain_heads_grad.reshape(D),
        kv_grad,
        router_grad.T,
        query_grad.reshape(OWN // HEAD, HEAD, D).swapaxes(1, 2),
        output_grad.reshape(OWN // HEAD, HEAD, D),
        gain_feed_grad.reshape(D),
        grad_up,
        grad_down,
    )


def solution(mesh):
    grid = Mesh(mesh.devices.reshape(4, 4, 4, 2), ("x", "y", "z", "core"))
    dp = ("y", "z", "core")
    return jax.shard_map(
        shards,
        mesh=grid,
        in_specs=(
            P(dp, "x", None),
            P(dp, "x", None),
            P(dp, "x", None),
            P(),
            P(),
            P(),
            P("x", None, None),
            P("x", None, None),
            P(),
            P(),
            P(),
        ),
        out_specs=(
            P(dp, "x", None),
            P(dp, "x", None),
            P(),
            P(),
            P(),
            P("x", None, None),
            P("x", None, None),
            P(),
            P(),
            P(),
        ),
        check_vma=False,
    )
```

```python
import math

import jax
import jax.numpy as jnp
from jax import lax
from jax.experimental import pallas as pl
from jax.experimental.pallas import tpu as pltpu
from jax.sharding import Mesh, PartitionSpec as P

D = 512
HEAD = 64
EXPERTS = 24
TOPK = 8
FF = 2048
TOK = 512
GROUPS = 4
LENGTH = TOK * GROUPS
OWN = EXPERTS // GROUPS * HEAD
HALF = OWN // 2
TILE = 256
LANES = TOPK * TILE
TILES = LENGTH // TILE
ROUTES = TOK * TOPK
CHUNK = 256
SMALL = 160
PIECE = 48
EXTRA = 3 * PIECE

EPSILON = 1e-06
CURVE_SCALE = 0.7978845608028654
CURVE_CUBIC = 0.044715
SCORE = HEAD**-0.5
SCORE2 = SCORE * 1.4426950408889634
LOW = -1e30

F32 = jnp.float32
BF16 = jnp.bfloat16
MIB = 1 << 20
LIMIT = 62 * MIB - (1 << 18)


def nn(a, b):
    return lax.dot_general(a, b, (((1,), (0,)), ((), ())), preferred_element_type=F32)


def nt(a, b):
    return lax.dot_general(a, b, (((1,), (1,)), ((), ())), preferred_element_type=F32)


def tn(a, b):
    return lax.dot_general(a, b, (((0,), (0,)), ((), ())), preferred_element_type=F32)


def split_two(value):
    high = value.astype(BF16)
    return high, (value - high.astype(F32)).astype(BF16)


def scale_of(rows):
    return lax.rsqrt(jnp.mean(rows * rows, axis=-1, keepdims=True) + EPSILON)


def lanes_of(tile, slot):
    return pl.ds(tile * LANES + slot * TILE, TILE)


def tokens_of(tile):
    return pl.ds(tile * TILE, TILE)


def block(index, size):
    return pl.ds(pl.multiple_of(index * size, size), size)


def slots_of(expert):
    return range(max(0, expert - (EXPERTS - TOPK)), min(TOPK - 1, expert) + 1)


def pairs_first(tok_ref, gain_ref, wkv_ref, first_ref, kv_ref):
    rows = tok_ref[...].astype(F32)
    first = (rows * scale_of(rows) * gain_ref[...]).astype(BF16)
    first_ref[...] = first[0:TILE]
    kv_ref[...] = nn(first, wkv_ref[...]).astype(BF16)


def prepare(
    first_ref,
    carried_ref,
    ids_ref,
    gain_ref,
    wr_ref,
    cot_ref,
    after1,
    after2,
    after3,
    after4,
    cot_high_ref,
    hid_ref,
    turned_ref,
    gates_ref,
    slot_ref,
):
    cot_high_ref[...] = cot_ref[TILE:TOK]
    rows = carried_ref[0:TILE].astype(F32)
    high = rows * scale_of(rows) * gain_ref[...]
    turned_ref[:, 0:TILE] = first_ref[...].astype(F32).T.astype(BF16)
    turned_ref[:, TILE:TOK] = high.T.astype(BF16)
    hidden = jnp.concatenate([first_ref[...], high.astype(BF16)], axis=0)
    hid_ref[...] = hidden
    logits = nt(wr_ref[...], hidden)[0:EXPERTS]
    ids = jnp.concatenate(
        [ids_ref[:, 0:TILE], carried_ref[TILE : TILE + 16, 0:TILE].astype(F32)[0:TOPK].astype(jnp.int32)], axis=1
    )
    names = lax.broadcasted_iota(jnp.int32, (EXPERTS, TOK), 0)
    chosen = names == ids[0:1]
    for route in range(1, TOPK):
        chosen = chosen | (names == ids[route : route + 1])
    count = jnp.where(chosen, 1.0, 0.0)
    below = lax.broadcasted_iota(jnp.int32, (EXPERTS, EXPERTS), 0) > lax.broadcasted_iota(
        jnp.int32, (EXPERTS, EXPERTS), 1
    )
    rank = nn(jnp.where(below, 1.0, 0.0).astype(BF16), count.astype(BF16))
    slot_ref[...] = jnp.where(chosen, rank, -1.0).astype(jnp.int32)
    peak = jnp.max(jnp.where(chosen, logits, -3e38), axis=0, keepdims=True)
    raised = jnp.where(chosen, jnp.exp(logits - peak), 0.0)
    gates_ref[...] = raised / jnp.sum(raised, axis=0, keepdims=True)


def compact(slot_ref, dense_ref, tile, slot):
    value = jnp.zeros((HEAD, TILE), F32)
    for expert in range(slot, slot + EXPERTS - TOPK + 1):
        here = slot_ref[pl.ds(expert, 1), tokens_of(tile)] == slot
        value = jnp.where(here, dense_ref[pl.ds(expert * HEAD, HEAD), tokens_of(tile)], value)
    return value


def expand(slot_ref, packed_ref, tile, expert):
    row = slot_ref[pl.ds(expert, 1), tokens_of(tile)]
    value = jnp.zeros((HEAD, TILE), F32)
    for slot in slots_of(expert):
        value = jnp.where(row == slot, packed_ref[:, lanes_of(tile, slot)].astype(F32), value)
    return value


def causal():
    return lax.broadcasted_iota(jnp.int32, (TILE, TILE), 0) <= lax.broadcasted_iota(
        jnp.int32, (TILE, TILE), 1
    )


def staged(count, *stages):
    for time in range(count + len(stages) - 1):
        for late, stage in enumerate(stages):
            if 0 <= time - late < count:
                stage(time - late)


def own_blocks(x):
    return 2 * x, 7 - 2 * x


def attend(
    arrive,
    turned_ref,
    slot_ref,
    gates_ref,
    mine_hbm,
    other_hbm,
    kv0,
    kv1,
    kv2,
    kv3,
    qc_ref,
    mixed_ref,
    lse_ref,
    kv_ref,
    dense_ref,
    qall,
    keys,
    vt,
    peak,
    acc,
    scores,
    shares,
    mine_ref,
    other_ref,
    sems,
):
    loads = (
        pltpu.make_async_copy(mine_hbm, mine_ref, sems.at[0]),
        pltpu.make_async_copy(other_hbm, other_ref, sems.at[1]),
    )
    for load in loads:
        load.start()
    arrive()
    x = lax.axis_index("x")
    core = lax.axis_index("core")
    owners = [lax.rem(x + GROUPS - away, GROUPS) for away in range(GROUPS)]
    for owner, kv in zip(owners, (kv0, kv1, kv2, kv3)):
        turned = kv[:, HEAD : 2 * HEAD].astype(F32).T.astype(BF16)
        kv_ref[block(owner, TOK), :] = kv[...]
        keys[block(owner, TOK), :] = kv[:, 0:HEAD]
        vt[owner, 0:HEAD, :] = turned
        vt[owner, HEAD : HEAD + 16, :] = jnp.ones((16, 2 * TILE), BF16)
    for load in loads:
        load.wait()
    for owner in range(GROUPS):
        qall[block(2 * owner + core, HALF), :] = nn(mine_ref[owner], turned_ref[...])
        qall[block(2 * owner + 1 - core, HALF), :] = nn(other_ref[owner], turned_ref[...])
    for tile in range(2):
        for slot in range(TOPK):
            qc_ref[:, lanes_of(tile, slot)] = compact(slot_ref, qall, tile, slot).astype(BF16)

    wide = 2 * TILE
    later = lax.broadcasted_iota(jnp.int32, (TILE, wide), 0) <= (
        lax.broadcasted_iota(jnp.int32, (TILE, wide), 1) & (TILE - 1)
    )
    later_two = lax.broadcasted_iota(jnp.int32, (wide, wide), 0) <= TILE + (
        lax.broadcasted_iota(jnp.int32, (wide, wide), 1) & (TILE - 1)
    )

    def step(tile, start, size, values, mask):
        fades = {}

        def multiply(unit):
            at = pl.ds(unit * wide, wide)
            route = pl.ds(tile * LANES + unit * wide, wide)
            scores[0:size, at] = nn(keys[pl.ds(start, size), :], qc_ref[:, route])

        def lift(unit):
            at = pl.ds(unit * wide, wide)
            value = scores[0:size, at]
            if mask is not None:
                value = jnp.where(mask, value, LOW)
            top = jnp.max(value, axis=0, keepdims=True)
            if mask is None:
                before = peak[:, at]
                top = jnp.maximum(before, top)
                fades[unit] = jnp.exp2((before - top) * SCORE2)
            shares[0:size, at] = jnp.exp2((value - top) * SCORE2).astype(BF16)
            peak[:, at] = top

        def gather(unit):
            at = pl.ds(unit * wide, wide)
            part = nn(values, shares[0:size, at])
            if mask is None:
                part = acc[:, at] * fades[unit] + part
            acc[:, at] = part

        staged(LANES // wide, multiply, lift, gather)

    for tile in range(2):
        if tile == 0:
            start = pl.multiple_of(2 * x * TILE, TILE)
            step(tile, start, TILE, vt[x, :, 0:TILE], later)
            count = x
        else:
            start = pl.multiple_of((3 - x) * wide, wide)
            step(tile, start, wide, vt[3 - x], later_two)
            count = 3 - x

        @pl.loop(0, count)
        def _(index):
            step(tile, pl.multiple_of(index * wide, wide), wide, vt[index], None)

        here = pl.ds(tile * LANES, LANES)
        total = acc[HEAD : HEAD + 1, :]
        mixed_ref[:, here] = (acc[0:HEAD, :] / total).astype(BF16)
        lse_ref[:, here] = peak[...] * SCORE2 + jnp.log2(total)
    for tile in range(2):
        for expert in range(EXPERTS):
            value = expand(slot_ref, mixed_ref, tile, expert)
            gate = gates_ref[pl.ds(expert, 1), tokens_of(tile)]
            dense_ref[pl.ds(expert * HEAD, HEAD), tokens_of(tile)] = (value * gate).astype(BF16)


def feed_part(
    arrive,
    tok_ref,
    high_ref,
    cot_ref,
    cot_high_ref,
    dense_ref,
    gain_ref,
    wo_hbm,
    up_hbm,
    down_hbm,
    out_ref,
    out_high_ref,
    middle_ref,
    back_ref,
    keep_hbm,
    send_hbm,
    feed,
    feed_t,
    cot,
    result,
    wo_ref,
    up_ref,
    down_ref,
    staging,
    sems,
    out_sems,
):
    core = lax.axis_index("core")
    sources = ((wo_hbm, wo_ref), (up_hbm, up_ref), (down_hbm, down_ref))
    loads = [
        pltpu.make_async_copy(source, target, sems.at[index])
        for index, (source, target) in enumerate(sources)
    ]
    for load in loads:
        load.start()
    arrive()
    cot[0:TILE] = cot_ref[0:TILE]
    cot[TILE:TOK] = cot_high_ref[...]
    total = jnp.concatenate([tok_ref[0:TILE], high_ref[0:TILE]], axis=0).astype(F32)
    loads[0].wait()
    total = total + tn(dense_ref[...], wo_ref[...])
    middle_ref[...] = total
    feed32 = total * scale_of(total) * gain_ref[...]
    feed[...] = feed32.astype(BF16)
    feed_t[...] = feed32.T.astype(BF16)
    result[...] = total
    back_ref[...] = jnp.zeros_like(back_ref)
    loads[1].wait()
    loads[2].wait()

    def out_copy(index, target):
        return pltpu.make_async_copy(
            staging.at[index],
            target.at[pl.ds(pl.multiple_of(lax.rem(index, 4) * 16, 16), 16)],
            out_sems.at[index],
        )

    @pl.loop(0, FF // CHUNK // 4)
    def _(turn_index):
        held = {}

        def multiply(unit):
            index = 4 * turn_index + unit
            up = up_ref[:, block(index, CHUNK)]
            down = down_ref[block(index, CHUNK), :]
            held[unit] = (up, down, nn(feed[...], up), nt(cot[...], down))

        def lift(unit):
            up, down, before, grad_active = held[unit]
            square = before * before
            curve = jnp.tanh(CURVE_SCALE * before * (1.0 + CURVE_CUBIC * square))
            rise = 0.5 * (1.0 + curve)
            slope = rise + 0.5 * before * (1.0 - curve * curve) * (
                CURVE_SCALE * (1.0 + 3.0 * CURVE_CUBIC * square)
            )
            active = (before * rise).astype(BF16)
            held[unit] = (up, down, active, (grad_active * slope).astype(BF16))

        def gather(unit):
            index = 4 * turn_index + unit
            up, down, active, grad_before = held[unit]
            result[...] += nn(active, down)
            back_ref[...] += nt(grad_before, up)
            grad_up = nn(feed_t[...], grad_before).astype(BF16).reshape(16, 32, CHUNK)
            grad_down = tn(active, cot[...]).astype(BF16).reshape(16, 16, D)
            for group in range(2):
                staging[index, :, pl.ds(32 * group, 32), :] = grad_up[
                    :, :, 128 * group : 128 * group + 128
                ]
            for group in range(4):
                staging[index, :, pl.ds(64 + 16 * group, 16), :] = grad_down[
                    :, :, 128 * group : 128 * group + 128
                ]

        staged(4, multiply, lift, gather)
        mine = turn_index == core

        @pl.when(mine)
        def _():
            for unit in range(4):
                out_copy(4 * turn_index + unit, keep_hbm).start()

        @pl.when(jnp.logical_not(mine))
        def _():
            for unit in range(4):
                out_copy(4 * turn_index + unit, send_hbm).start()

    out_ref[...] = result[...].astype(BF16)
    out_high_ref[...] = result[TILE:TOK].astype(BF16)
    for index in range(FF // CHUNK):
        out_copy(index, keep_hbm).wait()


def put_pieces(grad, owner, core, keep_ref, send_ref):
    def put(ref, half):
        part = grad[half * HALF : (half + 1) * HALF].reshape(4, PIECE, D)
        for group in range(4):
            ref[pl.ds(owner * 16 + 4 * group, 4), :, :] = part[
                :, :, 128 * group : 128 * group + 128
            ]

    @pl.when(core == 0)
    def _():
        put(keep_ref, 0)
        put(send_ref, 1)

    @pl.when(core == 1)
    def _():
        put(keep_ref, 1)
        put(send_ref, 0)


def norm_part(
    cot_ref,
    cot_high_ref,
    middle_ref,
    back_ref,
    dense_ref,
    gain_ref,
    gm_ref,
    turned_ref,
    gain_grad_ref,
    keep_ref,
    send_ref,
    gm16,
):
    core = lax.axis_index("core")
    total = middle_ref[...]
    scale = scale_of(total)
    unit = total * scale
    grad = back_ref[...]
    inner = grad * gain_ref[...]
    gain_grad_ref[...] = jnp.sum(grad * unit, axis=0, keepdims=True)
    cot = jnp.concatenate([cot_ref[0:TILE], cot_high_ref[...]], axis=0).astype(F32)
    grad_middle = cot + scale * (inner - unit * jnp.mean(inner * unit, axis=-1, keepdims=True))
    gm_ref[...] = grad_middle
    gm16[...] = grad_middle.astype(BF16)
    turned_ref[...] = grad_middle.T.astype(BF16)
    for owner in range(GROUPS):
        grad_out = nn(dense_ref[pl.ds(owner * OWN, OWN), :], gm16[...]).astype(BF16)
        put_pieces(grad_out, owner, core, keep_ref, send_ref)


def route_part(
    turned_ref,
    mixed_ref,
    slot_ref,
    gates_ref,
    hid_ref,
    wo_ref,
    gain_grad_ref,
    after_ref,
    gt_ref,
    delta_ref,
    gl_ref,
    small_ref,
    gdense,
    sums,
):
    gdense[...] = nn(wo_ref[...], turned_ref[...])
    sums[...] = jnp.zeros_like(sums)
    for tile in range(2):
        for slot in range(TOPK):
            at = lanes_of(tile, slot)
            value = jnp.zeros((HEAD, TILE), F32)
            gate = jnp.zeros((1, TILE), F32)
            for expert in range(slot, slot + EXPERTS - TOPK + 1):
                here = slot_ref[pl.ds(expert, 1), tokens_of(tile)] == slot
                value = jnp.where(
                    here, gdense[pl.ds(expert * HEAD, HEAD), tokens_of(tile)], value
                )
                gate = jnp.where(here, gates_ref[pl.ds(expert, 1), tokens_of(tile)], gate)
            mixed = mixed_ref[:, at].astype(F32)
            dots = jnp.sum(mixed * value, axis=0, keepdims=True)
            rounded = (value * gate).astype(BF16)
            gt_ref[:, at] = rounded
            delta_ref[:, at] = jnp.sum(mixed * rounded.astype(F32), axis=0, keepdims=True)
            for expert in range(slot, slot + EXPERTS - TOPK + 1):
                here = slot_ref[pl.ds(expert, 1), tokens_of(tile)] == slot
                sums[pl.ds(expert, 1), tokens_of(tile)] += jnp.where(here, dots, 0.0)
    gates = gates_ref[...]
    dots = sums[...]
    grad_logits = gates * (dots - jnp.sum(gates * dots, axis=0, keepdims=True))
    gl_ref[...] = grad_logits
    high, low = split_two(grad_logits)
    small_ref[...] = jnp.concatenate(
        [
            nn(high, hid_ref[...]) + nn(low, hid_ref[...]),
            gain_grad_ref[...],
            jnp.zeros((7, D), F32),
        ],
        axis=0,
    )


def attend_back(
    qc_ref,
    gt_ref,
    lse_ref,
    delta_ref,
    kv_ref,
    after_ref,
    pair0,
    pair1,
    pair2,
    pair3,
    dqc,
    keys,
    values,
    kt,
    dkeys,
    dvalues,
    dq,
    scores,
    grads,
    shares,
    slopes,
):
    x = lax.axis_index("x")
    keys[...] = kv_ref[:, 0:HEAD]
    values[...] = kv_ref[:, HEAD : 2 * HEAD]
    for tile in range(TILES):
        kt[tile] = kv_ref[pl.ds(tile * TILE, TILE), 0:HEAD].astype(F32).T.astype(BF16)
    dkeys[...] = jnp.zeros_like(dkeys)
    dvalues[...] = jnp.zeros_like(dvalues)
    later = causal()
    for tile in range(2):
        last = own_blocks(x)[tile]
        dq[...] = jnp.zeros_like(dq)

        def step(index, masked):
            at = block(index, TILE)
            sums = {}

            def multiply(slot):
                here = pl.ds(slot * TILE, TILE)
                route = lanes_of(tile, slot)
                scores[:, here] = nn(keys[at, :], qc_ref[:, route])
                grads[:, here] = nn(values[at, :], gt_ref[:, route])

            def lift(slot):
                here = pl.ds(slot * TILE, TILE)
                route = lanes_of(tile, slot)
                value = jnp.exp2(scores[:, here] * SCORE2 - lse_ref[:, route])
                if masked:
                    value = jnp.where(later, value, 0.0)
                shares[:, here] = value.astype(BF16)
                slopes[:, here] = (value * (grads[:, here] - delta_ref[:, route])).astype(BF16)

            def gather(slot):
                here = pl.ds(slot * TILE, TILE)
                route = lanes_of(tile, slot)
                dq[:, here] += nn(kt[index], slopes[:, here])
                one = nt(qc_ref[:, route], slopes[:, here])
                two = nt(gt_ref[:, route], shares[:, here])
                if slot:
                    one, two = sums[0] + one, sums[1] + two
                sums[0], sums[1] = one, two

            staged(TOPK, multiply, lift, gather)
            dkeys[index] += sums[0]
            dvalues[index] += sums[1]

        step(last, True)

        @pl.loop(0, last)
        def _(index):
            step(index, False)

        dqc[:, pl.ds(tile * LANES, LANES)] = (dq[...] * SCORE).astype(BF16)

    def pair(low, high):
        return jnp.concatenate(
            [
                jnp.concatenate([dkeys[low], dkeys[high]], axis=1) * SCORE,
                jnp.concatenate([dvalues[low], dvalues[high]], axis=1),
            ],
            axis=0,
        ).astype(BF16)

    for away, ref in enumerate((pair0, pair1, pair2, pair3)):
        ref[...] = pair(*own_blocks(lax.rem(x + away, GROUPS)))


def query_part(
    dqc,
    slot_ref,
    hid_ref,
    small_ref,
    wr_ref,
    mine_ref,
    other_ref,
    dqall,
    gain_ref,
    keep_ref,
    send_ref,
):
    core = lax.axis_index("core")
    for tile in range(2):
        for expert in range(EXPERTS):
            dqall[pl.ds(expert * HEAD, HEAD), tokens_of(tile)] = expand(
                slot_ref, dqc, tile, expert
            ).astype(BF16)
    gain = jnp.sum(
        small_ref[0:EXPERTS] * wr_ref[...].astype(F32)[0:EXPERTS], axis=0, keepdims=True
    )
    for owner in range(GROUPS):
        grad = nn(dqall[pl.ds(owner * OWN, OWN), :], hid_ref[...])
        put_pieces(grad.astype(BF16), owner, core, keep_ref, send_ref)
        one, two = mine_ref[owner].astype(F32), other_ref[owner].astype(F32)
        first, last = jnp.where(core == 0, one, two), jnp.where(core == 0, two, one)
        gain = gain + jnp.sum(grad[0:HALF] * first, axis=0, keepdims=True)
        gain = gain + jnp.sum(grad[HALF:OWN] * last, axis=0, keepdims=True)
    gain_ref[...] = gain


def back_part(
    qc_ref,
    gt_ref,
    lse_ref,
    delta_ref,
    kv_ref,
    after_ref,
    slot_ref,
    hid_ref,
    small_ref,
    wr_ref,
    mine_ref,
    other_ref,
    pair0,
    pair1,
    pair2,
    pair3,
    dqall,
    gain_ref,
    keep_ref,
    send_ref,
    dqc,
    *scratch,
):
    attend_back(
        qc_ref,
        gt_ref,
        lse_ref,
        delta_ref,
        kv_ref,
        after_ref,
        pair0,
        pair1,
        pair2,
        pair3,
        dqc,
        *scratch,
    )
    query_part(
        dqc,
        slot_ref,
        hid_ref,
        small_ref,
        wr_ref,
        mine_ref,
        other_ref,
        dqall,
        gain_ref,
        keep_ref,
        send_ref,
    )


def finish(
    tok_ref,
    high_ref,
    gm_ref,
    dqall,
    gl_ref,
    wr_ref,
    mine_ref,
    other_ref,
    pairs_ref,
    wkv_ref,
    gain_ref,
    out_ref,
    out_high_ref,
):
    core = lax.axis_index("core")
    high, low = split_two(jnp.concatenate([gl_ref[...], jnp.zeros((8, TOK), F32)], axis=0))
    grad = tn(high, wr_ref[...]) + tn(low, wr_ref[...])
    for owner in range(GROUPS):
        grad = grad + tn(dqall[block(2 * owner + core, HALF), :], mine_ref[owner])
        grad = grad + tn(dqall[block(2 * owner + 1 - core, HALF), :], other_ref[owner])
    grad = grad + lax.dot_general(
        pairs_ref[...], wkv_ref[...], (((0,), (1,)), ((), ())), preferred_element_type=F32
    )
    rows = jnp.concatenate([tok_ref[0:TILE], high_ref[0:TILE]], axis=0).astype(F32)
    scale = scale_of(rows)
    unit = rows * scale
    inner = grad * gain_ref[...]
    result = (
        gm_ref[...] + scale * (inner - unit * jnp.mean(inner * unit, axis=-1, keepdims=True))
    ).astype(BF16)
    out_ref[...] = result
    out_high_ref[...] = result[TILE:TOK]


def added(near, one, two, three):
    return (
        (near.astype(F32) + two.astype(F32)) + (one.astype(F32) + three.astype(F32))
    ).astype(BF16)


def pair_feed(arrive, keep, arrived, keep_o, arrived_o, out_hbm, one, two, three, four, out, sems):
    arrive()
    parts = [pl.ds(8 * index, 8) for index in range(8)]
    loads = []
    for index, part in enumerate(parts):
        loads.append(
            [
                pltpu.make_async_copy(source.at[part], target.at[part], sems.at[index, place])
                for place, (source, target) in enumerate(
                    ((keep, one), (arrived, two), (keep_o, three), (arrived_o, four))
                )
            ]
        )
        for load in loads[-1]:
            load.start()
    stores = []
    for index, part in enumerate(parts):
        for load in loads[index]:
            load.wait()
        out[part, 0:128, :] = (one[part].astype(F32) + two[part].astype(F32)).astype(BF16)
        out[part, 128:176, :] = (three[part].astype(F32) + four[part].astype(F32)).astype(BF16)
        stores.append(pltpu.make_async_copy(out.at[part], out_hbm.at[part], sems.at[index, 4]))
        stores[-1].start()
    for store in stores:
        store.wait()


def merge(
    arrive,
    pieces_hbm,
    keep_hbm,
    arrived_hbm,
    near,
    one,
    two,
    three,
    hid_ref,
    small_ref,
    gain_rows,
    wkv_ref,
    gain_ref,
    out_hbm,
    part_ref,
    pair_ref,
    pieces,
    keep_q,
    arrived_q,
    feed,
    rest,
    sems,
):
    parts = [pl.ds(16 * index, 16) for index in range(4)]
    first = [
        pltpu.make_async_copy(keep_hbm, keep_q, sems.at[0]),
        pltpu.make_async_copy(arrived_hbm, arrived_q, sems.at[1]),
    ]
    loads = [
        pltpu.make_async_copy(pieces_hbm.at[part], pieces.at[part], sems.at[2 + index])
        for index, part in enumerate(parts)
    ]
    for load in first + loads:
        load.start()
    arrive()
    pair = added(near[...], one[...], two[...], three[...])
    pair_ref[...] = pair
    grad_kv = nn(pair, hid_ref[...])
    gain_grad = (
        gain_rows[...]
        + jnp.sum(grad_kv * wkv_ref[...].astype(F32).T, axis=0, keepdims=True)
    ) / gain_ref[...]
    last = jnp.concatenate([small_ref[0:25], gain_grad, small_ref[26:32]], axis=0)
    shared = jnp.concatenate([grad_kv, last], axis=0).astype(BF16)
    for piece in range(16):
        for place in range(3):
            row, group = divmod(3 * piece + place, 4)
            if 16 * row < SMALL:
                value = shared[16 * row : 16 * row + 16, 128 * group : 128 * group + 128]
            else:
                value = jnp.zeros((16, 128), BF16)
            for far in range(GROUPS):
                rest[16 * far + piece, 48 + 16 * place : 64 + 16 * place] = value
    for load in first:
        load.wait()
    rest[:, 0:48, :] = (keep_q[...].astype(F32) + arrived_q[...].astype(F32)).astype(BF16)
    stores = [pltpu.make_async_copy(rest, out_hbm.at[:, pl.ds(128, 96), :], sems.at[6])]
    stores[0].start()
    total = jnp.zeros((176, 128), F32)
    for index in range(4):
        loads[index].wait()
        for piece in range(16 * index, 16 * index + 16):
            total = total + pieces[piece].astype(F32)
    total = total.astype(BF16)
    part_ref[...] = total[128:176]
    for index in range(64):
        feed[index] = total[0:128]
    stores.append(pltpu.make_async_copy(feed, out_hbm.at[:, pl.ds(0, 128), :], sems.at[7]))
    stores[1].start()
    for store in stores:
        store.wait()


def collect(spread, part_ref, out_ref, rest, sems):
    load = pltpu.make_async_copy(spread.at[:, pl.ds(128, 96), :], rest, sems.at[0])
    load.start()
    load.wait()
    total = rest[0].astype(F32)
    for index in range(1, 64):
        total = total + rest[index].astype(F32)
    total = total.astype(BF16)
    for index in range(16):
        out_ref[index, 0:PIECE] = part_ref[...]
        out_ref[index, PIECE:EXTRA] = total


def unpack(at_ref, half_ref, *refs):
    up_ref, down_ref = refs[-2:]
    for group in range(2):
        up_ref[:, 128 * group : 128 * group + 128] = (
            half_ref[:, pl.ds(32 * group, 32), :].astype(F32).reshape(D, 128)
        )
    for group in range(4):
        down_ref[:, 128 * group : 128 * group + 128] = (
            half_ref[:, pl.ds(64 + 16 * group, 16), :].astype(F32).reshape(CHUNK, 128)
        )


def assemble(mine_ref, other_ref, output_ref, query_ref, kv_ref, router_ref, heads_ref, feed_ref, shared):
    core = lax.axis_index("core")
    for ref, half in ((mine_ref, core), (other_ref, 1 - core)):
        for column in range(4):
            for row in range(4):
                rows = pl.ds(pl.multiple_of(half * HALF + row * PIECE, 16), PIECE)
                for index, target in enumerate((output_ref, query_ref)):
                    target[rows, pl.ds(128 * column, 128)] = ref[
                        4 * column + row, pl.ds(PIECE * index, PIECE), :
                    ].astype(F32)
    for piece in range(14):
        for place in range(3):
            row, group = divmod(3 * piece + place, 4)
            if 16 * row < SMALL:
                at = pl.ds(2 * PIECE + 16 * place, 16)
                shared[16 * row : 16 * row + 16, 128 * group : 128 * group + 128] = mine_ref[
                    piece, at, :
                ].astype(F32) + other_ref[piece, at, :].astype(F32)
    kv_ref[...] = shared[0:128].T
    router_ref[...] = shared[128:152]
    feed_ref[...] = shared[152:153]
    heads_ref[...] = shared[153:154]


def shape(dims, dtype=BF16):
    return jax.ShapeDtypeStruct(dims, dtype)


VMEM = pl.BlockSpec(memory_space=pltpu.VMEM)
SMEM = pl.BlockSpec(memory_space=pltpu.SMEM)
HBM = pl.BlockSpec(memory_space=pltpu.HBM)
ANY = pl.BlockSpec(memory_space=pl.ANY)


def nothing(*refs):
    pass


def after(value, *others):
    return pl.pallas_call(
        nothing,
        out_shape=shape(value.shape, value.dtype),
        in_specs=[ANY] * (1 + len(others)),
        out_specs=ANY,
        input_output_aliases={0: 0},
        name="after",
    )(value, *others)


def size_of(value):
    return math.prod(value.shape) * jnp.dtype(value.dtype).itemsize


def call(kernel, micros, inputs, outputs, scratch=(), far=(), far_out=(), sent=(), own_loads=False, limit=None):
    near = [index for index in range(len(inputs)) if index not in far]
    count, ends = len(inputs), len(inputs) + len(outputs)

    def body(*refs):
        sources, results, own = list(refs[:count]), refs[count:ends], refs[ends:]
        buffers, sems = own[len(scratch) : -1], own[-1]
        loads = []
        for index, (source, buffer) in enumerate(zip(near, buffers)):
            loads.append(pltpu.make_async_copy(sources[source], buffer, sems.at[index]))
            sources[source] = buffer
        def arrive():
            for load in loads:
                load.wait()

        for load in loads:
            load.start()
        if own_loads:
            kernel(arrive, *sources, *results, *own[: len(scratch)])
        else:
            arrive()
            kernel(*sources, *results, *own[: len(scratch)])

    buffers = [pltpu.VMEM(inputs[index].shape, inputs[index].dtype) for index in near]
    limit = limit or LIMIT - sum(size_of(inputs[index]) for index in sent)
    return pl.pallas_call(
        body,
        out_shape=outputs,
        in_specs=[ANY if index in sent else HBM for index in range(count)],
        out_specs=tuple(HBM if index in far_out else VMEM for index in range(len(outputs))),
        scratch_shapes=[
            *scratch,
            *buffers,
            pltpu.SemaphoreType.DMA((len(near),)),
        ],
        compiler_params=pltpu.CompilerParams(vmem_limit_bytes=limit),
        cost_estimate=pl.CostEstimate(
            flops=int(micros * 1e9), bytes_accessed=(1 << 20) if micros else 0, transcendentals=0
        ),
        name=kernel.__name__,
    )(*inputs)


def turn(size, step):
    return [(index, (index + step) % size) for index in range(size)]


def swap(value):
    return lax.ppermute(value, "core", turn(2, 1))


def mirror(value):
    return lax.ppermute(value, "x", [(0, 3), (3, 0), (1, 2), (2, 1)])


def around(value, axis):
    return [lax.ppermute(value, axis, turn(4, step)) for step in (1, 2, 3)]


def vmem(dims, dtype=F32):
    return pltpu.VMEM(dims, dtype)


def shards(
    tokens,
    expert_ids,
    cotangent,
    gain_heads,
    key_value_weight,
    router_weight,
    query_weight,
    output_weight,
    gain_feed,
    up_weight,
    down_weight,
):
    x = lax.axis_index("x")
    core = lax.axis_index("core")
    chips = ("x", "y", "z")
    tok = tokens[0]
    cot = cotangent[0]
    ids = expert_ids[0].T
    wq = jnp.swapaxes(query_weight, 1, 2).reshape(OWN, D)
    wr = jnp.pad(router_weight.T, ((0, 8), (0, 0)))
    wkv = key_value_weight
    gain1 = gain_heads.reshape(1, D)
    gain2 = gain_feed.reshape(1, D)

    carried = jnp.concatenate(
        [
            tok[TILE:TOK],
            jnp.pad(ids[:, TILE:TOK].astype(BF16), ((0, 8), (0, D - TILE))),
        ],
        axis=0,
    )
    carried = mirror(carried)
    mine = lax.dynamic_slice(wq, (core * HALF, 0), (HALF, D))
    mine = lax.all_to_all(
        jnp.broadcast_to(mine[None], (GROUPS, HALF, D)), "x", split_axis=0, concat_axis=0, tiled=True
    )
    first, kv = call(
        pairs_first,
        2,
        (tok, gain1, wkv),
        (shape((TILE, D)), shape((TOK, 2 * HEAD))),
    )
    kvs = [kv] + around(kv, "x")
    wo_copies = jnp.broadcast_to(output_weight.reshape(1, OWN, D), (GROUPS, OWN, D))
    cot_high, hidden, turned, gates, slots = call(
        prepare,
        3,
        (first, carried, ids, gain1, wr, cot, *kvs[1:], wo_copies),
        (
            shape((TILE, D)),
            shape((TOK, D)),
            shape((D, TOK)),
            shape((EXPERTS, TOK), F32),
            shape((EXPERTS, TOK), jnp.int32),
        ),
        far=(6, 7, 8, 9),
        sent=(1, 6, 7, 8),
    )
    mine = after(mine, slots)
    wqs = (mine, swap(mine))
    wo = after(wo_copies, wqs[1])
    wo = lax.all_to_all(wo, "x", split_axis=0, concat_axis=0, tiled=True)
    wo = wo.reshape(EXPERTS * HEAD, D)
    cot_high = mirror(cot_high)

    qc, mixed, lse, kv_all, dense = call(
        attend,
        14,
        (turned, slots, gates, *wqs, *kvs),
        (
            shape((HEAD, ROUTES)),
            shape((HEAD, ROUTES)),
            shape((1, ROUTES), F32),
            shape((LENGTH, 2 * HEAD)),
            shape((EXPERTS * HEAD, TOK)),
        ),
        [
            vmem((EXPERTS * HEAD, TOK)),
            vmem((LENGTH, HEAD), BF16),
            vmem((GROUPS, HEAD + 16, 2 * TILE), BF16),
            vmem((1, LANES)),
            vmem((HEAD + 16, LANES)),
            vmem((2 * TILE, LANES)),
            vmem((2 * TILE, LANES), BF16),
            vmem((GROUPS, HALF, D), BF16),
            vmem((GROUPS, HALF, D), BF16),
            pltpu.SemaphoreType.DMA((2,)),
        ],
        far=(3, 4),
        own_loads=True,
        sent=(3, 4, 6, 7, 8),
    )

    result, out_high, middle, back, keep, send = call(
        feed_part,
        17,
        (tok, carried, cot, cot_high, dense, gain2, wo, up_weight, down_weight),
        (
            shape((TOK, D)),
            shape((TILE, D)),
            shape((TOK, D), F32),
            shape((TOK, D), F32),
            shape((64, 128, 128)),
            shape((64, 128, 128)),
        ),
        [
            vmem((TOK, D), BF16),
            vmem((D, TOK), BF16),
            vmem((TOK, D), BF16),
            vmem((TOK, D)),
            vmem((EXPERTS * HEAD, D), BF16),
            vmem((D, FF), BF16),
            vmem((FF, D), BF16),
            vmem((8, 16, 128, 128), BF16),
            pltpu.SemaphoreType.DMA((3,)),
            pltpu.SemaphoreType.DMA((8,)),
        ],
        far=(6, 7, 8),
        far_out=(4, 5),
        sent=(3, 6),
        own_loads=True,
    )
    arrived = swap(send)
    out_back = mirror(out_high)

    grad_middle, turned_gm, gain_grad, keep_o, send_o = call(
        norm_part,
        4,
        (cot, cot_high, middle, back, dense, gain2),
        (
            shape((TOK, D), F32),
            shape((D, TOK)),
            shape((1, D), F32),
            shape((64, PIECE, 128)),
            shape((64, PIECE, 128)),
        ),
        [vmem((TOK, D), BF16)],
        sent=(1,),
    )
    arrived_o = swap(send_o)
    (paired,) = call(
        pair_feed,
        4,
        (keep, arrived, keep_o, arrived_o),
        (shape((64, 176, 128)),),
        [
            vmem((64, 128, 128), BF16),
            vmem((64, 128, 128), BF16),
            vmem((64, PIECE, 128), BF16),
            vmem((64, PIECE, 128), BF16),
            vmem((64, 176, 128), BF16),
            pltpu.SemaphoreType.DMA((8, 5)),
        ],
        far=(0, 1, 2, 3),
        far_out=(0,),
        sent=(1, 3),
        own_loads=True,
    )
    gt, delta, grad_logits, small = call(
        route_part,
        6,
        (turned_gm, mixed, slots, gates, hidden, wo, gain_grad, paired),
        (
            shape((HEAD, ROUTES)),
            shape((1, ROUTES), F32),
            shape((EXPERTS, TOK), F32),
            shape((32, D), F32),
        ),
        [vmem((EXPERTS * HEAD, TOK)), vmem((EXPERTS, TOK))],
        far=(7,),
        sent=(5,),
    )
    pieces = lax.all_to_all(paired, chips, split_axis=0, concat_axis=0, tiled=True)

    pair, *others, dqall, gain_rows, keep_q, send_q = call(
        back_part,
        20,
        (qc, gt, lse, delta, kv_all, out_back, slots, hidden, small, wr, *wqs),
        (
            *[shape((2 * HEAD, TOK))] * GROUPS,
            shape((EXPERTS * HEAD, TOK)),
            shape((1, D), F32),
            shape((64, PIECE, 128)),
            shape((64, PIECE, 128)),
        ),
        [
            vmem((HEAD, ROUTES), BF16),
            vmem((LENGTH, HEAD), BF16),
            vmem((LENGTH, HEAD), BF16),
            vmem((TILES, HEAD, TILE), BF16),
            vmem((TILES, HEAD, TILE)),
            vmem((TILES, HEAD, TILE)),
            vmem((HEAD, LANES)),
            vmem((TILE, LANES)),
            vmem((TILE, LANES)),
            vmem((TILE, LANES), BF16),
            vmem((TILE, LANES), BF16),
        ],
        far=(5,),
        sent=(5, 10, 11),
    )
    arrived_pairs = [
        lax.ppermute(value, "x", turn(4, step + 1)) for step, value in enumerate(others)
    ]
    arrived_q = swap(send_q)
    merged, part, pair_sum = call(
        merge,
        5,
        (
            pieces,
            keep_q,
            arrived_q,
            pair,
            *arrived_pairs,
            hidden,
            small,
            gain_rows,
            wkv,
            gain1,
        ),
        (shape((64, 224, 128)), shape((PIECE, 128)), shape((2 * HEAD, TOK))),
        [
            vmem((64, 176, 128), BF16),
            vmem((64, PIECE, 128), BF16),
            vmem((64, PIECE, 128), BF16),
            vmem((64, 128, 128), BF16),
            vmem((64, 96, 128), BF16),
            pltpu.SemaphoreType.DMA((8,)),
        ],
        far=(0, 1, 2),
        far_out=(0,),
        own_loads=True,
        sent=(0, 2, 4, 5, 6),
    )
    grad_whole, grad_high = call(
        finish,
        3,
        (tok, carried, grad_middle, dqall, grad_logits, wr, *wqs, pair_sum, wkv, gain1),
        (shape((TOK, D)), shape((TILE, D))),
    )
    spread = lax.all_to_all(merged, chips, split_axis=0, concat_axis=0, tiled=True)
    result = lax.dynamic_update_slice(result, out_back, (TILE, 0))
    grad_back = mirror(grad_high)
    spread = after(spread, grad_back, result)
    grad_tokens = lax.dynamic_update_slice(grad_whole, grad_back, (TILE, 0))
    (part,) = call(
        collect,
        0,
        (spread, part),
        (shape((16, EXTRA, 128)),),
        [vmem((64, 96, 128), BF16), pltpu.SemaphoreType.DMA((1,))],
        far=(0,),
        sent=(0,),
    )
    feed_other = swap(spread)
    part = lax.all_to_all(part, ("y", "z"), split_axis=0, concat_axis=0, tiled=True)

    def unpacked(value, half, *earlier, extra=()):
        half_spec = pl.BlockSpec((16, 128, 128), lambda index, at: (index, 0, 0))
        return pl.pallas_call(
            unpack,
            grid_spec=pltpu.PrefetchScalarGridSpec(
                num_scalar_prefetch=1,
                grid=(4,),
                in_specs=[half_spec] + [HBM] * len(earlier) + [ANY] * len(extra),
                out_specs=(
                    pl.BlockSpec((D, CHUNK), lambda index, at: (0, 4 * at[0] + index)),
                    pl.BlockSpec((CHUNK, D), lambda index, at: (4 * at[0] + index, 0)),
                ),
            ),
            out_shape=(shape((D, FF), F32), shape((FF, D), F32)),
            input_output_aliases={2: 0, 3: 1} if earlier else {},
            compiler_params=pltpu.CompilerParams(vmem_limit_bytes=LIMIT - 2 * MIB),
            name="unpack",
        )(half.reshape(1), value, *earlier, *extra)

    grads = unpacked(spread, core)
    grad_up, grad_down = unpacked(feed_other, 1 - core, *grads)
    part = after(part, grad_up)
    part_other = swap(part)
    output_grad, query_grad, kv_grad, router_grad, gain_heads_grad, gain_feed_grad = call(
        assemble,
        4,
        (part, part_other),
        (
            shape((OWN, D), F32),
            shape((OWN, D), F32),
            shape((D, 2 * HEAD), F32),
            shape((EXPERTS, D), F32),
            shape((1, D), F32),
            shape((1, D), F32),
        ),
        [vmem((SMALL, D))],
        sent=(0, 1),
        limit=20 * MIB,
    )
    return (
        result[None],
        grad_tokens[None],
        gain_heads_grad.reshape(D),
        kv_grad,
        router_grad.T,
        query_grad.reshape(OWN // HEAD, HEAD, D).swapaxes(1, 2),
        output_grad.reshape(OWN // HEAD, HEAD, D),
        gain_feed_grad.reshape(D),
        grad_up,
        grad_down,
    )


def solution(mesh):
    grid = Mesh(mesh.devices.reshape(4, 4, 4, 2), ("x", "y", "z", "core"))
    dp = ("y", "z", "core")
    return jax.shard_map(
        shards,
        mesh=grid,
        in_specs=(
            P(dp, "x", None),
            P(dp, "x", None),
            P(dp, "x", None),
            P(),
            P(),
            P(),
            P("x", None, None),
            P("x", None, None),
            P(),
            P(),
            P(),
        ),
        out_specs=(
            P(dp, "x", None),
            P(dp, "x", None),
            P(),
            P(),
            P(),
            P("x", None, None),
            P("x", None, None),
            P(),
            P(),
            P(),
        ),
        check_vma=False,
    )
```
